32 devices in a mesh: dp: 8 (over y, x, core), pix: 4 (over z).
Axes of the slice: x: 2, y: 2, z: 4, core: 2. Of those that a mesh axis runs over, the one named last changes fastest.
Arguments:
- latents: bfloat16 [512, 1024], replicated, may hold values from -6 to 6
- pixel_rgb: bfloat16 [3, 131072], P(None, ('dp', 'pix')), may hold values from -1 to 1
- coords: int32 [2, 131072], P(None, ('dp', 'pix')), may hold values from 0 to 111, as said below
- segment_ids: int32 [131072], P(('dp', 'pix')), may hold values from 0 to 4, as said below
- image_sizes: int32 [2, 32], P(None, 'dp'), may hold values from 16 to 112, as said below
- input_gain: float32 [261], replicated, may hold values from 0.5 to 1.5
- input_bias: float32 [261], replicated, may hold values from -1 to 1
- query_weight: bfloat16 [1024, 1024], replicated, may hold values from -0.375 to 0.375
- query_bias: float32 [1024], replicated, may hold values from -2.5 to 2.5
- key_weight: bfloat16 [261, 1024], replicated, may hold values from -0.375 to 0.375
- value_weight: bfloat16 [261, 1024], replicated, may hold values from -0.375 to 0.375
- value_bias: float32 [1024], replicated, may hold values from -1.5 to 1.5
- out_weight: bfloat16 [1024, 1024], replicated, may hold values from -1 to 1
- out_bias: float32 [1024], replicated, may hold values from -1.5 to 1.5
- latent_gain: float32 [1024], replicated, may hold values from 0.5 to 1.5
- latent_bias: float32 [1024], replicated, may hold values from -1 to 1
- mlp_gain: float32 [1024], replicated, may hold values from 0.5 to 1.5
- mlp_bias: float32 [1024], replicated, may hold values from -1 to 1
- up_weight: bfloat16 [1024, 1024], replicated, may hold values from -0.1875 to 0.1875
- up_bias: float32 [1024], replicated, may hold values from -1.5 to 1.5
- down_weight: bfloat16 [1024, 1024], replicated, may hold values from -0.1875 to 0.1875
- down_bias: float32 [1024], replicated, may hold values from -1.5 to 1.5
- cotangent: float32 [32, 512, 1024], P(('dp', 'pix')), may hold values from -6 to 6
Outputs:
- latents_out: float32 [32, 512, 1024], P(('dp', 'pix'))
- rgb_grad: bfloat16 [3, 131072], P(None, ('dp', 'pix'))
- latents_grad: float32 [512, 1024], P('pix', 'dp')
- query_weight_grad: float32 [1024, 1024], P('pix', 'dp')
- query_bias_grad: float32 [1024], replicated
- key_weight_grad: float32 [261, 1024], replicated
- value_weight_grad: float32 [261, 1024], replicated
- value_bias_grad: float32 [1024], replicated
- out_weight_grad: float32 [1024, 1024], P('pix', 'dp')
- out_bias_grad: float32 [1024], replicated
- latent_gain_grad: float32 [1024], replicated
- latent_bias_grad: float32 [1024], replicated
- mlp_gain_grad: float32 [1024], replicated
- mlp_bias_grad: float32 [1024], replicated
- up_weight_grad: float32 [1024, 1024], P('pix', 'dp')
- up_bias_grad: float32 [1024], replicated
- down_weight_grad: float32 [1024, 1024], P('pix', 'dp')
- down_bias_grad: float32 [1024], replicated
- input_gain_grad: float32 [261], replicated
- input_bias_grad: float32 [261], replicated
The draws below stay inside these ranges and needn't reach their ends.
Inputs may be any that keep to these rules, and one draw needn't show every extreme that they name: `image_sizes`: in every group one image is 112 x 112; the others have both sides between 16 and 32. `segment_ids`: A group's images fill its 16384 slots from the start, image 0 first, each taking height times width slots in a row; every later slot holds 4 and is padding. `coords`: row and column of the slot's pixel in its image, row-major along the image's slots; 0 and 0 in padding.
All inputs are finite; a program needn't handle non-finite values.
Results may differ from the reference program's by a relative error of at most 0.015.
Values may be sent and summed in bfloat16 or wider, within the bound.
A program may use at most 192 MiB of HBM per device.

```python
import math
import jax
import jax.numpy as jnp
from jax import lax

D = 1024
FF = 1024
LAT = 512
BANDS = 64
MAXRES = 224
BIG_SIDE = 112
SMALL_SIDE = 32
FEAT = 261
GROUPS = 8
GROUP_IMG = 4
IMAGES = 32
SLOTS = 16384
TOKENS = 131072


def image_sides(key):
    key = jax.random.fold_in(key, 11)
    side_key, big_key = jax.random.split(key)
    least_side = SMALL_SIDE // 2
    small_sides = jax.random.randint(side_key, (2, GROUPS, GROUP_IMG), least_side, SMALL_SIDE + 1)
    chosen = jax.random.randint(big_key, (GROUPS, 1), 0, GROUP_IMG)
    is_big = jnp.arange(GROUP_IMG)[None, :] == chosen
    return jnp.where(is_big[None], BIG_SIDE, small_sides).astype(jnp.int32)


def slot_layout(key):
    sides = image_sides(key)
    pixel_count = sides[0] * sides[1]
    ends = jnp.cumsum(pixel_count, axis=1)
    starts = ends - pixel_count
    slot_index = jnp.arange(SLOTS, dtype=jnp.int32)[None, :]
    segment = jnp.sum((slot_index[:, :, None] >= ends[:, None, :]).astype(jnp.int32), axis=2)
    onehot = segment[:, :, None] == jnp.arange(GROUP_IMG, dtype=jnp.int32)[None, None, :]
    start_of = jnp.sum(jnp.where(onehot, starts[:, None, :], 0), axis=2)
    width_of = jnp.maximum(jnp.sum(jnp.where(onehot, sides[1][:, None, :], 0), axis=2), 1)
    local = slot_index - start_of
    inside = segment < GROUP_IMG
    row_pos = jnp.where(inside, local // width_of, 0)
    col_pos = jnp.where(inside, local % width_of, 0)
    return (segment.astype(jnp.int32), row_pos.astype(jnp.int32), col_pos.astype(jnp.int32))


def draw_image_sizes(key, part):
    return image_sides(key).reshape(2, IMAGES)


def draw_segment_ids(key, part):
    return slot_layout(key)[0].reshape(TOKENS)


def draw_coords(key, part):
    segment, row_pos, col_pos = slot_layout(key)
    return jnp.stack([row_pos, col_pos]).reshape(2, TOKENS)


def level_of(key, dims, cuts, low, largest):
    loudness, own = 1.0, jax.random.fold_in(key, 6)
    for dim, shards_of in cuts:
        steps = jnp.exp(jax.random.uniform(jax.random.fold_in(own, dim), (shards_of,), jnp.float32, low / len(cuts), largest / len(cuts)))
        loudness = loudness * jnp.repeat(steps, dims[dim] // shards_of).reshape([-1 if axis == dim else 1 for axis in range(len(dims))])
    return loudness


def gaussian(rng, dims, scale, most, shards=(), kind=jnp.bfloat16):
    entries = jax.random.normal(rng, dims, jnp.float32) * scale
    if len(shards) > 0:
        entries = level_of(rng, dims, shards, -0.22, 0.18) * entries
    return jnp.clip(entries, min=-most, max=most).astype(kind)


def setup_inputs(seed: int = 0) -> dict:
    seeds = jax.random.split(jax.random.key(seed), 24)
    return {
        "latents": gaussian(seeds[0], (LAT, D), 1.0, 6.0),
        "pixel_rgb": jnp.clip(jax.random.uniform(seeds[1], (3, TOKENS), jnp.float32, -1.0, 1.0) * level_of(seeds[1], (3, TOKENS), ((1, 32),), -0.4, 0.0), -1.0, 1.0).astype(jnp.bfloat16),
        "coords": draw_coords(jax.random.fold_in(seeds[23], 71), 0),
        "segment_ids": draw_segment_ids(jax.random.fold_in(seeds[23], 71), 0),
        "image_sizes": draw_image_sizes(jax.random.fold_in(seeds[23], 71), 0),
        "input_gain": jnp.clip(1.0 + 0.1 * jax.random.normal(seeds[5], (FEAT,), jnp.float32), 0.5, 1.5),
        "input_bias": gaussian(seeds[6], (FEAT,), 0.2, 1.0, (), jnp.float32),
        "query_weight": gaussian(seeds[7], (D, D), (D // 4) ** -0.5, 0.375),
        "query_bias": gaussian(seeds[8], (D,), 0.5, 2.5, (), jnp.float32),
        "key_weight": gaussian(seeds[9], (FEAT, D), FEAT ** -0.5, 0.375),
        "value_weight": gaussian(seeds[10], (FEAT, D), FEAT ** -0.5, 0.375),
        "value_bias": gaussian(seeds[11], (D,), 0.3, 1.5, (), jnp.float32),
        "out_weight": gaussian(seeds[12], (D, D), (D // 32) ** -0.5, 1.0),
        "out_bias": gaussian(seeds[13], (D,), 0.3, 1.5, (), jnp.float32),
        "latent_gain": jnp.clip(1.0 + 0.1 * jax.random.normal(seeds[14], (D,), jnp.float32), 0.5, 1.5),
        "latent_bias": gaussian(seeds[15], (D,), 0.2, 1.0, (), jnp.float32),
        "mlp_gain": jnp.clip(1.0 + 0.1 * jax.random.normal(seeds[16], (D,), jnp.float32), 0.5, 1.5),
        "mlp_bias": gaussian(seeds[17], (D,), 0.2, 1.0, (), jnp.float32),
        "up_weight": gaussian(seeds[18], (D, FF), D ** -0.5, 0.1875),
        "up_bias": gaussian(seeds[19], (FF,), 0.3, 1.5, (), jnp.float32),
        "down_weight": gaussian(seeds[20], (FF, D), FF ** -0.5, 0.1875),
        "down_bias": gaussian(seeds[21], (D,), 0.3, 1.5, (), jnp.float32),
        "cotangent": gaussian(seeds[22], (IMAGES, LAT, D), 1.0, 6.0, ((0, 32),), jnp.float32),
    }


EPSILON = 1e-05

@jax.custom_vjp
def low(v):
    return lax.optimization_barrier(v.astype(jnp.bfloat16)).astype(jnp.float32)

@jax.custom_vjp
def low_back(v):
    return v

def low_keep(v):
    return (low(v), None)

def low_pass(kept, grad):
    return (grad,)

def back_keep(v):
    return (v, None)

def back_low(kept, grad):
    return (low(grad),)
low.defvjp(low_keep, low_pass)
low_back.defvjp(back_keep, back_low)

def layer_norm(inputs, norm_gain, norm_bias, along):
    centre = inputs - lax.optimization_barrier(jnp.mean(inputs, axis=along, keepdims=True))
    spread = lax.optimization_barrier(jnp.mean(centre * centre, axis=along, keepdims=True))
    scaled = centre * lax.rsqrt(spread + EPSILON)
    if along == 0:
        return scaled * norm_gain[:, None] + norm_bias[:, None]
    return scaled * norm_gain + norm_bias

def pixel_features(pixel_rgb, coords, segment_ids, image_sizes):
    image_count = image_sizes.shape[1]
    matches = segment_ids[None, :] == jnp.arange(image_count, dtype=jnp.int32)[:, None]
    row_span = lax.optimization_barrier(jnp.sum(jnp.where(matches, image_sizes[0][:, None], 0), axis=0))
    col_span = lax.optimization_barrier(jnp.sum(jnp.where(matches, image_sizes[1][:, None], 0), axis=0))
    pos_row = 2.0 * coords[0].astype(jnp.float32) / jnp.maximum(row_span - 1, 1).astype(jnp.float32) - 1.0
    pos_col = 2.0 * coords[1].astype(jnp.float32) / jnp.maximum(col_span - 1, 1).astype(jnp.float32) - 1.0
    band_index = jnp.arange(BANDS).astype(jnp.float32)
    frequency = 1.0 + band_index * (MAXRES / 2.0 - 1.0) / (BANDS - 1)

    def encode(position):
        phases = jnp.pi * frequency[:, None] * position[None, :]
        return jnp.concatenate([position[None, :], jnp.sin(phases), jnp.cos(phases)], axis=0)
    return jnp.concatenate([pixel_rgb.astype(jnp.float32), encode(pos_row), encode(pos_col)], axis=0)

def reference(latents, pixel_rgb, coords, segment_ids, image_sizes, input_gain, input_bias, query_weight, query_bias, key_weight, value_weight, value_bias, out_weight, out_bias, latent_gain, latent_bias, mlp_gain, mlp_bias, up_weight, up_bias, down_weight, down_bias, cotangent):
    highest = lax.Precision.HIGHEST
    scale_factor = 1.0 / math.sqrt(D)
    coord_groups = coords.reshape(2, GROUPS, SLOTS).transpose(1, 0, 2)
    segment_groups = segment_ids.reshape(GROUPS, SLOTS)
    size_groups = image_sizes.reshape(2, GROUPS, GROUP_IMG).transpose(1, 0, 2)
    image_index = jnp.arange(GROUP_IMG, dtype=jnp.int32)

    def forward(latents, pixel_rgb, input_gain, input_bias, query_weight, query_bias, key_weight, value_weight, value_bias, out_weight, out_bias, latent_gain, latent_bias, mlp_gain, mlp_bias, up_weight, up_bias, down_weight, down_bias):
        lat_in = low(layer_norm(latents, latent_gain, latent_bias, -1))
        query_base = (jnp.dot(lat_in, query_weight, precision=highest) + query_bias) * scale_factor
        rgb_split = pixel_rgb.reshape(3, GROUPS, SLOTS).transpose(1, 0, 2)

        def one_group(pieces):
            rgb_one, coord_one, segment_one, size_one = pieces
            features = low(low_back(pixel_features(rgb_one, coord_one, segment_one, size_one)))
            pixel_in = low(layer_norm(features, input_gain, input_bias, 0))
            key_rows = low(low_back(jnp.dot(pixel_in.T, key_weight, precision=highest)))
            value_rows = low(low_back(jnp.dot(pixel_in.T, value_weight, precision=highest) + value_bias))
            queries = low(low_back(jnp.broadcast_to(query_base, (GROUP_IMG, LAT, D))))
            scores = low_back(jnp.einsum('nld,td->nlt', queries, key_rows, precision=highest))
            member = segment_one[None, :] == image_index[:, None]
            weights = jnp.where(member[:, None, :], jnp.exp(scores), 0.0)
            totals = lax.optimization_barrier(jnp.sum(weights, axis=2))
            numerator = low_back(jnp.einsum('nlt,td->nld', low(weights), value_rows, precision=highest))
            attended = numerator / totals[:, :, None]
            branch = low_back(jnp.einsum('nld,de->nle', low(attended), out_weight, precision=highest) + out_bias)
            middle = latents[None] + branch
            mid_in = low(layer_norm(middle, mlp_gain, mlp_bias, -1))
            hidden = low_back(jnp.einsum('nld,df->nlf', mid_in, up_weight, precision=highest) + up_bias)
            active = low(jax.nn.gelu(hidden))
            return middle + low_back(jnp.einsum('nlf,fd->nld', active, down_weight, precision=highest) + down_bias)
        outputs = lax.map(jax.checkpoint(one_group), (rgb_split, coord_groups, segment_groups, size_groups))
        return outputs.reshape(IMAGES, LAT, D)
    primals = (latents.astype(jnp.float32), pixel_rgb.astype(jnp.float32), input_gain, input_bias, query_weight.astype(jnp.float32), query_bias, key_weight.astype(jnp.float32), value_weight.astype(jnp.float32), value_bias, out_weight.astype(jnp.float32), out_bias, latent_gain, latent_bias, mlp_gain, mlp_bias, up_weight.astype(jnp.float32), up_bias, down_weight.astype(jnp.float32), down_bias)
    result, pullback = jax.vjp(forward, *primals)
    gradients = pullback(cotangent)
    return (result, gradients[1].astype(jnp.bfloat16), gradients[0], gradients[4], gradients[5], gradients[6], gradients[7], gradients[8], gradients[9], gradients[10], gradients[11], gradients[12], gradients[13], gradients[14], gradients[15], gradients[16], gradients[17], gradients[18], gradients[2], gradients[3])
```

```python
from functools import partial
import math

import jax
import jax.numpy as jnp
from jax import lax
from jax.sharding import PartitionSpec as P

BANDS = 64
MAXRES = 224
EPSILON = 1e-05
FEAT = 4 * BANDS + 5
WIDE = FEAT + 3

bf16 = jnp.bfloat16
f32 = jnp.float32


def dot(a, b, dims):
    return lax.dot_general(a, b, (dims, ((), ())), preferred_element_type=f32)


def nn(a, b):
    return dot(a, b, ((1,), (0,)))


def nt(a, b):
    return dot(a, b, ((1,), (1,)))


def tn(a, b):
    return dot(a, b, ((0,), (0,)))


def reorder(rows):
    b = 2 * BANDS
    pad = [(0, WIDE - FEAT)] + [(0, 0)] * (rows.ndim - 1)
    return jnp.pad(
        jnp.concatenate([rows[4 : 4 + b], rows[5 + b :], rows[0:4], rows[4 + b : 5 + b]], axis=0), pad
    )


def restore(rows):
    b = 2 * BANDS
    return jnp.concatenate(
        [rows[2 * b : 2 * b + 4], rows[:b], rows[2 * b + 4 : 2 * b + 5], rows[b : 2 * b]], axis=0
    )


def centred(rows, axis):
    live = (lax.broadcasted_iota(jnp.int32, rows.shape, axis) < FEAT).astype(f32)
    return (rows - jnp.sum(rows, axis=axis, keepdims=True) * (1.0 / FEAT)) * live


def layout(sizes, slots):
    images = sizes.shape[1]
    slot = jnp.arange(slots, dtype=jnp.int32)
    segment = jnp.zeros((slots,), jnp.int32)
    start = jnp.zeros((slots,), jnp.int32)
    end = jnp.int32(0)
    for i in range(images):
        end = end + sizes[0, i] * sizes[1, i]
        past = slot >= end
        segment = segment + past.astype(jnp.int32)
        start = jnp.where(past, end, start)
    high = jnp.zeros((slots,), jnp.int32)
    wide = jnp.zeros((slots,), jnp.int32)
    for i in range(images):
        high = jnp.where(segment == i, sizes[0, i], high)
        wide = jnp.where(segment == i, sizes[1, i], wide)
    local = jnp.where(segment < images, slot - start, 0)
    row = local // jnp.maximum(wide, 1)
    col = local - row * wide
    y = 2.0 * row.astype(f32) / jnp.maximum(high - 1, 1).astype(f32) - 1.0
    x = 2.0 * col.astype(f32) / jnp.maximum(wide - 1, 1).astype(f32) - 1.0
    return segment, y, x


def pixel_features(rgb, y, x):
    frequency = 1.0 + jnp.arange(BANDS).astype(f32) * ((MAXRES / 2.0 - 1.0) / (BANDS - 1))
    py = jnp.pi * frequency[:, None] * y[None]
    px = jnp.pi * frequency[:, None] * x[None]
    rest = jnp.concatenate(
        [rgb.astype(f32), y[None], x[None], jnp.zeros((WIDE - FEAT, y.shape[0]), f32)], axis=0
    )
    return jnp.concatenate(
        [jnp.sin(py), jnp.cos(py), jnp.sin(px), jnp.cos(px), rest], axis=0
    ).astype(bf16)


def norm(rows):
    centre = rows - jnp.mean(rows, axis=-1, keepdims=True)
    scale = lax.rsqrt(jnp.mean(centre * centre, axis=-1, keepdims=True) + EPSILON)
    return centre * scale, scale


def norm_back(grad, unit, scale):
    return (
        grad
        - jnp.mean(grad, axis=-1, keepdims=True)
        - unit * jnp.mean(grad * unit, axis=-1, keepdims=True)
    ) * scale


def shards(
    latents,
    pixel_rgb,
    coords,
    segment_ids,
    image_sizes,
    input_gain,
    input_bias,
    query_weight,
    query_bias,
    key_weight,
    value_weight,
    value_bias,
    out_weight,
    out_bias,
    latent_gain,
    latent_bias,
    mlp_gain,
    mlp_bias,
    up_weight,
    up_bias,
    down_weight,
    down_bias,
    cotangent,
):
    images = image_sizes.shape[1]
    count, width = latents.shape
    parts = lax.axis_size("pix")
    place = lax.axis_index("pix")
    own = count // parts
    factor = 1.0 / math.sqrt(query_weight.shape[0])
    slots = pixel_rgb.shape[1] * parts

    rgb = lax.all_gather(pixel_rgb, "pix", axis=1, tiled=True)
    cot_low = cotangent[0].astype(bf16).reshape(parts, own, width)
    cot = lax.all_to_all(cot_low, "pix", split_axis=0, concat_axis=0, tiled=True).astype(f32)

    gain = reorder(input_gain)
    bias = reorder(input_bias)
    wk = reorder(key_weight)
    wv = reorder(value_weight)

    latent_rows = latents.astype(f32)
    lat_unit, lat_scale = norm(latent_rows)
    lat_in = (lat_unit * latent_gain + latent_bias).astype(bf16)
    queries = ((nn(lat_in, query_weight) + query_bias) * factor).astype(bf16)
    own_queries = lax.dynamic_slice_in_dim(queries, place * own, own, axis=0)
    own_latents = lax.dynamic_slice_in_dim(latent_rows, place * own, own, axis=0)

    qk = nt(own_queries, wk)
    qc = centred(qk * gain, 1).astype(bf16)
    qb = jnp.sum(qk * bias, axis=1)
    segment, y, x = layout(image_sizes, slots)
    feat = pixel_features(rgb, y, x)
    featf = feat.astype(f32)
    mean = jnp.sum(featf, axis=0) * (1.0 / FEAT)
    spread = jnp.sum(featf * featf, axis=0) * (1.0 / FEAT) - mean * mean
    scale = lax.rsqrt(spread + EPSILON)
    raw = nn(qc, feat) * scale
    member = (segment[None] == jnp.arange(images)[:, None]).astype(f32)
    weights = jnp.where(segment < images, jnp.exp(raw + qb[:, None]), 0.0)
    totals = dot(member, weights, ((1,), (1,)))
    scaled = ((weights * scale)[None] * member[:, None]).astype(bf16).reshape(images * own, slots)
    mix = centred(nt(scaled, feat), 1)
    unit = mix / totals.reshape(-1, 1)
    px = (unit * gain + bias).astype(bf16)

    wvo = nn(wv, out_weight).astype(bf16)
    const = nn(value_bias[None].astype(f32), out_weight.astype(f32))[0] + out_bias
    middle = jnp.tile(own_latents, (images, 1)) + nn(px, wvo) + const
    mid_unit, mid_scale = norm(middle)
    mid_in = (mid_unit * mlp_gain + mlp_bias).astype(bf16)
    hidden = nn(mid_in, up_weight) + up_bias
    k = math.sqrt(2.0 / math.pi)
    th = jnp.tanh(k * (hidden + 0.044715 * hidden**3))
    active = (0.5 * hidden * (1.0 + th)).astype(bf16)
    slope = 0.5 * (1.0 + th) + 0.5 * hidden * (1.0 - th * th) * k * (1.0 + 3 * 0.044715 * hidden**2)
    out = (middle + nn(active, down_weight) + down_bias).astype(bf16).reshape(images, own, width)
    latents_out = (
        lax.all_to_all(out, "pix", split_axis=0, concat_axis=0, tiled=True)
        .reshape(1, count, width)
        .astype(f32)
    )
    cot = cot.reshape(images * own, width)
    grad_down = cot.astype(bf16)
    down_grad = tn(active, grad_down)
    down_bias_grad = jnp.sum(cot, axis=0)
    grad_hidden = (slope * nt(grad_down, down_weight)).astype(bf16)
    up_grad = tn(mid_in, grad_hidden)
    up_bias_grad = jnp.sum(grad_hidden.astype(f32), axis=0)
    grad_mid = nt(grad_hidden, up_weight)
    mlp_gain_grad = jnp.sum(grad_mid * mid_unit, axis=0)
    mlp_bias_grad = jnp.sum(grad_mid, axis=0)
    grad_middle = cot + norm_back(grad_mid * mlp_gain, mid_unit, mid_scale)
    branch = grad_middle.astype(bf16)
    moment = tn(px, branch)
    out_bias_grad = jnp.sum(branch.astype(f32), axis=0)
    latents_part = jnp.sum(grad_middle.reshape(images, own, width), axis=0)

    gx = nt(branch, wvo)
    gain_part = jnp.sum(gx * unit, axis=0)
    bias_part = jnp.sum(gx, axis=0)
    gc = centred(gx / totals.reshape(-1, 1) * gain, 1).astype(bf16)
    level = jnp.sum(gc.astype(f32) * unit, axis=1).reshape(images, own)

    pull = nn(gc, feat).reshape(images, own, slots)
    pull = jnp.sum(pull * member[:, None], axis=0) * scale
    level_t = dot(level, member, ((0,), (0,)))
    gs = weights * (pull - level_t)
    gs_sum = jnp.sum(gs, axis=1)
    dq = centred(nt((gs * scale).astype(bf16), feat), 1)
    lean = jnp.sum(gs * raw + weights * pull, axis=0) * (1.0 / FEAT)
    ext = slice(4 * BANDS, 4 * BANDS + 3)
    grad_ext = tn(qc[:, ext], gs.astype(bf16))
    back = tn(gc[:, ext].reshape(images, own, 3)[0] * 0, gs.astype(bf16))
    for n in range(images):
        back = back + member[n] * tn(gc[n * own : (n + 1) * own, ext], weights.astype(bf16))
    u_ext = (featf[ext] - mean) * scale
    rgb_part = (grad_ext + back - u_ext * lean) * scale
    rgb_grad = lax.psum_scatter(rgb_part, "pix", scatter_dimension=1, tiled=True).astype(bf16)

    latents_sum = lax.psum_scatter(latents_part, "dp", scatter_dimension=1, tiled=True)
    down_total = lax.psum_scatter(
        lax.psum_scatter(down_grad, "dp", scatter_dimension=1, tiled=True),
        "pix", scatter_dimension=0, tiled=True)
    up_total = lax.psum_scatter(
        lax.psum_scatter(up_grad, "dp", scatter_dimension=1, tiled=True),
        "pix", scatter_dimension=0, tiled=True)
    moment_t, ob, ub, db, mg, mb, gp, bp = lax.psum(
        (moment, out_bias_grad, up_bias_grad, down_bias_grad, mlp_gain_grad, mlp_bias_grad, gain_part, bias_part),
        ("dp", "pix"))
    dq_all = lax.psum(jnp.concatenate([dq, gs_sum[:, None]], axis=1), "dp")
    dq_all = lax.all_gather(dq_all, "pix", axis=0, tiled=True)
    dq_t, gs_t = dq_all[:, :WIDE], dq_all[:, WIDE]

    group = lax.axis_index("dp")
    groups = lax.axis_size("dp")
    cols = width // groups
    rows = width // parts
    moment_low = moment_t.astype(bf16)
    my_wv = lax.dynamic_slice_in_dim(wv, place * rows, rows, axis=1)
    my_vb = lax.dynamic_slice_in_dim(value_bias, place * rows, rows, axis=0)
    out_total = tn(my_wv, lax.dynamic_slice_in_dim(moment_low, group * cols, cols, axis=1)) + (
        my_vb[:, None] * lax.dynamic_slice_in_dim(ob, group * cols, cols, axis=0)[None]
    )
    value_total = restore(nt(moment_low, out_weight))
    value_bias_total = nt(ob[None], out_weight.astype(f32))[0]
    qk_all = nt(queries, wk)
    dx = dq_t * gain + gs_t[:, None] * bias
    gain_t = restore(gp + jnp.sum(qk_all * dq_t, axis=0))
    bias_t = restore(bp + jnp.sum(qk_all * gs_t[:, None], axis=0))
    dx_low = dx.astype(bf16)
    key_total = restore(tn(dx_low, queries))
    gq = nn(dx_low, wk) * factor
    gq_low = gq.astype(bf16)
    query_bias_total = jnp.sum(gq, axis=0)
    query_total = tn(
        lax.dynamic_slice_in_dim(lat_in, place * rows, rows, axis=1),
        lax.dynamic_slice_in_dim(gq_low, group * cols, cols, axis=1),
    )
    grad_lat = nt(gq_low, query_weight)
    latent_gain_total = jnp.sum(grad_lat * lat_unit, axis=0)
    latent_bias_total = jnp.sum(grad_lat, axis=0)
    lat_back = norm_back(grad_lat * latent_gain, lat_unit, lat_scale)
    latents_total = latents_sum + lax.dynamic_slice(
        lat_back, (place * own, group * cols), (own, cols)
    )
    return (
        latents_out,
        rgb_grad,
        latents_total,
        query_total,
        query_bias_total,
        key_total,
        value_total,
        value_bias_total,
        out_total,
        ob,
        latent_gain_total,
        latent_bias_total,
        mg,
        mb,
        up_total,
        ub,
        down_total,
        db,
        gain_t,
        bias_t,
    )


def solution(mesh):
    whole = P()
    placed = (
        whole,
        P(None, ("dp", "pix")),
        P(None, ("dp", "pix")),
        P(("dp", "pix")),
        P(None, "dp"),
    ) + (whole,) * 17 + (P(("dp", "pix"), None, None),)
    square = P("pix", "dp")
    return jax.shard_map(
        shards,
        mesh=mesh,
        in_specs=placed,
        out_specs=(
            P(("dp", "pix"), None, None),
            P(None, ("dp", "pix")),
            square,
            square,
            whole,
            whole,
            whole,
            whole,
            square,
            whole,
            whole,
            whole,
            whole,
            whole,
            square,
            whole,
            square,
            whole,
            whole,
            whole,
        ),
        check_vma=False,
    )
```

```python
from functools import partial
import math
from types import SimpleNamespace

import jax
import jax.numpy as jnp
from jax import lax
from jax.experimental import pallas as pl
from jax.experimental.pallas import tpu as pltpu
from jax.sharding import PartitionSpec as P

BANDS = 64
MAXRES = 224
BIG_SIDE = 112
SMALL_SIDE = 32
EPSILON = 1e-05
FEAT = 4 * BANDS + 5
WIDE = FEAT + 11
DQ = 384
PACK = 320
TILE = 512
LANES = 128
MESH = pl.DeviceIdType.MESH
SENDS = 49
VMEM_LIMIT = 62 * 2**20

bf16 = jnp.bfloat16
f32 = jnp.float32


def dot(a, b, dims):
    return lax.dot_general(a, b, (dims, ((), ())), preferred_element_type=f32)


def nn(a, b):
    return dot(a, b, ((1,), (0,)))


def nt(a, b):
    return dot(a, b, ((1,), (1,)))


def tn(a, b):
    return dot(a, b, ((0,), (0,)))


def order_of(rows, cols, flip=False):
    b = 2 * BANDS
    f = lax.broadcasted_iota(jnp.int32, (rows, cols), 1 if flip else 0)
    g = lax.broadcasted_iota(jnp.int32, (rows, cols), 0 if flip else 1)
    to = jnp.where(f < 4, f + 2 * b, jnp.where(f < 4 + b, f - 4, jnp.where(f == 4 + b, 2 * b + 4, f - 5)))
    return ((to == g) & (f < FEAT)).astype(bf16)


def moved(rows, order, product):
    total = None
    for _ in range(3):
        part = rows.astype(bf16)
        rows = rows - part.astype(f32)
        piece = product(part, order)
        total = piece if total is None else total + piece
    return total


def centred(rows, axis):
    live = lax.broadcasted_iota(jnp.int32, rows.shape, axis) < FEAT
    rows = jnp.where(live, rows, 0.0)
    return jnp.where(live, rows - jnp.sum(rows, axis=axis, keepdims=True) * (1.0 / FEAT), 0.0)


def norm(rows):
    centre = rows - jnp.mean(rows, axis=-1, keepdims=True)
    scale = lax.rsqrt(jnp.mean(centre * centre, axis=-1, keepdims=True) + EPSILON)
    return centre * scale, scale


def norm_back(grad, unit, scale):
    return (
        grad
        - jnp.mean(grad, axis=-1, keepdims=True)
        - unit * jnp.mean(grad * unit, axis=-1, keepdims=True)
    ) * scale


def tanh(a):
    return 1.0 - 2.0 / (1.0 + jnp.exp(jnp.minimum(2.0 * a, 80.0)))


def sin_cos_pi(p):
    n = jnp.floor(p + 0.5)
    z = (p - n) * math.pi
    q = z * z
    s = z * (1.0 + q * (-1.0 / 6 + q * (1.0 / 120 + q * (-1.0 / 5040 + q * (1.0 / 362880 - q * (1.0 / 39916800))))))
    c = 1.0 + q * (
        -0.5 + q * (1.0 / 24 + q * (-1.0 / 720 + q * (1.0 / 40320 + q * (-1.0 / 3628800 + q * (1.0 / 479001600)))))
    )
    sign = 1.0 - 2.0 * (n - 2.0 * jnp.floor(n * 0.5))
    return s * sign, c * sign


def tiles_of(images, slots):
    spare = (images - 1) * SMALL_SIDE * SMALL_SIDE
    head = -(-spare // TILE)
    tail = BIG_SIDE * BIG_SIDE // TILE
    last = min(-(-(BIG_SIDE * BIG_SIDE + spare) // TILE), slots // TILE)
    return head, max(head, tail), last


def loop(lo, hi, body, unroll):
    steps = (hi - lo) // unroll
    if steps > 0:
        lax.fori_loop(0, steps, lambda i, c: (body([lo + i * unroll + k for k in range(unroll)]), c)[1], 0)
    if lo + steps * unroll < hi:
        body(list(range(lo + steps * unroll, hi)))


def wait(copies):
    for copy in copies:
        copy.wait()


def summed(first, others):
    total = first.astype(f32)
    for i in range(others.shape[0]):
        total = total + others[i].astype(f32)
    return total


MLP_UNROLL = 2
HEAD_UNROLL = 2
BIG_UNROLL = 3


def layer_kernel(images, slots, parts, fused, names, *refs):
    r = SimpleNamespace(**dict(zip(names, refs)))
    group, place = lax.axis_index("dp"), lax.axis_index("pix")
    count, width = r.latents.shape
    own, chunk = count // parts, width // parts
    rows_all = images * own
    head, tail, last = tiles_of(images, slots)
    per = r.rgb_in.shape[0] // 4
    factor = 1.0 / math.sqrt(width)
    core, quad = lax.rem(group, 2), lax.rem(group // 2, 4)
    base = group // 8 * 4
    x, y = lax.rem(quad, 2), quad // 2
    mate = ((base + quad) * 2 + 1 - core, place)

    def away(k):
        other = (1 - x if k % 2 else x) + 2 * (1 - y if k // 2 else y)
        return other, ((base + other) * 2 + core, place)

    zs = [(s, lax.rem(place + s, parts), lax.rem(place + parts - s, parts)) for s in range(1, parts)]
    used = [0]

    def send(src, dst, target):
        i = used[0]
        used[0] += 1
        copy = pltpu.make_async_remote_copy(
            src_ref=src, dst_ref=dst, send_sem=r.sems.at[0, i], recv_sem=r.sems.at[1, i],
            device_id=target, device_id_type=MESH,
        )
        copy.start()
        return copy

    def send_z(pick, put):
        return [send(pick(to), put(s), (group, to)) for s, to, _ in zs]

    def send_quad(pick, put):
        return [send(pick(away(k)[0]), put(k), away(k)[1]) for k in (1, 2, 3)]

    loads = [
        pltpu.make_async_copy(a, b, r.load_sems.at[i])
        for i, (a, b) in enumerate(
            ((r.cot_h, r.cot_f), (r.wq_h, r.wq), (r.wo_h, r.wo), (r.up_h, r.up), (r.down_h, r.down))
        )
    ]
    for copy in loads:
        copy.start()

    barrier = pltpu.get_barrier_semaphore()
    friends = [(group, to) for _, to, _ in zs]
    if fused:
        friends += [mate] + [away(k)[1] for k in (1, 2, 3)]
    for device in friends:
        pl.semaphore_signal(barrier, inc=1, device_id=device, device_id_type=MESH)
    pl.semaphore_wait(barrier, len(friends))

    rgb_copies = send_z(lambda to: r.rgb_in, lambda s: r.rgb_recv.at[s - 1])
    loads[0].wait()
    r.cot_send[...] = r.cot_f[0].astype(bf16).reshape(parts, own, width)
    cot_copies = send_z(lambda to: r.cot_send.at[to], lambda s: r.cot_low.at[place])
    r.cot_low[place] = r.cot_send[place]

    to_waves = order_of(WIDE, FEAT, flip=True)
    r.wk[:WIDE] = nn(to_waves, r.wk_in[...]).astype(bf16)
    r.wk[WIDE:] = jnp.zeros_like(r.wk[WIDE:])
    vb = r.vecs[10:11, :]
    vb_high = vb.astype(bf16).astype(f32)
    row = lax.broadcasted_iota(jnp.int32, (WIDE, width), 0)
    wv = nn(to_waves, r.wv_in[...])
    r.wv[...] = jnp.where(row == FEAT, vb_high, jnp.where(row == FEAT + 1, vb - vb_high, wv)).astype(bf16)
    feats = moved(r.vecs[8:16, :DQ], order_of(DQ, DQ), nn)
    r.feats[...] = feats
    gain, bias = feats[0:1, :WIDE], feats[1:2, :WIDE]

    loads[1].wait()
    rows = pl.ds(pl.multiple_of(place * own, own), own)
    lat_rows = r.latents[rows, :].astype(f32)
    own_unit, _ = norm(lat_rows)
    own_in = (own_unit * r.vecs[2:3, :] + r.vecs[3:4, :]).astype(bf16)
    own_queries = ((nn(own_in, r.wq[...]) + r.vecs[0:1, :]) * factor).astype(bf16)
    qk = nt(own_queries, r.wk[:WIDE])
    qc = centred(qk * gain, 1).astype(bf16)
    r.qc[...] = qc
    r.qb[...] = jnp.sum(qk * bias, axis=1, keepdims=True)
    pick = (
        lax.broadcasted_iota(jnp.int32, (16, WIDE), 1)
        == lax.broadcasted_iota(jnp.int32, (16, WIDE), 0) + 4 * BANDS
    ).astype(bf16)
    r.ext[images * 16 :, :] = nt(pick, qc).astype(bf16)

    wait(rgb_copies)
    for c in range(3):
        at = slice(c * per, (c + 1) * per)
        r.rgbf[c, pl.ds(pl.multiple_of(place * per, per), per), :] = r.rgb_in[at, :].astype(f32)
        for s, _, source in zs:
            r.rgbf[c, pl.ds(pl.multiple_of(source * per, per), per), :] = r.rgb_recv[s - 1, at, :].astype(f32)

    ends, high, wide = [], [], []
    end = jnp.int32(0)
    for i in range(images):
        end = end + r.sizes[0, i] * r.sizes[1, i]
        ends.append(end.astype(f32))
        high.append(jnp.maximum(r.sizes[0, i] - 1, 1).astype(f32))
        wide.append(r.sizes[1, i].astype(f32))
    is_big = [(r.sizes[0, n] > SMALL_SIDE).astype(f32) for n in range(images)]

    def features(j):
        shape = (8, TILE)
        lane = lax.broadcasted_iota(jnp.int32, shape, 1)
        sub = lax.broadcasted_iota(jnp.int32, shape, 0)
        slot = (lane + j * TILE).astype(f32)
        segment = jnp.zeros(shape, f32)
        start = jnp.zeros(shape, f32)
        tall = jnp.full(shape, high[0])
        across = jnp.full(shape, wide[0])
        for i in range(images):
            past = slot >= ends[i]
            segment = jnp.where(past, segment + 1.0, segment)
            if i + 1 < images:
                start = jnp.where(past, ends[i], start)
                tall = jnp.where(past, high[i + 1], tall)
                across = jnp.where(past, wide[i + 1], across)
            else:
                start = jnp.where(past, slot, start)
        local = slot - start
        row = jnp.floor((local + 0.5) / across)
        col = local - row * across
        y = 2.0 * row / tall - 1.0
        x = 2.0 * col / jnp.maximum(across - 1.0, 1.0) - 1.0
        step = (MAXRES / 2.0 - 1.0) / (BANDS - 1)
        lowest = 1.0 + sub.astype(f32) * step
        total = None
        pieces = []
        for spot in (y, x):
            s, c = sin_cos_pi(lowest * spot)
            rs, rc = sin_cos_pi((8 * step) * spot)
            sines, cosines = [s], [c]
            for _ in range(BANDS // 8 - 1):
                s, c = s * rc + c * rs, c * rc - s * rs
                sines.append(s)
                cosines.append(c)
            for k in range(BANDS // 8):
                total = sines[k] + cosines[k] if total is None else total + (sines[k] + cosines[k])
            pieces.append(jnp.concatenate(sines, axis=0).astype(bf16))
            pieces.append(jnp.concatenate(cosines, axis=0).astype(bf16))
        total = jnp.sum(total, axis=0, keepdims=True)
        red, green, blue = (r.rgbf[c, pl.ds(j, 1), :] for c in range(3))
        y, x, segment = y[0:1], x[0:1], segment[0:1]
        total = total + (red + green + blue + y + x)
        squares = red * red + green * green + blue * blue + y * y + x * x + 2.0 * BANDS
        mean = total * (1.0 / FEAT)
        spread = squares * (1.0 / FEAT) - mean * mean + EPSILON
        scale = lax.rsqrt(spread)
        deviation = spread * scale
        rest = deviation - deviation.astype(bf16).astype(f32)
        ext = jnp.zeros(shape, f32)
        for k, v in enumerate((red, green, blue, y, x, deviation, rest)):
            ext = jnp.where(sub == k, v, ext)
        pieces.append(jnp.concatenate([ext, jnp.zeros(shape, f32)], axis=0).astype(bf16))
        tile = jnp.concatenate(pieces, axis=0)
        r.feat[j] = tile
        r.stat[j] = jnp.where(sub == 0, scale, jnp.where(sub == 1, mean, segment))
        return tile, scale, segment

    r.acc[...] = jnp.zeros_like(r.acc)
    r.acc_big[...] = jnp.zeros_like(r.acc_big)

    def side(parts_of):
        return parts_of[0] if len(parts_of) == 1 else jnp.concatenate(parts_of, axis=1)

    def forward(mixed, js):
        tiles, mixes = [], []
        for j in js:
            tile, scale, segment = features(j)
            weights = jnp.exp(nn(r.qc[...], tile) * scale + r.qb[...])
            if mixed:
                weights = jnp.where(segment < images, weights, 0.0)
            r.wst[j] = weights.astype(bf16)
            scaled = (weights * scale).astype(bf16)
            if mixed:
                none = jnp.zeros_like(scaled)
                scaled = jnp.concatenate([jnp.where(segment == n, scaled, none) for n in range(images)], axis=0)
            tiles.append(tile)
            mixes.append(scaled)
        into = r.acc if mixed else r.acc_big
        into[...] += nt(side(tiles), side(mixes))

    loop(0, head, partial(forward, True), HEAD_UNROLL)
    loop(head, tail, partial(forward, False), BIG_UNROLL)
    loop(tail, last, partial(forward, True), HEAD_UNROLL)

    loads[2].wait()
    wvo = nn(r.wv[...], r.wo[...])
    const = wvo[FEAT : FEAT + 1] + wvo[FEAT + 1 : FEAT + 2] + r.vecs[1:2, :]
    r.wvo[...] = jnp.where(row < FEAT, wvo, 0.0).astype(bf16)
    lane = lax.broadcasted_iota(jnp.int32, (own, WIDE), 1)
    ones = ((lane == FEAT) | (lane == FEAT + 1)).astype(f32)
    big = r.acc_big[...]
    mix_all = (r.acc[...] + jnp.concatenate([big * is_big[n] for n in range(images)], axis=1)).T
    for n in range(images):
        at = slice(n * own, (n + 1) * own)
        mix = mix_all[at]
        totals = mix[:, FEAT : FEAT + 1] + mix[:, FEAT + 1 : FEAT + 2]
        unit = centred(mix, 1) / totals
        r.tot[at, :] = totals
        r.unit[at, :] = unit
        r.px[at, :] = (unit * gain + bias + ones).astype(bf16)

    loads[3].wait()
    loads[4].wait()
    k = math.sqrt(2.0 / math.pi)
    half = 2 * own
    out_copies = []
    for blk in range(rows_all // half):
        at = slice(blk * half, (blk + 1) * half)
        px = r.px[at, :]
        middle = jnp.concatenate([lat_rows] * (half // own), axis=0) + nn(px, r.wvo[...]) + const
        mid_unit, mid_scale = norm(middle)
        mid_in = (mid_unit * r.vecs[4:5, :] + r.vecs[5:6, :]).astype(bf16)
        hidden = nn(mid_in, r.up[...]) + r.vecs[6:7, :]
        th = tanh(k * (hidden + 0.044715 * hidden * hidden * hidden))
        active = (0.5 * hidden * (1.0 + th)).astype(bf16)
        r.cot_f[0, at, :] = 0.5 * (1.0 + th) + 0.5 * hidden * (1.0 - th * th) * k * (
            1.0 + 3 * 0.044715 * hidden * hidden
        )
        done = (middle + nn(active, r.down[...]) + r.vecs[7:8, :]).astype(bf16)
        r.out_send[2 * blk] = done[:own]
        r.out_send[2 * blk + 1] = done[own:]
        r.mid_unit[at, :] = mid_unit
        r.mid_scale[at, :] = mid_scale
        r.act_t[:, at] = active.T
        r.mid_t[:, at] = mid_in.T
        r.px_t[:, at] = px.T
    out_copies = send_z(lambda to: r.out_send.at[to], lambda s: r.out_rows.at[place])
    r.out_rows[place] = r.out_send[place]

    wait(cot_copies)

    def down_grads(jj, c):
        cols = pl.ds(pl.multiple_of(jj * 256, 256), 256)
        grads = jnp.concatenate([r.cot_low[n, :, cols] for n in range(images)], axis=0)
        part = nn(r.act_t[...], grads).astype(bf16)
        for i in range(2):
            r.down_pay[i, lax.rem(jj, 2) * 2 + jj // 2] = part[:, i * LANES : (i + 1) * LANES]
        return c

    lax.fori_loop(0, width // 256, down_grads, 0)
    if fused:
        core_down = send(r.down_pay.at[1 - core], r.down_c, mate)

    total_sums, lat_sum, ext_total = None, None, None
    for blk in range(rows_all // half):
        at = slice(blk * half, (blk + 1) * half)
        grad_down = r.cot_low[2 * blk : 2 * blk + 2].reshape(half, width)
        grad_hidden = (r.cot_f[0, at, :] * nt(grad_down, r.down[...])).astype(bf16)
        r.gh[at, :] = grad_hidden
        grad_mid = nt(grad_hidden, r.up[...])
        mid_unit = r.mid_unit[at, :]
        cot = grad_down.astype(f32)
        grad_middle = cot + norm_back(grad_mid * r.vecs[4:5, :], mid_unit, r.mid_scale[at, :])
        branch = grad_middle.astype(bf16)
        r.branch[at, :] = branch
        part = [
            jnp.sum(v, axis=0, keepdims=True)
            for v in (cot, grad_hidden.astype(f32), branch.astype(f32), grad_mid * mid_unit, grad_mid)
        ]
        total_sums = part if total_sums is None else [u + v for u, v in zip(total_sums, part)]
        both = grad_middle[:own] + grad_middle[own:]
        lat_sum = both if lat_sum is None else lat_sum + both
        gx = nt(branch, r.wvo[...])
        r.gx[at, :] = gx
        part = [jnp.sum(gx * r.unit[at, :], axis=0, keepdims=True), jnp.sum(gx, axis=0, keepdims=True)]
        ext_total = part if ext_total is None else [u + v for u, v in zip(ext_total, part)]
    small = jnp.concatenate(
        total_sums
        + [jnp.pad(v, ((0, 0), (0, width - WIDE))) for v in ext_total]
        + [jnp.zeros((PACK - WIDE - 7, width), f32)],
        axis=0,
    ).astype(bf16)
    lat_low = lat_sum.astype(bf16)
    for d in range(width // LANES):
        cols = slice(d * LANES, (d + 1) * LANES)
        r.pack[d % 2, d // 2, WIDE:, :] = small[:, cols]
        r.up_pay[d % 2, d // 2, width:, :] = lat_low[:, cols]

    if fused:
        core_down.wait()
        for b in range(4):
            r.down_c[b] = r.down_c[b] + r.down_pay[core, b]
        first_down = send(r.down_c.at[pl.ds((1 - x) * 2, 2)], r.down_1, away(1)[1])

    def moments(jj, c):
        cols = pl.ds(pl.multiple_of(jj * 256, 256), 256)
        part = nn(r.px_t[...], r.branch[:, cols]).astype(bf16)
        for i in range(2):
            r.pack[i, jj, :WIDE] = part[:, i * LANES : (i + 1) * LANES]
        return c

    def up_grads(jj, c):
        cols = pl.ds(pl.multiple_of(jj * 256, 256), 256)
        part = nn(r.mid_t[...], r.gh[:, cols]).astype(bf16)
        for i in range(2):
            r.up_pay[i, jj, :width] = part[:, i * LANES : (i + 1) * LANES]
        return c

    lax.fori_loop(0, width // 256, moments, 0)
    if fused:
        core_pack = send(r.pack.at[1 - core], r.pack_c, mate)
    lax.fori_loop(0, width // 256, up_grads, 0)
    if fused:
        core_up = send(r.up_pay.at[1 - core], r.up_c, mate)

    gcb = jnp.zeros((own, WIDE), f32)
    levb = jnp.zeros((own, 1), f32)
    for n in range(images):
        at = slice(n * own, (n + 1) * own)
        gc = centred(r.gx[at, :] / r.tot[at, :] * gain, 1)
        gc_low = gc.astype(bf16)
        level = jnp.sum(gc_low.astype(f32) * r.unit[at, :], axis=1, keepdims=True)
        r.gc[at, :] = gc_low
        r.lev[at, :] = level
        r.ext[n * 16 : (n + 1) * 16, :] = nt(pick, gc_low).astype(bf16)
        gcb = gcb + gc * is_big[n]
        levb = levb + level * is_big[n]
    r.gcb[...] = gcb.astype(bf16)
    r.levb[...] = levb
    r.extb[:, own:] = nt(pick, r.gcb[...]).astype(bf16)
    r.extb[:, :own] = r.ext[images * 16 :, :]

    if fused:
        core_pack.wait()
        r.pack_c[...] = r.pack_c[...] + r.pack[core]
        quad_pack = send_quad(lambda q: r.pack_c.at[q], lambda k: r.pack_q.at[k - 1])
        core_up.wait()
        for b in range(4):
            r.up_c[b] = r.up_c[b] + r.up_pay[core, b]
        first_up = send(r.up_c.at[pl.ds((1 - y) * 2, 2)], r.up_1, away(2)[1])

    r.dq_sum[...] = jnp.zeros_like(r.dq_sum)
    r.rgbp[...] = jnp.zeros_like(r.rgbp)

    def backward(mixed, js):
        tiles, grads = [], []
        for j in js:
            tile = r.feat[j]
            scale = r.stat[j, 0:1, :]
            mean = r.stat[j, 1:2, :]
            low_weights = r.wst[j]
            weights = low_weights.astype(f32)
            raw = nn(r.qc[...], tile) * scale
            if mixed:
                segment = r.stat[j, 2:3, :]
                pulls = nn(r.gc[...], tile)
                pull = jnp.zeros_like(weights)
                level = jnp.zeros_like(weights)
                for n in range(images):
                    at = slice(n * own, (n + 1) * own)
                    here = segment == n
                    pull = jnp.where(here, pulls[at], pull)
                    level = jnp.where(here, r.lev[at, :], level)
            else:
                pull = nn(r.gcb[...], tile)
                level = r.levb[...]
            pull = pull * scale
            grad = weights * (pull - level)
            lean = jnp.sum(grad * raw + weights * pull, axis=0, keepdims=True) * (1.0 / FEAT)
            if mixed:
                colours = nn(r.ext[: images * 16, :], low_weights)
                back = nn(r.ext[images * 16 :, :], grad.astype(bf16))
                picked = jnp.zeros_like(back)
                for n in range(images):
                    picked = jnp.where(segment == n, colours[n * 16 : (n + 1) * 16], picked)
                back = back + picked
            else:
                back = nn(r.extb[...], jnp.concatenate([grad.astype(bf16), low_weights], axis=0))
            ext = tile[4 * BANDS :, :].astype(f32)
            part = (back - (ext - mean) * scale * lean) * scale
            for c in range(3):
                r.rgbp[c, pl.ds(j, 1), :] = part[c : c + 1]
            tiles.append(tile)
            grads.append((grad * scale).astype(bf16))
        r.dq_sum[...] += nt(side(tiles), side(grads))

    middle_tile = head + (tail - head) // 2 // BIG_UNROLL * BIG_UNROLL
    loop(0, head, partial(backward, True), HEAD_UNROLL)
    loop(head, middle_tile, partial(backward, False), BIG_UNROLL)
    if fused:
        pack_rows = PACK // parts
        mine = pl.ds(pl.multiple_of(place * pack_rows, 16), pack_rows)
        wait(quad_pack)
        r.pack_m[...] = summed(r.pack_c[quad], r.pack_q).astype(bf16)
        z_pack = send_z(
            lambda to: r.pack_m.at[pl.ds(pl.multiple_of(to * pack_rows, 16), pack_rows)], lambda s: r.pack_z.at[s - 1]
        )
        first_down.wait()
        for b in range(2):
            r.down_1[b] = r.down_1[b] + r.down_c[x * 2 + b]
        second_down = send(r.down_1.at[1 - y], r.down_2, away(2)[1])
    loop(middle_tile, tail, partial(backward, False), BIG_UNROLL)
    if fused:
        wait(z_pack)
        r.pack_own[...] = summed(r.pack_m[mine, :], r.pack_z).astype(bf16)
        r.pack_all[core, quad, mine, :] = r.pack_own[...]
        all_pack = send_z(lambda to: r.pack_own, lambda s: r.pack_all.at[core, quad, mine])
    loop(tail, last, partial(backward, True), HEAD_UNROLL)

    dq = r.dq_sum[...].T
    lanes = lax.broadcasted_iota(jnp.int32, dq.shape, 1)
    gs_sum = dq[:, FEAT : FEAT + 1] + dq[:, FEAT + 1 : FEAT + 2]
    dq = jnp.where(lanes == FEAT, gs_sum, centred(dq, 1)).astype(bf16)
    r.dq_pay[...] = jnp.zeros_like(r.dq_pay)
    each = own // 8
    for d in range(8):
        r.dq_pay[d % 2, d // 2, :, :WIDE] = dq[d * each : (d + 1) * each]
    if fused:
        core_dq = send(r.dq_pay.at[1 - core], r.dq_c, mate)

    for t in range(parts):
        r.rgb_send[t] = jnp.concatenate(
            [r.rgbp[c, t * per : (t + 1) * per, :] for c in range(3)] + [jnp.zeros((per, TILE), f32)], axis=0
        ).astype(bf16)
    back_copies = send_z(lambda to: r.rgb_send.at[to], lambda s: r.rgb_back.at[s - 1])

    if fused:
        core_dq.wait()
        r.dq_c[...] = r.dq_c[...] + r.dq_pay[core]
        quad_dq = send_quad(lambda q: r.dq_c.at[q], lambda k: r.dq_q.at[k - 1])
        wait(out_copies)
        unit, scale = norm(r.latents[...].astype(f32))
        r.mid_unit[...] = unit
        r.mid_scale[...] = scale
        lat_low = (unit * r.vecs[2:3, :] + r.vecs[3:4, :]).astype(bf16)
        r.cot_send[...] = lat_low.reshape(parts, own, width)
        queries = ((nn(lat_low, r.wq[...]) + r.vecs[0:1, :]) * factor).astype(bf16)
        r.out_send[...] = queries.reshape(parts, own, width)
        r.qk_all[...] = nt(queries, r.wk[...])
        wait(all_pack)
        all_pack = send_quad(lambda q: r.pack_all.at[core, quad], lambda k: r.pack_all.at[core, quad])
        first_up.wait()
        for b in range(2):
            r.up_1[b] = r.up_1[b] + r.up_c[y * 2 + b]
        second_up = send(r.up_1.at[1 - x], r.up_2, away(1)[1])
        wait(quad_dq)
        r.dq_own[...] = summed(r.dq_c[quad], r.dq_q).astype(bf16)
        r.dq_all[core, quad, place] = r.dq_own[...]
        z_dq = send_z(lambda to: r.dq_own, lambda s: r.dq_all.at[core, quad, place])
        second_down.wait()
        r.down_m[...] = (r.down_1[y].astype(f32) + r.down_2[...].astype(f32)).astype(bf16)
        z_down = send_z(
            lambda to: r.down_m.at[pl.ds(pl.multiple_of(to * chunk, 16), chunk)], lambda s: r.down_z.at[s - 1]
        )
        wait(z_dq)
        all_dq = send_quad(lambda q: r.dq_all.at[core, quad], lambda k: r.dq_all.at[core, quad])

    wait(back_copies)
    r.rgb_out[...] = summed(r.rgb_send[place], r.rgb_back).astype(bf16)

    if fused:
        wait(all_dq)
        all_dq = send(r.dq_all.at[core], r.dq_all.at[core], mate)
        wait(all_pack)
        all_pack = send(r.pack_all.at[core], r.pack_all.at[core], mate)
        second_up.wait()
        up_sum = r.up_1[x].astype(f32) + r.up_2[...].astype(f32)
        r.up_m[...] = up_sum[:width].astype(bf16)
        z_up = send_z(
            lambda to: r.up_m.at[pl.ds(pl.multiple_of(to * chunk, 16), chunk)], lambda s: r.up_z.at[s - 1]
        )
        all_dq.wait()

        for z in range(parts):
            for d in range(8):
                r.dq[(z * 8 + d) * each : (z * 8 + d + 1) * each, :] = r.dq_all[d % 2, d // 2, z]
        own_cols = pl.ds(pl.multiple_of(lax.rem(group, 8) * LANES, LANES), LANES)
        lat_cols = pl.ds(pl.multiple_of(place * chunk, LANES), chunk)
        units = r.dq[...].astype(f32)
        lean = units[:, FEAT : FEAT + 1]
        units = jnp.where(lax.broadcasted_iota(jnp.int32, units.shape, 1) < FEAT, units, 0.0)
        gain_sum = jnp.sum(r.qk_all[...] * units, axis=0, keepdims=True)
        bias_sum = jnp.sum(r.qk_all[...] * lean, axis=0, keepdims=True)
        dx = (units * r.feats[0:1, :] + lean * r.feats[1:2, :]).astype(bf16)
        order = order_of(264, DQ)
        r.key_out[...] = nn(nt(order, dx).astype(bf16), r.out_send[...].reshape(count, width))[:FEAT]
        gq = nn(dx, r.wk[...]) * factor
        gq_low = gq.astype(bf16)
        query_bias = jnp.sum(gq, axis=0, keepdims=True)
        grad_lat = nt(gq_low, r.wq[...])
        latent_gain = jnp.sum(grad_lat * r.mid_unit[...], axis=0, keepdims=True)
        latent_bias = jnp.sum(grad_lat, axis=0, keepdims=True)
        r.out_send[...] = gq_low.reshape(parts, own, width)
        r.query_out[...] = tn(
            r.cot_send[:, :, lat_cols].reshape(count, chunk), r.out_send[:, :, own_cols].reshape(count, LANES)
        )
        r.mid_unit[...] = norm_back(grad_lat * r.vecs[2:3, :], r.mid_unit[...], r.mid_scale[...])
        r.latents_out[...] = up_sum[width:] + r.mid_unit[rows, own_cols]

        all_pack.wait()
        for d in range(8):
            r.moment[:, d * LANES : (d + 1) * LANES] = r.pack_all[d % 2, d // 2]
        r.value_out[...] = nt(nn(order[:, :WIDE], r.moment[:WIDE, :]).astype(bf16), r.wo[...])[:FEAT]
        r.out_out[...] = tn(r.wv[:, lat_cols], r.moment[:WIDE, own_cols])
        small = r.moment[WIDE : WIDE + 16, :]
        value_bias = nt(small, r.wo[...])[2:3]
        small = small.astype(f32)
        r.vec_out[...] = jnp.concatenate(
            [small[:8], value_bias, query_bias, latent_gain, latent_bias, jnp.zeros((4, width), f32)], axis=0
        )
        ends_of = jnp.concatenate(
            [small[5:6, :DQ] + gain_sum, small[6:7, :DQ] + bias_sum, jnp.zeros((6, DQ), f32)], axis=0
        )
        r.ext_out[...] = moved(ends_of, order_of(DQ, DQ), nt)

        block = pl.ds(pl.multiple_of(place * chunk, 16), chunk)
        wait(z_down)
        r.down_out[...] = summed(r.down_m[block, :], r.down_z)
        wait(z_up)
        r.up_out[...] = summed(r.up_m[block, :], r.up_z)
    else:
        wait(out_copies)


def layer(images, slots, parts, fused, sizes, rgb, latents, wq, wo, up, down, wk, wv, cot, vecs):
    count, width = latents.shape
    own, chunk = count // parts, width // parts
    rows = images * own
    hidden = up.shape[1]
    tiles = slots // TILE
    last = tiles_of(images, slots)[2]
    each = own // 8
    any_, vm = pl.BlockSpec(memory_space=pl.ANY), pl.BlockSpec(memory_space=pltpu.VMEM)
    sds = jax.ShapeDtypeStruct
    V = pltpu.VMEM
    ins = [
        ("sizes", sizes, pl.BlockSpec(memory_space=pltpu.SMEM)), ("rgb_in", rgb, vm), ("latents", latents, vm),
        ("wq_h", wq, any_), ("wo_h", wo, any_), ("up_h", up, any_), ("down_h", down, any_),
        ("wk_in", wk, vm), ("wv_in", wv, vm), ("cot_h", cot, any_), ("vecs", vecs, vm),
    ]
    pays = [
        ("down_pay", (2, 4, hidden, LANES), bf16), ("up_pay", (2, 4, width + own, LANES), bf16),
        ("pack", (2, 4, PACK, LANES), bf16), ("dq_pay", (2, 4, each, DQ), bf16),
        ("wk", (DQ, width), bf16), ("wv", (WIDE, width), bf16), ("feats", (8, DQ), f32),
    ]
    outs = [("out_rows", (parts, own, width), bf16), ("rgb_out", rgb.shape, bf16)]
    scratch = [
        ("feat", (last, WIDE, TILE), bf16), ("stat", (last, 8, TILE), f32), ("wst", (last, own, TILE), bf16),
        ("rgb_recv", (parts - 1,) + rgb.shape, bf16), ("rgbf", (3, tiles, TILE), f32), ("rgbp", (3, tiles, TILE), f32),
        ("rgb_send", (parts,) + rgb.shape, bf16), ("rgb_back", (parts - 1,) + rgb.shape, bf16),
        ("wq", wq.shape, bf16), ("wo", wo.shape, bf16), ("up", up.shape, bf16), ("down", down.shape, bf16),
        ("cot_f", cot.shape, f32), ("cot_send", (parts, own, width), bf16), ("cot_low", (parts, own, width), bf16),
        ("out_send", (parts, own, width), bf16),
        ("qc", (own, WIDE), bf16), ("qb", (own, 1), f32), ("ext", (images * 16 + 16, own), bf16),
        ("extb", (16, 2 * own), bf16),
        ("acc", (WIDE, rows), f32), ("acc_big", (WIDE, own), f32), ("unit", (rows, WIDE), f32), ("px", (rows, WIDE), bf16),
        ("wvo", (WIDE, width), bf16), ("tot", (rows, 1), f32),
        ("mid_unit", (rows, width), f32), ("mid_scale", (rows, 1), f32),
        ("act_t", (hidden, rows), bf16), ("mid_t", (width, rows), bf16), ("px_t", (WIDE, rows), bf16),
        ("gh", (rows, hidden), bf16), ("branch", (rows, width), bf16), ("gx", (rows, WIDE), f32),
        ("gc", (rows, WIDE), bf16), ("gcb", (own, WIDE), bf16), ("lev", (rows, 1), f32), ("levb", (own, 1), f32),
        ("dq_sum", (WIDE, own), f32),
    ]
    if fused:
        outs += [
            ("down_out", (chunk, LANES), f32), ("up_out", (chunk, LANES), f32), ("out_out", (chunk, LANES), f32),
            ("query_out", (chunk, LANES), f32), ("latents_out", (own, LANES), f32), ("key_out", (FEAT, width), f32),
            ("value_out", (FEAT, width), f32), ("vec_out", (16, width), f32), ("ext_out", (8, DQ), f32),
        ]
        tall = width + own
        scratch += pays + [
            ("down_c", (4, hidden, LANES), bf16), ("down_1", (2, hidden, LANES), bf16), ("down_2", (hidden, LANES), bf16),
            ("down_m", (hidden, LANES), bf16), ("down_z", (parts - 1, chunk, LANES), bf16),
            ("up_c", (4, tall, LANES), bf16), ("up_1", (2, tall, LANES), bf16), ("up_2", (tall, LANES), bf16),
            ("up_m", (width, LANES), bf16), ("up_z", (parts - 1, chunk, LANES), bf16),
            ("pack_c", (4, PACK, LANES), bf16), ("pack_q", (3, PACK, LANES), bf16), ("pack_m", (PACK, LANES), bf16),
            ("pack_z", (parts - 1, PACK // parts, LANES), bf16), ("pack_own", (PACK // parts, LANES), bf16),
            ("pack_all", (2, 4, PACK, LANES), bf16),
            ("dq_c", (4, each, DQ), bf16), ("dq_q", (3, each, DQ), bf16), ("dq_own", (each, DQ), bf16),
            ("dq_all", (2, 4, parts, each, DQ), bf16), ("dq", (count, DQ), bf16), ("moment", (PACK, width), bf16),
            ("qk_all", (count, DQ), f32),
        ]
    else:
        outs += pays
    names = [n for n, _, _ in ins + outs + scratch] + ["load_sems", "sems"]
    return pl.pallas_call(
        partial(layer_kernel, images, slots, parts, fused, names),
        out_shape=tuple(sds(s, d) for _, s, d in outs),
        in_specs=[spec for _, _, spec in ins],
        out_specs=(vm,) * len(outs),
        scratch_shapes=[V(s, d) for _, s, d in scratch]
        + [pltpu.SemaphoreType.DMA((5,)), pltpu.SemaphoreType.DMA((2, SENDS))],
        compiler_params=pltpu.CompilerParams(collective_id=0, has_side_effects=True, vmem_limit_bytes=VMEM_LIMIT),
        name="layer",
    )(*[a for _, a, _ in ins])


def finish_kernel(moves, *refs):
    rows, rgb, vec, ext = refs[:4]
    whole = refs[4 : 4 + moves]
    lat_out, rgb_grad = refs[4 + moves : 6 + moves]
    whole_out = refs[6 + moves : 6 + 2 * moves]
    vec_out = refs[6 + 2 * moves : -1]
    sems = refs[-1]
    copies = [pltpu.make_async_copy(a, b, sems.at[i]) for i, (a, b) in enumerate(zip(whole, whole_out))]
    for copy in copies:
        copy.start()
    parts, own, width = rows.shape
    lat_out[0] = rows[...].reshape(parts * own, width).astype(f32)
    colours = rgb[...].astype(f32)
    per = rgb.shape[0] // 4
    rgb_grad[...] = jnp.concatenate(
        [
            jnp.concatenate([colours[c * per + j : c * per + j + 1] for j in range(per)], axis=1)
            for c in range(3)
        ],
        axis=0,
    ).astype(bf16)
    for i, out in enumerate(vec_out[:9]):
        out[...] = vec[i if i < 5 else i + 3, :]
    for i, out in enumerate(vec_out[9:]):
        out[...] = ext[i, :FEAT]
    wait(copies)


def finish(rows, rgb, vec, ext, *whole):
    parts, own, width = rows.shape
    any_, vm = pl.BlockSpec(memory_space=pl.ANY), pl.BlockSpec(memory_space=pltpu.VMEM)
    sds = jax.ShapeDtypeStruct
    n = len(whole)
    return pl.pallas_call(
        partial(finish_kernel, n),
        out_shape=(sds((1, parts * own, width), f32), sds((3, rgb.shape[0] // 4 * TILE), bf16))
        + tuple(sds(a.shape, a.dtype) for a in whole)
        + (sds((width,), f32),) * 9
        + (sds((FEAT,), f32),) * 2,
        in_specs=[vm] * 4 + [any_] * n,
        out_specs=(vm,) * 2 + (any_,) * n + (vm,) * 11,
        scratch_shapes=[pltpu.SemaphoreType.DMA((n,))],
        compiler_params=pltpu.CompilerParams(vmem_limit_bytes=32 * 2**20),
        name="finish",
    )(rows, rgb, vec, ext, *whole)


def restore(rows):
    b = 2 * BANDS
    return jnp.concatenate(
        [rows[2 * b : 2 * b + 4], rows[:b], rows[2 * b + 4 : 2 * b + 5], rows[b : 2 * b]], axis=0
    )


def sums_plain(parts, down_pay, up_pay, pack, dq, latents, wq, wo, wk, wv, vecs, feats):
    count, width = latents.shape
    own, chunk = count // parts, width // parts
    place, group, groups = lax.axis_index("pix"), lax.axis_index("dp"), lax.axis_size("dp")
    cols = width // groups
    factor = 1.0 / math.sqrt(width)

    def flat(a):
        return a.transpose(2, 1, 0, 3).reshape(a.shape[2], width).astype(f32)

    down_pay = down_pay.reshape(2, 2, 2, *down_pay.shape[2:]).transpose(0, 2, 1, 3, 4).reshape(down_pay.shape)

    def scattered(a):
        a = lax.psum_scatter(a, "dp", scatter_dimension=1, tiled=True)
        return lax.psum_scatter(a, "pix", scatter_dimension=0, tiled=True)

    up_all = flat(up_pay)
    down_total, up_total = scattered(flat(down_pay)), scattered(up_all[:width])
    latents_sum = lax.psum_scatter(up_all[width:], "dp", scatter_dimension=1, tiled=True)
    moment = lax.psum(flat(pack), ("dp", "pix"))
    small, moment = moment[WIDE : WIDE + 8], moment[:WIDE].astype(bf16)
    units = lax.psum(dq.transpose(1, 0, 2, 3).reshape(own, DQ).astype(f32), "dp")
    units = lax.all_gather(units, "pix", axis=0, tiled=True)

    unit, scale = norm(latents.astype(f32))
    lat_in = (unit * vecs[2] + vecs[3]).astype(bf16)
    queries = ((nn(lat_in, wq) + vecs[0]) * factor).astype(bf16)
    lean = units[:, FEAT : FEAT + 1]
    units = units * (jnp.arange(DQ) < FEAT)
    qk = nt(queries, wk)
    ext = jnp.zeros((8, DQ), f32)
    ext = ext.at[0].set(small[5, :DQ] + jnp.sum(qk * units, axis=0))
    ext = ext.at[1].set(small[6, :DQ] + jnp.sum(qk * lean, axis=0))
    dx = (units * feats[0] + lean * feats[1]).astype(bf16)
    key_total = restore(tn(dx, queries))
    gq = nn(dx, wk) * factor
    gq_low = gq.astype(bf16)
    grad_lat = nt(gq_low, wq)
    own_cols = lambda a: lax.dynamic_slice_in_dim(a, group * cols, cols, axis=1)
    own_rows = lambda a: lax.dynamic_slice_in_dim(a, place * chunk, chunk, axis=1)
    query_total = tn(own_rows(lat_in), own_cols(gq_low))
    back = norm_back(grad_lat * vecs[2], unit, scale)
    latents_total = latents_sum + own_cols(lax.dynamic_slice_in_dim(back, place * own, own, axis=0))
    value_total = restore(nt(moment, wo))
    out_total = tn(own_rows(wv), own_cols(moment))
    vec = jnp.concatenate(
        [
            small,
            nt(small.astype(bf16), wo)[2:3],
            jnp.sum(gq, axis=0, keepdims=True),
            jnp.sum(grad_lat * unit, axis=0, keepdims=True),
            jnp.sum(grad_lat, axis=0, keepdims=True),
        ],
        axis=0,
    )
    return down_total, up_total, out_total, query_total, latents_total, key_total, value_total, vec, ext

def shards(
    latents,
    pixel_rgb,
    coords,
    segment_ids,
    image_sizes,
    input_gain,
    input_bias,
    query_weight,
    query_bias,
    key_weight,
    value_weight,
    value_bias,
    out_weight,
    out_bias,
    latent_gain,
    latent_bias,
    mlp_gain,
    mlp_bias,
    up_weight,
    up_bias,
    down_weight,
    down_bias,
    cotangent,
):
    images = image_sizes.shape[1]
    width = latents.shape[1]
    parts = lax.axis_size("pix")
    slots = pixel_rgb.shape[1] * parts
    tiles = pixel_rgb.shape[1] // TILE
    rgb = jnp.pad(pixel_rgb.reshape(3, tiles, TILE), ((0, 1), (0, 0), (0, 0))).reshape(4 * tiles, TILE)
    fill = lambda v: jnp.pad(v, (0, width - FEAT))
    none = jnp.zeros((width,), f32)
    vecs = jnp.stack(
        [
            query_bias, out_bias, latent_gain, latent_bias, mlp_gain, mlp_bias, up_bias, down_bias,
            fill(input_gain), fill(input_bias), value_bias, none, none, none, none, none,
        ],
        axis=0,
    )
    fused = lax.axis_size("dp") == 8
    rows, rgb_out, *rest = layer(
        images, slots, parts, fused, image_sizes, rgb, latents, query_weight, out_weight, up_weight, down_weight,
        key_weight, value_weight, cotangent, vecs,
    )
    if fused:
        down, up, out, query, latents_sum, key, value, vec, ext = rest
        (
            latents_out, rgb_grad, down, up, out, query, latents_sum, key, value,
            db, ub, ob, mg, mb, vb, qb, lg, lb, gain, bias,
        ) = finish(rows, rgb_out, vec, ext, down, up, out, query, latents_sum, key, value)
    else:
        down, up, out, query, latents_sum, key, value, vec, ext = sums_plain(
            parts, *rest[:4], latents, query_weight, out_weight, rest[4], rest[5], vecs, rest[6]
        )
        latents_out = rows.reshape(1, latents.shape[0], width).astype(f32)
        rgb_grad = rgb_out.reshape(4, tiles, TILE)[:3].reshape(3, tiles * TILE)
        db, ub, ob, mg, mb = (vec[i] for i in range(5))
        vb, qb, lg, lb = (vec[i] for i in range(8, 12))
        gain, bias = restore(ext[0]), restore(ext[1])
    return (
        latents_out, rgb_grad, latents_sum, query, qb, key, value, vb, out, ob, lg, lb, mg, mb, up, ub, down, db,
        gain, bias,
    )


def solution(mesh):
    whole = P()
    placed = (
        whole,
        P(None, ("dp", "pix")),
        P(None, ("dp", "pix")),
        P(("dp", "pix")),
        P(None, "dp"),
    ) + (whole,) * 17 + (P(("dp", "pix"), None, None),)
    square = P("pix", "dp")
    return jax.shard_map(
        shards,
        mesh=mesh,
        in_specs=placed,
        out_specs=(
            P(("dp", "pix"), None, None),
            P(None, ("dp", "pix")),
            square,
            square,
            whole,
            whole,
            whole,
            whole,
            square,
            whole,
            whole,
            whole,
            whole,
            whole,
            square,
            whole,
            square,
            whole,
            whole,
            whole,
        ),
        check_vma=False,
    )
```

```python
from functools import partial
import math
from types import SimpleNamespace

import jax
import jax.numpy as jnp
from jax import lax
from jax.experimental import pallas as pl
from jax.experimental.pallas import tpu as pltpu
from jax.sharding import PartitionSpec as P

BANDS = 64
MAXRES = 224
BIG_SIDE = 112
SMALL_SIDE = 32
EPSILON = 1e-05
FEAT = 4 * BANDS + 5
WIDE = FEAT + 11
DQ = 384
PACK = 320
TILE = 512
LANES = 128
MESH = pl.DeviceIdType.MESH
SENDS = 55
VMEM_LIMIT = 62 * 2**20

bf16 = jnp.bfloat16
f32 = jnp.float32


def dot(a, b, dims):
    return lax.dot_general(a, b, (dims, ((), ())), preferred_element_type=f32)


def nn(a, b):
    return dot(a, b, ((1,), (0,)))


def nt(a, b):
    return dot(a, b, ((1,), (1,)))


def tn(a, b):
    return dot(a, b, ((0,), (0,)))


def order_of(rows, cols, flip=False):
    b = 2 * BANDS
    f = lax.broadcasted_iota(jnp.int32, (rows, cols), 1 if flip else 0)
    g = lax.broadcasted_iota(jnp.int32, (rows, cols), 0 if flip else 1)
    to = jnp.where(f < 4, f + 2 * b, jnp.where(f < 4 + b, f - 4, jnp.where(f == 4 + b, 2 * b + 4, f - 5)))
    return ((to == g) & (f < FEAT)).astype(bf16)


def moved(rows, order, product):
    total = None
    for _ in range(3):
        part = rows.astype(bf16)
        rows = rows - part.astype(f32)
        piece = product(part, order)
        total = piece if total is None else total + piece
    return total


def centred(rows, axis):
    live = lax.broadcasted_iota(jnp.int32, rows.shape, axis) < FEAT
    rows = jnp.where(live, rows, 0.0)
    return jnp.where(live, rows - jnp.sum(rows, axis=axis, keepdims=True) * (1.0 / FEAT), 0.0)


def norm(rows):
    centre = rows - jnp.mean(rows, axis=-1, keepdims=True)
    scale = lax.rsqrt(jnp.mean(centre * centre, axis=-1, keepdims=True) + EPSILON)
    return centre * scale, scale


def norm_back(grad, unit, scale):
    return (
        grad
        - jnp.mean(grad, axis=-1, keepdims=True)
        - unit * jnp.mean(grad * unit, axis=-1, keepdims=True)
    ) * scale


def tanh(a):
    return 1.0 - 2.0 / (1.0 + jnp.exp(jnp.minimum(2.0 * a, 80.0)))


def sin_cos_pi(p):
    n = jnp.floor(p + 0.5)
    z = (p - n) * math.pi
    q = z * z
    s = z * (1.0 + q * (-1.0 / 6 + q * (1.0 / 120 + q * (-1.0 / 5040 + q * (1.0 / 362880 - q * (1.0 / 39916800))))))
    c = 1.0 + q * (
        -0.5 + q * (1.0 / 24 + q * (-1.0 / 720 + q * (1.0 / 40320 + q * (-1.0 / 3628800 + q * (1.0 / 479001600)))))
    )
    sign = 1.0 - 2.0 * (n - 2.0 * jnp.floor(n * 0.5))
    return s * sign, c * sign


def tiles_of(images, slots):
    spare = (images - 1) * SMALL_SIDE * SMALL_SIDE
    head = -(-spare // TILE)
    tail = BIG_SIDE * BIG_SIDE // TILE
    last = min(-(-(BIG_SIDE * BIG_SIDE + spare) // TILE), slots // TILE)
    return head, max(head, tail), last


def loop(lo, hi, body, unroll):
    steps = (hi - lo) // unroll
    if steps > 0:
        lax.fori_loop(0, steps, lambda i, c: (body([lo + i * unroll + k for k in range(unroll)]), c)[1], 0)
    if lo + steps * unroll < hi:
        body(list(range(lo + steps * unroll, hi)))


def wait(copies):
    for copy in copies:
        copy.wait()


def summed(first, others):
    total = first.astype(f32)
    for i in range(others.shape[0]):
        total = total + others[i].astype(f32)
    return total


MLP_UNROLL = 2
HEAD_UNROLL = 2
BIG_UNROLL = 3


def layer_kernel(images, slots, parts, fused, names, *refs):
    r = SimpleNamespace(**dict(zip(names, refs)))
    group, place = lax.axis_index("dp"), lax.axis_index("pix")
    count, width = r.latents_h.shape
    own, chunk = count // parts, width // parts
    rows_all = images * own
    head, tail, last = tiles_of(images, slots)
    per = r.rgb_in.shape[0] // 4
    factor = 1.0 / math.sqrt(width)
    core, quad = lax.rem(group, 2), lax.rem(group // 2, 4)
    base = group // 8 * 4
    x, y = lax.rem(quad, 2), quad // 2
    mate = ((base + quad) * 2 + 1 - core, place)

    def away(k):
        other = (1 - x if k % 2 else x) + 2 * (1 - y if k // 2 else y)
        return other, ((base + other) * 2 + core, place)

    zs = [(s, lax.rem(place + s, parts), lax.rem(place + parts - s, parts)) for s in range(1, parts)]
    used = [0]

    def send(src, dst, target):
        i = used[0]
        used[0] += 1
        copy = pltpu.make_async_remote_copy(
            src_ref=src, dst_ref=dst, send_sem=r.sems.at[0, i], recv_sem=r.sems.at[1, i],
            device_id=target, device_id_type=MESH,
        )
        copy.start()
        return copy

    def send_z(pick, put):
        return [send(pick(to), put(s), (group, to)) for s, to, _ in zs]

    def send_quad(pick, put):
        return [send(pick(away(k)[0]), put(k), away(k)[1]) for k in (1, 2, 3)]

    barrier = pltpu.get_barrier_semaphore()
    friends = [(group, to) for _, to, _ in zs]
    if fused:
        friends += [mate] + [away(k)[1] for k in (1, 2, 3)]
    for device in friends:
        pl.semaphore_signal(barrier, inc=1, device_id=device, device_id_type=MESH)
    loads = [
        pltpu.make_async_copy(a, b, r.load_sems.at[i])
        for i, (a, b) in enumerate(
            (
                (r.wq_h, r.wq), (r.wo_h, r.wo), (r.cot_h, r.cot_f), (r.up_h, r.up), (r.down_h, r.down),
                (r.latents_h, r.latents), (r.wv_h, r.wv_in),
            )
        )
    ]
    for i in (5, 0, 6, 1, 2, 3, 4):
        loads[i].start()

    shades = r.pixel_rgb[...].astype(f32)
    pieces = [shades[c : c + 1, j * TILE : (j + 1) * TILE] for c in range(3) for j in range(per)]
    r.rgb_in[...] = jnp.concatenate(pieces + [jnp.zeros((per, TILE), f32)], axis=0).astype(bf16)
    r.vecs[...] = jnp.zeros_like(r.vecs)
    for i in range(11):
        vec = getattr(r, f"vec{i}")
        r.vecs[i : i + 1, : vec.shape[0]] = vec[...].reshape(1, vec.shape[0])

    to_waves = order_of(WIDE, FEAT, flip=True)
    r.wk[:WIDE] = nn(to_waves, r.wk_in[...]).astype(bf16)
    r.wk[WIDE:] = jnp.zeros_like(r.wk[WIDE:])
    feats = moved(r.vecs[8:16, :DQ], order_of(DQ, DQ), nn)
    r.feats[...] = feats
    gain, bias = feats[0:1, :WIDE], feats[1:2, :WIDE]

    pl.semaphore_wait(barrier, len(friends))
    rgb_copies = send_z(lambda to: r.rgb_in, lambda s: r.rgb_recv.at[s - 1])

    loads[5].wait()
    loads[0].wait()
    rows = pl.ds(pl.multiple_of(place * own, own), own)
    lat_rows = r.latents[rows, :].astype(f32)
    own_unit, _ = norm(lat_rows)
    own_in = (own_unit * r.vecs[2:3, :] + r.vecs[3:4, :]).astype(bf16)
    own_queries = ((nn(own_in, r.wq[...]) + r.vecs[0:1, :]) * factor).astype(bf16)
    qk = nt(own_queries, r.wk[:WIDE])
    qc = centred(qk * gain, 1).astype(bf16)
    r.qc[...] = qc
    r.qb[...] = jnp.sum(qk * bias, axis=1, keepdims=True)
    pick = (
        lax.broadcasted_iota(jnp.int32, (16, WIDE), 1)
        == lax.broadcasted_iota(jnp.int32, (16, WIDE), 0) + 4 * BANDS
    ).astype(bf16)
    r.ext[images * 16 :, :] = nt(pick, qc).astype(bf16)

    loads[6].wait()
    vb = r.vecs[10:11, :]
    vb_high = vb.astype(bf16).astype(f32)
    row = lax.broadcasted_iota(jnp.int32, (WIDE, width), 0)
    wv = nn(to_waves, r.wv_in[...])
    r.wv[...] = jnp.where(row == FEAT, vb_high, jnp.where(row == FEAT + 1, vb - vb_high, wv)).astype(bf16)

    wait(rgb_copies)
    for c in range(3):
        at = slice(c * per, (c + 1) * per)
        r.rgbf[c, pl.ds(pl.multiple_of(place * per, per), per), :] = r.rgb_in[at, :].astype(f32)
        for s, _, source in zs:
            r.rgbf[c, pl.ds(pl.multiple_of(source * per, per), per), :] = r.rgb_recv[s - 1, at, :].astype(f32)

    ends, high, wide = [], [], []
    end = jnp.int32(0)
    for i in range(images):
        end = end + r.sizes[0, i] * r.sizes[1, i]
        ends.append(end.astype(f32))
        high.append(jnp.maximum(r.sizes[0, i] - 1, 1).astype(f32))
        wide.append(r.sizes[1, i].astype(f32))
    is_big = [(r.sizes[0, n] > SMALL_SIDE).astype(f32) for n in range(images)]

    def features(j):
        shape = (8, TILE)
        lane = lax.broadcasted_iota(jnp.int32, shape, 1)
        sub = lax.broadcasted_iota(jnp.int32, shape, 0)
        slot = (lane + j * TILE).astype(f32)
        segment = jnp.zeros(shape, f32)
        start = jnp.zeros(shape, f32)
        tall = jnp.full(shape, high[0])
        across = jnp.full(shape, wide[0])
        for i in range(images):
            past = slot >= ends[i]
            segment = jnp.where(past, segment + 1.0, segment)
            if i + 1 < images:
                start = jnp.where(past, ends[i], start)
                tall = jnp.where(past, high[i + 1], tall)
                across = jnp.where(past, wide[i + 1], across)
            else:
                start = jnp.where(past, slot, start)
        local = slot - start
        row = jnp.floor((local + 0.5) / across)
        col = local - row * across
        y = 2.0 * row / tall - 1.0
        x = 2.0 * col / jnp.maximum(across - 1.0, 1.0) - 1.0
        step = (MAXRES / 2.0 - 1.0) / (BANDS - 1)
        lowest = 1.0 + sub.astype(f32) * step
        total = None
        pieces = []
        for spot in (y, x):
            s, c = sin_cos_pi(lowest * spot)
            rs, rc = sin_cos_pi((8 * step) * spot)
            sines, cosines = [s], [c]
            for _ in range(BANDS // 8 - 1):
                s, c = s * rc + c * rs, c * rc - s * rs
                sines.append(s)
                cosines.append(c)
            for k in range(BANDS // 8):
                total = sines[k] + cosines[k] if total is None else total + (sines[k] + cosines[k])
            pieces.append(jnp.concatenate(sines, axis=0).astype(bf16))
            pieces.append(jnp.concatenate(cosines, axis=0).astype(bf16))
        total = jnp.sum(total, axis=0, keepdims=True)
        red, green, blue = (r.rgbf[c, pl.ds(j, 1), :] for c in range(3))
        y, x, segment = y[0:1], x[0:1], segment[0:1]
        total = total + (red + green + blue + y + x)
        squares = red * red + green * green + blue * blue + y * y + x * x + 2.0 * BANDS
        mean = total * (1.0 / FEAT)
        spread = squares * (1.0 / FEAT) - mean * mean + EPSILON
        scale = lax.rsqrt(spread)
        deviation = spread * scale
        rest = deviation - deviation.astype(bf16).astype(f32)
        ext = jnp.zeros(shape, f32)
        for k, v in enumerate((red, green, blue, y, x, deviation, rest)):
            ext = jnp.where(sub == k, v, ext)
        pieces.append(jnp.concatenate([ext, jnp.zeros(shape, f32)], axis=0).astype(bf16))
        tile = jnp.concatenate(pieces, axis=0)
        r.feat[j] = tile
        r.stat[j] = jnp.where(sub == 0, scale, jnp.where(sub == 1, mean, segment))
        return tile, scale, segment

    r.acc[...] = jnp.zeros_like(r.acc)
    r.acc_big[...] = jnp.zeros_like(r.acc_big)

    def side(parts_of):
        return parts_of[0] if len(parts_of) == 1 else jnp.concatenate(parts_of, axis=1)

    def forward(mixed, js):
        tiles, mixes = [], []
        for j in js:
            tile, scale, segment = features(j)
            weights = jnp.exp(nn(r.qc[...], tile) * scale + r.qb[...])
            if mixed:
                weights = jnp.where(segment < images, weights, 0.0)
            r.wst[j] = weights.astype(bf16)
            scaled = (weights * scale).astype(bf16)
            if mixed:
                none = jnp.zeros_like(scaled)
                scaled = jnp.concatenate([jnp.where(segment == n, scaled, none) for n in range(images)], axis=0)
            tiles.append(tile)
            mixes.append(scaled)
        into = r.acc if mixed else r.acc_big
        into[...] += nt(side(tiles), side(mixes))

    loop(0, head, partial(forward, True), HEAD_UNROLL)
    loop(head, tail, partial(forward, False), BIG_UNROLL)
    loop(tail, last, partial(forward, True), HEAD_UNROLL)

    lane = lax.broadcasted_iota(jnp.int32, (own, WIDE), 1)
    ones = ((lane == FEAT) | (lane == FEAT + 1)).astype(f32)
    big = r.acc_big[...]
    mix_all = (r.acc[...] + jnp.concatenate([big * is_big[n] for n in range(images)], axis=1)).T
    for n in range(images):
        at = slice(n * own, (n + 1) * own)
        mix = mix_all[at]
        totals = mix[:, FEAT : FEAT + 1] + mix[:, FEAT + 1 : FEAT + 2]
        unit = centred(mix, 1) / totals
        r.tot[at, :] = totals
        r.unit[at, :] = unit
        r.px_send[n] = (unit * gain + bias + ones).astype(bf16).T
    px_copies = send_z(lambda to: r.px_send.at[to], lambda s: r.px_recv.at[place])
    r.px_recv[place] = r.px_send[place]

    loads[1].wait()
    wvo = nn(r.wv[...], r.wo[...])
    const = wvo[FEAT : FEAT + 1] + wvo[FEAT + 1 : FEAT + 2] + r.vecs[1:2, :]
    r.wvo[...] = jnp.where(row < FEAT, wvo, 0.0).astype(bf16)
    loads[2].wait()
    loads[3].wait()
    loads[4].wait()
    k = math.sqrt(2.0 / math.pi)
    half = 2 * own
    wait(px_copies)
    out_copies = []
    for blk in range(count // half):
        at = slice(blk * half, (blk + 1) * half)
        px_t = jnp.concatenate([r.px_recv[2 * blk + i] for i in range(2)], axis=1)
        r.px_t[:, at] = px_t
        middle = r.latents[at, :].astype(f32) + nn(px_t.T, r.wvo[...]) + const
        mid_unit, mid_scale = norm(middle)
        mid_in = (mid_unit * r.vecs[4:5, :] + r.vecs[5:6, :]).astype(bf16)
        hidden = nn(mid_in, r.up[...]) + r.vecs[6:7, :]
        th = tanh(k * (hidden + 0.044715 * hidden * hidden * hidden))
        active = (0.5 * hidden * (1.0 + th)).astype(bf16)
        r.slope[at, :] = 0.5 * (1.0 + th) + 0.5 * hidden * (1.0 - th * th) * k * (
            1.0 + 3 * 0.044715 * hidden * hidden
        )
        stage = (r.key_out, r.value_out)[blk].at[pl.ds(0, half)] if fused else (r.stage0, r.stage1)[blk]
        stage[...] = middle + nn(active, r.down[...]) + r.vecs[7:8, :]
        copy = pltpu.make_async_copy(stage, r.out_rows.at[0, pl.ds(blk * half, half)], r.load_sems.at[7 + blk])
        copy.start()
        out_copies.append(copy)
        r.mid_unit[at, :] = mid_unit
        r.mid_scale[at, :] = mid_scale
        r.act_t[:, at] = active.T
        r.mid_t[:, at] = mid_in.T

    def down_grads(jj, c):
        cols = pl.ds(pl.multiple_of(jj * 256, 256), 256)
        part = nn(r.act_t[...], r.cot_f[0, :, cols].astype(bf16)).astype(bf16)
        for i in range(2):
            r.down_pay[i, lax.rem(jj, 2) * 2 + jj // 2] = part[:, i * LANES : (i + 1) * LANES]
        return c

    lax.fori_loop(0, width // 256, down_grads, 0)
    if fused:
        core_down = send(r.down_pay.at[1 - core], r.down_c, mate)

    def fold(first, value):
        for i in range(width // count):
            r.act_t[i * count + first : i * count + first + value.shape[0], :] = value[:, i * count : (i + 1) * count]

    def unfold(first, size):
        at = pl.ds(pl.multiple_of(first // count * count, count), count)
        return r.act_t[at, pl.ds(pl.multiple_of(lax.rem(first, count), LANES), size)]

    total_sums, ext_total = None, None
    for blk in range(count // half):
        at = slice(blk * half, (blk + 1) * half)
        grad_down = r.cot_f[0, at, :].astype(bf16)
        grad_hidden = (r.slope[at, :] * nt(grad_down, r.down[...])).astype(bf16)
        fold(blk * half, grad_hidden)
        grad_mid = nt(grad_hidden, r.up[...])
        mid_unit = r.mid_unit[at, :]
        grad_middle = r.cot_f[0, at, :] + norm_back(grad_mid * r.vecs[4:5, :], mid_unit, r.mid_scale[at, :])
        branch = grad_middle.astype(bf16)
        r.branch[at, :] = branch
        for d in range(width // LANES):
            q = d // 2
            r.lat_pay[d % 2, q % 2 * 2 + q // 2, at, :] = branch[:, d * LANES : (d + 1) * LANES]
        part = [
            jnp.sum(v, axis=0, keepdims=True)
            for v in (grad_down.astype(f32), grad_hidden.astype(f32), branch.astype(f32), grad_mid * mid_unit, grad_mid)
        ]
        total_sums = part if total_sums is None else [u + v for u, v in zip(total_sums, part)]
        gx = nt(r.wvo[...], branch)
        r.px_send[2 * blk] = gx[:, :own].astype(bf16)
        r.px_send[2 * blk + 1] = gx[:, own:].astype(bf16)
        part = [jnp.sum(gx * r.px_t[:, at].astype(f32), axis=1, keepdims=True), jnp.sum(gx, axis=1, keepdims=True)]
        ext_total = part if ext_total is None else [u + v for u, v in zip(ext_total, part)]
    gx_copies = send_z(lambda to: r.px_send.at[to], lambda s: r.gx_recv.at[place])
    r.gx_recv[place] = r.px_send[place]
    lane = lax.broadcasted_iota(jnp.int32, (WIDE, LANES), 1)
    ext_rows = jnp.where(lane == 0, ext_total[0], jnp.where(lane == 1, ext_total[1], 0.0)).T
    live = lax.broadcasted_iota(jnp.int32, (1, WIDE), 1) < FEAT
    gain_part = jnp.where(live, (ext_rows[0:1] - bias * ext_rows[1:2]) / jnp.where(live, gain, 1.0), 0.0)
    small = jnp.concatenate(
        total_sums
        + [jnp.pad(v, ((0, 0), (0, width - WIDE))) for v in (gain_part, jnp.where(live, ext_rows[1:2], 0.0))]
        + [jnp.zeros((PACK - WIDE - 7, width), f32)],
        axis=0,
    ).astype(bf16)
    for d in range(width // LANES):
        r.pack[d % 2, d // 2, WIDE:, :] = small[:, d * LANES : (d + 1) * LANES]

    if fused:
        core_down.wait()
        for b in range(4):
            r.down_c[b] = r.down_c[b] + r.down_pay[core, b]
        first_down = send(r.down_c.at[pl.ds((1 - x) * 2, 2)], r.down_1, away(1)[1])

    def moments(jj, c):
        cols = pl.ds(pl.multiple_of(jj * 256, 256), 256)
        part = nn(r.px_t[...], r.branch[:, cols]).astype(bf16)
        for i in range(2):
            r.pack[i, jj, :WIDE] = part[:, i * LANES : (i + 1) * LANES]
        return c

    def up_grads(jj, c):
        cols = pl.ds(pl.multiple_of(jj * 256, 256), 256)
        part = nn(r.mid_t[...], unfold(jj * 256, 256)).astype(bf16)
        for i in range(2):
            r.up_pay[i, jj] = part[:, i * LANES : (i + 1) * LANES]
        return c

    lax.fori_loop(0, width // 256, moments, 0)
    if fused:
        core_pack = send(r.pack.at[1 - core], r.pack_c, mate)
        core_lat = send(r.lat_pay.at[1 - core], r.lat_c, mate)
    lax.fori_loop(0, width // 256, up_grads, 0)
    if fused:
        core_up = send(r.up_pay.at[1 - core], r.up_c, mate)

    if fused:
        unit, scale = norm(r.latents[...].astype(f32))
        r.mid_unit[...] = unit
        r.mid_scale[...] = scale
        lat_low = (unit * r.vecs[2:3, :] + r.vecs[3:4, :]).astype(bf16)
        fold(0, lat_low)
        queries = ((nn(lat_low, r.wq[...]) + r.vecs[0:1, :]) * factor).astype(bf16)
        r.branch[...] = queries
        r.qk_all[...] = nt(queries, r.wk[...])
    wait(gx_copies)
    gcb = jnp.zeros((own, WIDE), f32)
    levb = jnp.zeros((own, 1), f32)
    for n in range(images):
        at = slice(n * own, (n + 1) * own)
        gc = centred(r.gx_recv[n].T.astype(f32) * gain, 1) / r.tot[at, :]
        gc_low = gc.astype(bf16)
        level = jnp.sum(gc_low.astype(f32) * r.unit[at, :], axis=1, keepdims=True)
        r.gc[at, :] = gc_low
        r.lev[at, :] = level
        r.ext[n * 16 : (n + 1) * 16, :] = nt(pick, gc_low).astype(bf16)
        gcb = gcb + gc * is_big[n]
        levb = levb + level * is_big[n]
    r.gc[rows_all :, :] = r.qc[...]
    r.gcb[:own, :] = gcb.astype(bf16)
    r.gcb[own:, :] = r.qc[...]
    r.levb[...] = levb
    r.extb[:, own:] = nt(pick, r.gcb[:own, :]).astype(bf16)
    r.extb[:, :own] = r.ext[images * 16 :, :]

    if fused:
        core_pack.wait()
        r.pack_c[...] = r.pack_c[...] + r.pack[core]
        quad_pack = send_quad(lambda q: r.pack_c.at[q], lambda k: r.pack_q.at[k - 1])
        core_lat.wait()
        for b in range(4):
            r.lat_c[b] = r.lat_c[b] + r.lat_pay[core, b]
        first_lat = send(r.lat_c.at[pl.ds((1 - x) * 2, 2)], r.lat_1, away(1)[1])
        core_up.wait()
        for b in range(4):
            r.up_c[b] = r.up_c[b] + r.up_pay[core, b]
        first_up = send(r.up_c.at[pl.ds((1 - y) * 2, 2)], r.up_1, away(2)[1])

    r.dq_sum[...] = jnp.zeros_like(r.dq_sum)
    r.rgbp[...] = jnp.zeros_like(r.rgbp)

    def backward(mixed, js):
        tiles, grads = [], []
        for j in js:
            tile = r.feat[j]
            scale = r.stat[j, 0:1, :]
            mean = r.stat[j, 1:2, :]
            low_weights = r.wst[j]
            weights = low_weights.astype(f32)
            pulls = nn(r.gc[...] if mixed else r.gcb[...], tile)
            raw = pulls[-own:] * scale
            if mixed:
                segment = r.stat[j, 2:3, :]
                pull = jnp.zeros_like(weights)
                level = jnp.zeros_like(weights)
                for n in range(images):
                    at = slice(n * own, (n + 1) * own)
                    here = segment == n
                    pull = jnp.where(here, pulls[at], pull)
                    level = jnp.where(here, r.lev[at, :], level)
            else:
                pull = pulls[:own]
                level = r.levb[...]
            pull = pull * scale
            grad = weights * (pull - level)
            lean = jnp.sum(grad * raw + weights * pull, axis=0, keepdims=True) * (1.0 / FEAT)
            if mixed:
                colours = nn(r.ext[: images * 16, :], low_weights)
                back = nn(r.ext[images * 16 :, :], grad.astype(bf16))
                picked = jnp.zeros_like(back)
                for n in range(images):
                    picked = jnp.where(segment == n, colours[n * 16 : (n + 1) * 16], picked)
                back = back + picked
            else:
                back = nn(r.extb[...], jnp.concatenate([grad.astype(bf16), low_weights], axis=0))
            ext = tile[4 * BANDS :, :].astype(f32)
            part = (back - (ext - mean) * scale * lean) * scale
            for c in range(3):
                r.rgbp[c, pl.ds(j, 1), :] = part[c : c + 1]
            tiles.append(tile)
            grads.append((grad * scale).astype(bf16))
        r.dq_sum[...] += nt(side(tiles), side(grads))

    step = 2 * BIG_UNROLL
    loop(0, head, partial(backward, True), HEAD_UNROLL)
    loop(head, head + BIG_UNROLL, partial(backward, False), BIG_UNROLL)
    if fused:
        pack_rows = PACK // parts
        mine = pl.ds(pl.multiple_of(place * pack_rows, 16), pack_rows)
        wait(quad_pack)
        r.pack_m[...] = summed(r.pack_c[quad], r.pack_q).astype(bf16)
        z_pack = send_z(
            lambda to: r.pack_m.at[pl.ds(pl.multiple_of(to * pack_rows, 16), pack_rows)], lambda s: r.pack_z.at[s - 1]
        )
    at = head + BIG_UNROLL
    loop(at, at + step, partial(backward, False), BIG_UNROLL)
    if fused:
        first_down.wait()
        for b in range(2):
            r.down_1[b] = r.down_1[b] + r.down_c[x * 2 + b]
        second_down = send(r.down_1.at[1 - y], r.down_2, away(2)[1])
        wait(z_pack)
        r.pack_own[...] = summed(r.pack_m[mine, :], r.pack_z).astype(bf16)
        r.pack_all[core, quad, mine, :] = r.pack_own[...]
        all_pack = send_z(lambda to: r.pack_own, lambda s: r.pack_all.at[core, quad, mine])
    loop(at + step, at + 2 * step, partial(backward, False), BIG_UNROLL)
    if fused:
        wait(all_pack)
        all_pack = send_quad(lambda q: r.pack_all.at[core, quad], lambda k: r.pack_all.at[core, quad])
        first_lat.wait()
        for b in range(2):
            r.lat_1[b] = r.lat_1[b] + r.lat_c[x * 2 + b]
        second_lat = send(r.lat_1.at[1 - y], r.lat_2, away(2)[1])
        first_up.wait()
        for b in range(2):
            r.up_1[b] = r.up_1[b] + r.up_c[y * 2 + b]
        second_up = send(r.up_1.at[1 - x], r.up_2, away(1)[1])
    loop(at + 2 * step, tail, partial(backward, False), BIG_UNROLL)
    if fused:
        second_down.wait()
        r.down_2[...] = (r.down_1[y].astype(f32) + r.down_2[...].astype(f32)).astype(bf16)
        z_down = send_z(
            lambda to: r.down_2.at[pl.ds(pl.multiple_of(to * chunk, 16), chunk)], lambda s: r.down_z.at[s - 1]
        )
    loop(tail, last, partial(backward, True), HEAD_UNROLL)

    dq = r.dq_sum[...].T
    lanes = lax.broadcasted_iota(jnp.int32, dq.shape, 1)
    gs_sum = dq[:, FEAT : FEAT + 1] + dq[:, FEAT + 1 : FEAT + 2]
    dq = jnp.where(lanes == FEAT, gs_sum, centred(dq, 1)).astype(bf16)
    r.dq_pay[...] = jnp.zeros_like(r.dq_pay)
    each = own // 8
    for d in range(8):
        r.dq_pay[d % 2, d // 2, :, :WIDE] = dq[d * each : (d + 1) * each]
    if fused:
        core_dq = send(r.dq_pay.at[1 - core], r.dq_c, mate)

    for t in range(parts):
        r.rgb_send[t] = jnp.concatenate(
            [r.rgbp[c, t * per : (t + 1) * per, :] for c in range(3)] + [jnp.zeros((per, TILE), f32)], axis=0
        ).astype(bf16)
    back_copies = send_z(lambda to: r.rgb_send.at[to], lambda s: r.rgb_back.at[s - 1])

    if fused:
        core_dq.wait()
        r.dq_c[...] = r.dq_c[...] + r.dq_pay[core]
        quad_dq = send_quad(lambda q: r.dq_c.at[q], lambda k: r.dq_q.at[k - 1])
        wait(all_pack)
        all_pack = send(r.pack_all.at[core], r.pack_all.at[core], mate)
        wait(quad_dq)
        r.dq_own[...] = summed(r.dq_c[quad], r.dq_q).astype(bf16)
        r.dq_all[core, quad, place] = r.dq_own[...]
        z_dq = send_z(lambda to: r.dq_own, lambda s: r.dq_all.at[core, quad, place])
        all_pack.wait()

        own_cols = pl.ds(pl.multiple_of(lax.rem(group, 8) * LANES, LANES), LANES)
        lat_cols = pl.ds(pl.multiple_of(place * chunk, LANES), chunk)
        for d in range(8):
            r.moment[:, d * LANES : (d + 1) * LANES] = r.pack_all[d % 2, d // 2]
        order = order_of(264, DQ)
        wait(out_copies)
        r.value_out[...] = nt(nn(order[:, :WIDE], r.moment[:WIDE, :]).astype(bf16), r.wo[...])[:FEAT]
        r.out_out[...] = tn(r.wv[:, lat_cols], r.moment[:WIDE, own_cols])
        small = r.moment[WIDE : WIDE + 16, :]
        value_bias = nt(small, r.wo[...])[2:3]
        small = small.astype(f32)
        wait(z_dq)
        all_dq = send_quad(lambda q: r.dq_all.at[core, quad], lambda k: r.dq_all.at[core, quad])

        second_up.wait()
        r.up_2[...] = (r.up_1[x].astype(f32) + r.up_2[...].astype(f32)).astype(bf16)
        z_up = send_z(
            lambda to: r.up_2.at[pl.ds(pl.multiple_of(to * chunk, 16), chunk)], lambda s: r.up_z.at[s - 1]
        )
        second_lat.wait()
        r.lat_2[...] = (r.lat_1[y].astype(f32) + r.lat_2[...].astype(f32)).astype(bf16)
        z_lat = send_z(
            lambda to: r.lat_2.at[pl.ds(pl.multiple_of(to * own, 16), own)], lambda s: r.lat_z.at[s - 1]
        )
    wait(back_copies)
    r.rgb_out[...] = summed(r.rgb_send[place], r.rgb_back).astype(bf16)

    if fused:
        block = pl.ds(pl.multiple_of(place * chunk, 16), chunk)
        wait(z_down)
        r.down_out[...] = summed(r.down_2[block, :], r.down_z)
        wait(all_dq)
        all_dq = send(r.dq_all.at[core], r.dq_all.at[core], mate)
        all_dq.wait()

        for z in range(parts):
            for d in range(8):
                r.dq[(z * 8 + d) * each : (z * 8 + d + 1) * each, :] = r.dq_all[d % 2, d // 2, z]
        units = r.dq[...].astype(f32)
        lean = units[:, FEAT : FEAT + 1]
        units = jnp.where(lax.broadcasted_iota(jnp.int32, units.shape, 1) < FEAT, units, 0.0)
        gain_sum = jnp.sum(r.qk_all[...] * units, axis=0, keepdims=True)
        bias_sum = jnp.sum(r.qk_all[...] * lean, axis=0, keepdims=True)
        dx = (units * r.feats[0:1, :] + lean * r.feats[1:2, :]).astype(bf16)
        r.key_out[...] = nn(nt(order, dx).astype(bf16), r.branch[...])[:FEAT]
        gq = nn(dx, r.wk[...]) * factor
        gq_low = gq.astype(bf16)
        query_bias = jnp.sum(gq, axis=0, keepdims=True)
        grad_lat = nt(gq_low, r.wq[...])
        latent_gain = jnp.sum(grad_lat * r.mid_unit[...], axis=0, keepdims=True)
        latent_bias = jnp.sum(grad_lat, axis=0, keepdims=True)
        r.branch[...] = gq_low
        r.query_out[...] = tn(unfold(place * chunk, chunk), r.branch[:, own_cols])
        r.mid_unit[...] = norm_back(grad_lat * r.vecs[2:3, :], r.mid_unit[...], r.mid_scale[...])

        r.vec_out[...] = jnp.concatenate(
            [small[:8], value_bias, query_bias, latent_gain, latent_bias, jnp.zeros((4, width), f32)], axis=0
        )
        ends_of = jnp.concatenate(
            [small[5:6, :DQ] + gain_sum, small[6:7, :DQ] + bias_sum, jnp.zeros((6, DQ), f32)], axis=0
        )
        r.ext_out[...] = moved(ends_of, order_of(DQ, DQ), nt)

        wait(z_up)
        r.up_out[...] = summed(r.up_2[block, :], r.up_z)
        wait(z_lat)
        r.latents_out[...] = summed(r.lat_2[rows, :], r.lat_z) + r.mid_unit[rows, own_cols]
    else:
        wait(out_copies)


def layer(images, slots, parts, fused, sizes, pixel_rgb, latents, wq, wo, up, down, wk, wv, cot, vectors):
    count, width = latents.shape
    own, chunk = count // parts, width // parts
    rows = images * own
    hidden = up.shape[1]
    tiles = slots // TILE
    colours = (4 * tiles // parts, TILE)
    last = tiles_of(images, slots)[2]
    each = own // 8
    any_, vm = pl.BlockSpec(memory_space=pl.ANY), pl.BlockSpec(memory_space=pltpu.VMEM)
    sds = jax.ShapeDtypeStruct
    V = pltpu.VMEM
    ins = [
        ("sizes", sizes, pl.BlockSpec(memory_space=pltpu.SMEM)), ("pixel_rgb", pixel_rgb, vm), ("latents_h", latents, any_),
        ("wq_h", wq, any_), ("wo_h", wo, any_), ("up_h", up, any_), ("down_h", down, any_),
        ("wk_in", wk, vm), ("wv_h", wv, any_), ("cot_h", cot, any_),
    ] + [(f"vec{i}", v, vm) for i, v in enumerate(vectors)]
    pays = [
        ("down_pay", (2, 4, hidden, LANES), bf16), ("up_pay", (2, 4, width, LANES), bf16), ("lat_pay", (2, 4, count, LANES), bf16),
        ("pack", (2, 4, PACK, LANES), bf16), ("dq_pay", (2, 4, each, DQ), bf16),
        ("wk", (DQ, width), bf16), ("wv", (WIDE, width), bf16), ("feats", (8, DQ), f32),
    ]
    outs = [("out_rows", cot.shape, f32), ("rgb_out", colours, bf16)]
    scratch = [
        ("feat", (last, WIDE, TILE), bf16), ("stat", (last, 8, TILE), f32), ("wst", (last, own, TILE), bf16),
        ("rgb_in", colours, bf16), ("vecs", (16, width), f32), ("rgb_recv", (parts - 1,) + colours, bf16), ("rgbf", (3, tiles, TILE), f32), ("rgbp", (3, tiles, TILE), f32),
        ("rgb_send", (parts,) + colours, bf16), ("rgb_back", (parts - 1,) + colours, bf16),
        ("latents", latents.shape, bf16), ("wv_in", wv.shape, bf16), ("wq", wq.shape, bf16), ("wo", wo.shape, bf16), ("up", up.shape, bf16), ("down", down.shape, bf16),
        ("cot_f", cot.shape, f32), ("slope", (count, hidden), f32),
        ("px_send", (images, WIDE, own), bf16), ("px_recv", (parts, WIDE, own), bf16),
        ("gx_recv", (images, WIDE, own), bf16),
        ("qc", (own, WIDE), bf16), ("qb", (own, 1), f32), ("ext", (images * 16 + 16, own), bf16),
        ("extb", (16, 2 * own), bf16),
        ("acc", (WIDE, rows), f32), ("acc_big", (WIDE, own), f32), ("unit", (rows, WIDE), f32),
        ("wvo", (WIDE, width), bf16), ("tot", (rows, 1), f32),
        ("mid_unit", (count, width), f32), ("mid_scale", (count, 1), f32),
        ("act_t", (hidden, count), bf16), ("mid_t", (width, count), bf16), ("px_t", (WIDE, count), bf16),
        ("branch", (count, width), bf16),
        ("gc", (rows + own, WIDE), bf16), ("gcb", (2 * own, WIDE), bf16), ("lev", (rows, 1), f32), ("levb", (own, 1), f32),
        ("dq_sum", (WIDE, own), f32),
    ]
    if fused:
        outs += [
            ("down_out", (chunk, LANES), f32), ("up_out", (chunk, LANES), f32), ("out_out", (chunk, LANES), f32),
            ("query_out", (chunk, LANES), f32), ("latents_out", (own, LANES), f32), ("key_out", (FEAT, width), f32),
            ("value_out", (FEAT, width), f32), ("vec_out", (16, width), f32), ("ext_out", (8, DQ), f32),
        ]
        scratch += pays + [
            ("down_c", (4, hidden, LANES), bf16), ("down_1", (2, hidden, LANES), bf16), ("down_2", (hidden, LANES), bf16),
            ("down_z", (parts - 1, chunk, LANES), bf16),
            ("up_c", (4, width, LANES), bf16), ("up_1", (2, width, LANES), bf16), ("up_2", (width, LANES), bf16),
            ("lat_c", (4, count, LANES), bf16), ("lat_1", (2, count, LANES), bf16), ("lat_2", (count, LANES), bf16),
            ("up_z", (parts - 1, chunk, LANES), bf16),
            ("lat_z", (parts - 1, own, LANES), bf16),
            ("pack_c", (4, PACK, LANES), bf16), ("pack_q", (3, PACK, LANES), bf16), ("pack_m", (PACK, LANES), bf16),
            ("pack_z", (parts - 1, PACK // parts, LANES), bf16), ("pack_own", (PACK // parts, LANES), bf16),
            ("pack_all", (2, 4, PACK, LANES), bf16),
            ("dq_c", (4, each, DQ), bf16), ("dq_q", (3, each, DQ), bf16), ("dq_own", (each, DQ), bf16),
            ("dq_all", (2, 4, parts, each, DQ), bf16), ("dq", (count, DQ), bf16), ("moment", (PACK, width), bf16),
            ("qk_all", (count, DQ), f32),
        ]
    else:
        outs += pays
        scratch += [("stage0", (2 * own, width), f32), ("stage1", (2 * own, width), f32)]
    names = [n for n, _, _ in ins + outs + scratch] + ["load_sems", "sems"]
    return pl.pallas_call(
        partial(layer_kernel, images, slots, parts, fused, names),
        out_shape=tuple(sds(s, d) for _, s, d in outs),
        in_specs=[spec for _, _, spec in ins],
        out_specs=(any_,) + (vm,) * (len(outs) - 1),
        scratch_shapes=[V(s, d) for _, s, d in scratch]
        + [pltpu.SemaphoreType.DMA((9,)), pltpu.SemaphoreType.DMA((2, SENDS))],
        compiler_params=pltpu.CompilerParams(collective_id=0, has_side_effects=True, vmem_limit_bytes=VMEM_LIMIT),
        name="layer",
    )(*[a for _, a, _ in ins])


def finish_kernel(moves, rgb, vec, ext, *refs):
    whole, whole_out = refs[:moves], refs[moves : 2 * moves]
    rgb_grad, *vec_out = refs[2 * moves : -moves - 1]
    held, sems = refs[-moves - 1 : -1], refs[-1]
    ins = [pltpu.make_async_copy(a, b, sems.at[0, i]) for i, (a, b) in enumerate(zip(whole, held))]
    outs = [pltpu.make_async_copy(a, b, sems.at[1, i]) for i, (a, b) in enumerate(zip(held, whole_out))]
    for copy in ins:
        copy.start()
    colours = rgb[...].astype(f32)
    per = rgb.shape[0] // 4
    rgb_grad[...] = jnp.concatenate(
        [
            jnp.concatenate([colours[c * per + j : c * per + j + 1] for j in range(per)], axis=1)
            for c in range(3)
        ],
        axis=0,
    ).astype(bf16)
    for i, out in enumerate(vec_out[:9]):
        out[...] = vec[i if i < 5 else i + 3, :]
    for i, out in enumerate(vec_out[9:]):
        out[...] = ext[i, :FEAT]
    for copy, out in zip(ins, outs):
        copy.wait()
        out.start()
    wait(outs)


def finish(rgb, vec, ext, *whole):
    width = vec.shape[1]
    any_, vm = pl.BlockSpec(memory_space=pl.ANY), pl.BlockSpec(memory_space=pltpu.VMEM)
    sds = jax.ShapeDtypeStruct
    n = len(whole)
    outs = (
        tuple(sds(a.shape, a.dtype) for a in whole)
        + (sds((3, rgb.shape[0] // 4 * TILE), bf16),)
        + (sds((width,), f32),) * 9
        + (sds((FEAT,), f32),) * 2
    )
    return pl.pallas_call(
        partial(finish_kernel, n),
        out_shape=outs,
        in_specs=[vm] * 3 + [any_] * n,
        out_specs=(any_,) * n + (vm,) * (len(outs) - n),
        scratch_shapes=[pltpu.VMEM(a.shape, a.dtype) for a in whole] + [pltpu.SemaphoreType.DMA((2, n))],
        compiler_params=pltpu.CompilerParams(vmem_limit_bytes=VMEM_LIMIT),
        name="finish",
    )(rgb, vec, ext, *whole)


def restore(rows):
    b = 2 * BANDS
    return jnp.concatenate(
        [rows[2 * b : 2 * b + 4], rows[:b], rows[2 * b + 4 : 2 * b + 5], rows[b : 2 * b]], axis=0
    )


def sums_plain(parts, down_pay, up_pay, lat_pay, pack, dq, latents, wq, wo, wk, wv, vecs, feats):
    count, width = latents.shape
    own, chunk = count // parts, width // parts
    place, group, groups = lax.axis_index("pix"), lax.axis_index("dp"), lax.axis_size("dp")
    cols = width // groups
    factor = 1.0 / math.sqrt(width)

    def flat(a):
        return a.transpose(2, 1, 0, 3).reshape(a.shape[2], width).astype(f32)

    def scattered(a):
        a = lax.psum_scatter(a, "dp", scatter_dimension=1, tiled=True)
        return lax.psum_scatter(a, "pix", scatter_dimension=0, tiled=True)

    def turned(a):
        return a.reshape(2, 2, 2, *a.shape[2:]).transpose(0, 2, 1, 3, 4).reshape(a.shape)

    down_total, up_total = scattered(flat(turned(down_pay))), scattered(flat(up_pay))
    latents_sum = scattered(flat(turned(lat_pay)))
    moment = lax.psum(flat(pack), ("dp", "pix"))
    small, moment = moment[WIDE : WIDE + 8], moment[:WIDE].astype(bf16)
    units = lax.psum(dq.transpose(1, 0, 2, 3).reshape(own, DQ).astype(f32), "dp")
    units = lax.all_gather(units, "pix", axis=0, tiled=True)

    unit, scale = norm(latents.astype(f32))
    lat_in = (unit * vecs[2] + vecs[3]).astype(bf16)
    queries = ((nn(lat_in, wq) + vecs[0]) * factor).astype(bf16)
    lean = units[:, FEAT : FEAT + 1]
    units = units * (jnp.arange(DQ) < FEAT)
    qk = nt(queries, wk)
    ext = jnp.zeros((8, DQ), f32)
    ext = ext.at[0].set(small[5, :DQ] + jnp.sum(qk * units, axis=0))
    ext = ext.at[1].set(small[6, :DQ] + jnp.sum(qk * lean, axis=0))
    dx = (units * feats[0] + lean * feats[1]).astype(bf16)
    key_total = restore(tn(dx, queries))
    gq = nn(dx, wk) * factor
    gq_low = gq.astype(bf16)
    grad_lat = nt(gq_low, wq)
    own_cols = lambda a: lax.dynamic_slice_in_dim(a, group * cols, cols, axis=1)
    own_rows = lambda a: lax.dynamic_slice_in_dim(a, place * chunk, chunk, axis=1)
    query_total = tn(own_rows(lat_in), own_cols(gq_low))
    back = norm_back(grad_lat * vecs[2], unit, scale)
    latents_total = latents_sum + own_cols(lax.dynamic_slice_in_dim(back, place * own, own, axis=0))
    value_total = restore(nt(moment, wo))
    out_total = tn(own_rows(wv), own_cols(moment))
    vec = jnp.concatenate(
        [
            small,
            nt(small.astype(bf16), wo)[2:3],
            jnp.sum(gq, axis=0, keepdims=True),
            jnp.sum(grad_lat * unit, axis=0, keepdims=True),
            jnp.sum(grad_lat, axis=0, keepdims=True),
        ],
        axis=0,
    )
    return down_total, up_total, out_total, query_total, latents_total, key_total, value_total, vec, ext

def shards(
    latents,
    pixel_rgb,
    coords,
    segment_ids,
    image_sizes,
    input_gain,
    input_bias,
    query_weight,
    query_bias,
    key_weight,
    value_weight,
    value_bias,
    out_weight,
    out_bias,
    latent_gain,
    latent_bias,
    mlp_gain,
    mlp_bias,
    up_weight,
    up_bias,
    down_weight,
    down_bias,
    cotangent,
):
    images = image_sizes.shape[1]
    width = latents.shape[1]
    parts = lax.axis_size("pix")
    slots = pixel_rgb.shape[1] * parts
    tiles = pixel_rgb.shape[1] // TILE
    vectors = (
        query_bias, out_bias, latent_gain, latent_bias, mlp_gain, mlp_bias, up_bias, down_bias,
        input_gain, input_bias, value_bias,
    )
    fused = lax.axis_size("dp") == 8
    rows, rgb_out, *rest = layer(
        images, slots, parts, fused, image_sizes, pixel_rgb, latents, query_weight, out_weight, up_weight, down_weight,
        key_weight, value_weight, cotangent, vectors,
    )
    if fused:
        down, up, out, query, latents_sum, key, value, vec, ext = rest
        (
            latents_out, down, up, out, query, latents_sum, key, value, rgb_grad,
            db, ub, ob, mg, mb, vb, qb, lg, lb, gain, bias,
        ) = finish(rgb_out, vec, ext, rows, down, up, out, query, latents_sum, key, value)
    else:
        down, up, out, query, latents_sum, key, value, vec, ext = sums_plain(
            parts, *rest[:5], latents, query_weight, out_weight, rest[5], rest[6], jnp.stack(vectors[:8]), rest[7]
        )
        latents_out = rows
        rgb_grad = rgb_out.reshape(4, tiles, TILE)[:3].reshape(3, tiles * TILE)
        db, ub, ob, mg, mb = (vec[i] for i in range(5))
        vb, qb, lg, lb = (vec[i] for i in range(8, 12))
        gain, bias = restore(ext[0]), restore(ext[1])
    return (
        latents_out, rgb_grad, latents_sum, query, qb, key, value, vb, out, ob, lg, lb, mg, mb, up, ub, down, db,
        gain, bias,
    )


def solution(mesh):
    whole = P()
    placed = (
        whole,
        P(None, ("dp", "pix")),
        P(None, ("dp", "pix")),
        P(("dp", "pix")),
        P(None, "dp"),
    ) + (whole,) * 17 + (P(("dp", "pix"), None, None),)
    square = P("pix", "dp")
    return jax.shard_map(
        shards,
        mesh=mesh,
        in_specs=placed,
        out_specs=(
            P(("dp", "pix"), None, None),
            P(None, ("dp", "pix")),
            square,
            square,
            whole,
            whole,
            whole,
            whole,
            square,
            whole,
            whole,
            whole,
            whole,
            whole,
            square,
            whole,
            square,
            whole,
            whole,
            whole,
        ),
        check_vma=False,
    )
```

```python
from functools import partial
import math
from types import SimpleNamespace

import jax
import jax.numpy as jnp
from jax import lax
from jax.experimental import pallas as pl
from jax.experimental.pallas import tpu as pltpu
from jax.sharding import PartitionSpec as P

BANDS = 64
MAXRES = 224
BIG_SIDE = 112
SMALL_SIDE = 32
EPSILON = 1e-05
FEAT = 4 * BANDS + 5
WIDE = FEAT + 11
DQ = 384
PACK = 320
TILE = 512
LANES = 128
MESH = pl.DeviceIdType.MESH
SENDS = 55
VMEM_LIMIT = 62 * 2**20

bf16 = jnp.bfloat16
f32 = jnp.float32


def dot(a, b, dims):
    return lax.dot_general(a, b, (dims, ((), ())), preferred_element_type=f32)


def nn(a, b):
    return dot(a, b, ((1,), (0,)))


def nt(a, b):
    return dot(a, b, ((1,), (1,)))


def tn(a, b):
    return dot(a, b, ((0,), (0,)))


def order_of(rows, cols, flip=False):
    b = 2 * BANDS
    f = lax.broadcasted_iota(jnp.int32, (rows, cols), 1 if flip else 0)
    g = lax.broadcasted_iota(jnp.int32, (rows, cols), 0 if flip else 1)
    to = jnp.where(f < 4, f + 2 * b, jnp.where(f < 4 + b, f - 4, jnp.where(f == 4 + b, 2 * b + 4, f - 5)))
    return ((to == g) & (f < FEAT)).astype(bf16)


def moved(rows, order, product):
    total = None
    for _ in range(3):
        part = rows.astype(bf16)
        rows = rows - part.astype(f32)
        piece = product(part, order)
        total = piece if total is None else total + piece
    return total


def centred(rows, axis):
    live = lax.broadcasted_iota(jnp.int32, rows.shape, axis) < FEAT
    rows = jnp.where(live, rows, 0.0)
    return jnp.where(live, rows - jnp.sum(rows, axis=axis, keepdims=True) * (1.0 / FEAT), 0.0)


def norm(rows):
    centre = rows - jnp.mean(rows, axis=-1, keepdims=True)
    scale = lax.rsqrt(jnp.mean(centre * centre, axis=-1, keepdims=True) + EPSILON)
    return centre * scale, scale


def norm_back(grad, unit, scale):
    return (
        grad
        - jnp.mean(grad, axis=-1, keepdims=True)
        - unit * jnp.mean(grad * unit, axis=-1, keepdims=True)
    ) * scale


def tanh(a):
    return 1.0 - 2.0 / (1.0 + jnp.exp(jnp.minimum(2.0 * a, 80.0)))


def sin_cos_pi(p):
    n = jnp.floor(p + 0.5)
    z = (p - n) * math.pi
    q = z * z
    s = z * (1.0 + q * (-1.0 / 6 + q * (1.0 / 120 + q * (-1.0 / 5040 + q * (1.0 / 362880 - q * (1.0 / 39916800))))))
    c = 1.0 + q * (
        -0.5 + q * (1.0 / 24 + q * (-1.0 / 720 + q * (1.0 / 40320 + q * (-1.0 / 3628800 + q * (1.0 / 479001600)))))
    )
    sign = 1.0 - 2.0 * (n - 2.0 * jnp.floor(n * 0.5))
    return s * sign, c * sign


def tiles_of(images, slots):
    spare = (images - 1) * SMALL_SIDE * SMALL_SIDE
    head = -(-spare // TILE)
    tail = BIG_SIDE * BIG_SIDE // TILE
    last = min(-(-(BIG_SIDE * BIG_SIDE + spare) // TILE), slots // TILE)
    return head, max(head, tail), last


def loop(lo, hi, body, unroll):
    steps = (hi - lo) // unroll
    if steps > 0:
        lax.fori_loop(0, steps, lambda i, c: (body([lo + i * unroll + k for k in range(unroll)]), c)[1], 0)
    if lo + steps * unroll < hi:
        body(list(range(lo + steps * unroll, hi)))


def wait(copies):
    for copy in copies:
        copy.wait()


def summed(first, others):
    total = first.astype(f32)
    for i in range(others.shape[0]):
        total = total + others[i].astype(f32)
    return total


MLP_UNROLL = 2
HEAD_UNROLL = 3
BIG_UNROLL = 3


def layer_kernel(images, slots, parts, fused, names, *refs):
    r = SimpleNamespace(**dict(zip(names, refs)))
    group, place = lax.axis_index("dp"), lax.axis_index("pix")
    count, width = r.latents_h.shape
    own, chunk = count // parts, width // parts
    rows_all = images * own
    head, tail, last = tiles_of(images, slots)
    per = r.rgb_in.shape[0] // 4
    factor = 1.0 / math.sqrt(width)
    core, quad = lax.rem(group, 2), lax.rem(group // 2, 4)
    base = group // 8 * 4
    x, y = lax.rem(quad, 2), quad // 2
    mate = ((base + quad) * 2 + 1 - core, place)

    def away(k):
        other = (1 - x if k % 2 else x) + 2 * (1 - y if k // 2 else y)
        return other, ((base + other) * 2 + core, place)

    zs = [(s, lax.rem(place + s, parts), lax.rem(place + parts - s, parts)) for s in range(1, parts)]
    used = [0]

    def send(src, dst, target):
        i = used[0]
        used[0] += 1
        copy = pltpu.make_async_remote_copy(
            src_ref=src, dst_ref=dst, send_sem=r.sems.at[0, i], recv_sem=r.sems.at[1, i],
            device_id=target, device_id_type=MESH,
        )
        copy.start()
        return copy

    def send_z(pick, put):
        return [send(pick(to), put(s), (group, to)) for s, to, _ in zs]

    def send_quad(pick, put):
        return [send(pick(away(k)[0]), put(k), away(k)[1]) for k in (1, 2, 3)]

    barrier = pltpu.get_barrier_semaphore()
    friends = [(group, to) for _, to, _ in zs]
    if fused:
        friends += [mate] + [away(k)[1] for k in (1, 2, 3)]
    for device in friends:
        pl.semaphore_signal(barrier, inc=1, device_id=device, device_id_type=MESH)
    loads = [
        pltpu.make_async_copy(a, b, r.load_sems.at[i])
        for i, (a, b) in enumerate(
            (
                (r.wq_h, r.wq), (r.wo_h, r.wo), (r.cot_h, r.cot_f), (r.up_h, r.up), (r.down_h, r.down),
                (r.latents_h, r.latents), (r.wv_h, r.wv_in),
            )
        )
    ]
    for i in (5, 0, 6, 1, 2, 3, 4):
        loads[i].start()

    shades = r.pixel_rgb[...].astype(f32)
    pieces = [shades[c : c + 1, j * TILE : (j + 1) * TILE] for c in range(3) for j in range(per)]
    r.rgb_in[...] = jnp.concatenate(pieces + [jnp.zeros((per, TILE), f32)], axis=0).astype(bf16)
    r.vecs[...] = jnp.zeros_like(r.vecs)
    for i in range(11):
        vec = getattr(r, f"vec{i}")
        r.vecs[i : i + 1, : vec.shape[0]] = vec[...].reshape(1, vec.shape[0])

    to_waves = order_of(WIDE, FEAT, flip=True)
    r.wk[:WIDE] = nn(to_waves, r.wk_in[...]).astype(bf16)
    r.wk[WIDE:] = jnp.zeros_like(r.wk[WIDE:])
    feats = moved(r.vecs[8:16, :DQ], order_of(DQ, DQ), nn)
    r.feats[...] = feats
    gain, bias = feats[0:1, :WIDE], feats[1:2, :WIDE]

    pl.semaphore_wait(barrier, len(friends))
    rgb_copies = send_z(lambda to: r.rgb_in, lambda s: r.rgb_recv.at[s - 1])

    loads[5].wait()
    loads[0].wait()
    rows = pl.ds(pl.multiple_of(place * own, own), own)
    lat_rows = r.latents[rows, :].astype(f32)
    own_unit, _ = norm(lat_rows)
    own_in = (own_unit * r.vecs[2:3, :] + r.vecs[3:4, :]).astype(bf16)
    own_queries = ((nn(own_in, r.wq[...]) + r.vecs[0:1, :]) * factor).astype(bf16)
    qk = nt(own_queries, r.wk[:WIDE])
    qc = centred(qk * gain, 1).astype(bf16)
    r.qc[...] = qc
    r.qb[...] = jnp.sum(qk * bias, axis=1, keepdims=True)
    pick = (
        lax.broadcasted_iota(jnp.int32, (16, WIDE), 1)
        == lax.broadcasted_iota(jnp.int32, (16, WIDE), 0) + 4 * BANDS
    ).astype(bf16)
    r.ext[images * 16 :, :] = nt(pick, qc).astype(bf16)

    loads[6].wait()
    vb = r.vecs[10:11, :]
    vb_high = vb.astype(bf16).astype(f32)
    row = lax.broadcasted_iota(jnp.int32, (WIDE, width), 0)
    wv = nn(to_waves, r.wv_in[...])
    r.wv[...] = jnp.where(row == FEAT, vb_high, jnp.where(row == FEAT + 1, vb - vb_high, wv)).astype(bf16)

    wait(rgb_copies)
    for c in range(3):
        at = slice(c * per, (c + 1) * per)
        r.rgbf[c, pl.ds(pl.multiple_of(place * per, per), per), :] = r.rgb_in[at, :].astype(f32)
        for s, _, source in zs:
            r.rgbf[c, pl.ds(pl.multiple_of(source * per, per), per), :] = r.rgb_recv[s - 1, at, :].astype(f32)

    ends, high, wide = [], [], []
    end = jnp.int32(0)
    for i in range(images):
        end = end + r.sizes[0, i] * r.sizes[1, i]
        ends.append(end.astype(f32))
        high.append(jnp.maximum(r.sizes[0, i] - 1, 1).astype(f32))
        wide.append(r.sizes[1, i].astype(f32))
    is_big = [(r.sizes[0, n] > SMALL_SIDE).astype(f32) for n in range(images)]

    def features(j):
        shape = (8, TILE)
        lane = lax.broadcasted_iota(jnp.int32, shape, 1)
        sub = lax.broadcasted_iota(jnp.int32, shape, 0)
        slot = (lane + j * TILE).astype(f32)
        segment = jnp.zeros(shape, f32)
        start = jnp.zeros(shape, f32)
        tall = jnp.full(shape, high[0])
        across = jnp.full(shape, wide[0])
        for i in range(images):
            past = slot >= ends[i]
            segment = jnp.where(past, segment + 1.0, segment)
            if i + 1 < images:
                start = jnp.where(past, ends[i], start)
                tall = jnp.where(past, high[i + 1], tall)
                across = jnp.where(past, wide[i + 1], across)
            else:
                start = jnp.where(past, slot, start)
        local = slot - start
        row = jnp.floor((local + 0.5) / across)
        col = local - row * across
        y = 2.0 * row / tall - 1.0
        x = 2.0 * col / jnp.maximum(across - 1.0, 1.0) - 1.0
        step = (MAXRES / 2.0 - 1.0) / (BANDS - 1)
        lowest = 1.0 + sub.astype(f32) * step
        total = None
        pieces = []
        for spot in (y, x):
            s, c = sin_cos_pi(lowest * spot)
            rs, rc = sin_cos_pi((8 * step) * spot)
            sines, cosines = [s], [c]
            for _ in range(BANDS // 8 - 1):
                s, c = s * rc + c * rs, c * rc - s * rs
                sines.append(s)
                cosines.append(c)
            for k in range(BANDS // 8):
                total = sines[k] + cosines[k] if total is None else total + (sines[k] + cosines[k])
            pieces.append(jnp.concatenate(sines, axis=0).astype(bf16))
            pieces.append(jnp.concatenate(cosines, axis=0).astype(bf16))
        total = jnp.sum(total, axis=0, keepdims=True)
        red, green, blue = (r.rgbf[c, pl.ds(j, 1), :] for c in range(3))
        y, x, segment = y[0:1], x[0:1], segment[0:1]
        total = total + (red + green + blue + y + x)
        squares = red * red + green * green + blue * blue + y * y + x * x + 2.0 * BANDS
        mean = total * (1.0 / FEAT)
        spread = squares * (1.0 / FEAT) - mean * mean + EPSILON
        scale = lax.rsqrt(spread)
        deviation = spread * scale
        rest = deviation - deviation.astype(bf16).astype(f32)
        ext = jnp.zeros(shape, f32)
        for k, v in enumerate((red, green, blue, y, x, deviation, rest)):
            ext = jnp.where(sub == k, v, ext)
        pieces.append(jnp.concatenate([ext, jnp.zeros(shape, f32)], axis=0).astype(bf16))
        tile = jnp.concatenate(pieces, axis=0)
        r.feat[j] = tile
        r.stat[j] = jnp.where(sub == 0, scale, jnp.where(sub == 1, mean, segment))
        return tile, scale, segment

    r.acc[...] = jnp.zeros_like(r.acc)
    r.acc_big[...] = jnp.zeros_like(r.acc_big)

    def side(parts_of):
        return parts_of[0] if len(parts_of) == 1 else jnp.concatenate(parts_of, axis=1)

    def forward(mixed, js):
        tiles, mixes = [], []
        for j in js:
            tile, scale, segment = features(j)
            weights = jnp.exp(nn(r.qc[...], tile) * scale + r.qb[...])
            if mixed:
                weights = jnp.where(segment < images, weights, 0.0)
            r.wst[j] = weights.astype(bf16)
            scaled = (weights * scale).astype(bf16)
            if mixed:
                none = jnp.zeros_like(scaled)
                scaled = jnp.concatenate([jnp.where(segment == n, scaled, none) for n in range(images)], axis=0)
            tiles.append(tile)
            mixes.append(scaled)
        into = r.acc if mixed else r.acc_big
        into[...] += nt(side(tiles), side(mixes))

    loop(0, head, partial(forward, True), HEAD_UNROLL)
    loop(head, tail, partial(forward, False), BIG_UNROLL)
    loop(tail, last, partial(forward, True), HEAD_UNROLL)

    lane = lax.broadcasted_iota(jnp.int32, (own, WIDE), 1)
    ones = ((lane == FEAT) | (lane == FEAT + 1)).astype(f32)
    big = r.acc_big[...]
    mix_all = (r.acc[...] + jnp.concatenate([big * is_big[n] for n in range(images)], axis=1)).T
    for n in range(images):
        at = slice(n * own, (n + 1) * own)
        mix = mix_all[at]
        totals = mix[:, FEAT : FEAT + 1] + mix[:, FEAT + 1 : FEAT + 2]
        unit = centred(mix, 1) / totals
        r.tot[at, :] = totals
        r.unit[at, :] = unit
        r.px_send[n] = (unit * gain + bias + ones).astype(bf16).T
    px_copies = send_z(lambda to: r.px_send.at[to], lambda s: r.px_recv.at[place])
    r.px_recv[place] = r.px_send[place]

    loads[1].wait()
    wvo = nn(r.wv[...], r.wo[...])
    const = wvo[FEAT : FEAT + 1] + wvo[FEAT + 1 : FEAT + 2] + r.vecs[1:2, :]
    r.wvo[...] = jnp.where(row < FEAT, wvo, 0.0).astype(bf16)
    loads[2].wait()
    loads[3].wait()
    loads[4].wait()
    k = math.sqrt(2.0 / math.pi)
    half = 2 * own
    wait(px_copies)
    out_copies = []
    for blk in range(count // half):
        at = slice(blk * half, (blk + 1) * half)
        px_t = jnp.concatenate([r.px_recv[2 * blk + i] for i in range(2)], axis=1)
        r.px_t[:, at] = px_t
        middle = r.latents[at, :].astype(f32) + nn(px_t.T, r.wvo[...]) + const
        mid_unit, mid_scale = norm(middle)
        mid_in = (mid_unit * r.vecs[4:5, :] + r.vecs[5:6, :]).astype(bf16)
        hidden = nn(mid_in, r.up[...]) + r.vecs[6:7, :]
        th = tanh(k * (hidden + 0.044715 * hidden * hidden * hidden))
        active = (0.5 * hidden * (1.0 + th)).astype(bf16)
        r.slope[at, :] = 0.5 * (1.0 + th) + 0.5 * hidden * (1.0 - th * th) * k * (
            1.0 + 3 * 0.044715 * hidden * hidden
        )
        stage = (r.key_out, r.value_out)[blk].at[pl.ds(0, half)] if fused else (r.stage0, r.stage1)[blk]
        stage[...] = middle + nn(active, r.down[...]) + r.vecs[7:8, :]
        copy = pltpu.make_async_copy(stage, r.out_rows.at[0, pl.ds(blk * half, half)], r.load_sems.at[7 + blk])
        copy.start()
        out_copies.append(copy)
        r.mid_unit[at, :] = mid_unit
        r.mid_scale[at, :] = mid_scale
        r.act_t[:, at] = active.T
        r.mid_t[:, at] = mid_in.T

    def down_grads(jj, c):
        cols = pl.ds(pl.multiple_of(jj * 256, 256), 256)
        part = nn(r.act_t[...], r.cot_f[0, :, cols].astype(bf16)).astype(bf16)
        for i in range(2):
            r.down_pay[i, lax.rem(jj, 2) * 2 + jj // 2] = part[:, i * LANES : (i + 1) * LANES]
        return c

    lax.fori_loop(0, width // 256, down_grads, 0)
    if fused:
        core_down = send(r.down_pay.at[1 - core], r.down_c, mate)

    def fold(first, value):
        for i in range(width // count):
            r.act_t[i * count + first : i * count + first + value.shape[0], :] = value[:, i * count : (i + 1) * count]

    def unfold(first, size):
        at = pl.ds(pl.multiple_of(first // count * count, count), count)
        return r.act_t[at, pl.ds(pl.multiple_of(lax.rem(first, count), LANES), size)]

    total_sums, ext_total = None, None
    for blk in range(count // half):
        at = slice(blk * half, (blk + 1) * half)
        if fused and blk == 1:
            core_down.wait()
            for b in range(4):
                r.down_c[b] = r.down_c[b] + r.down_pay[core, b]
            first_down = send(r.down_c.at[pl.ds((1 - x) * 2, 2)], r.down_1, away(1)[1])
        grad_down = r.cot_f[0, at, :].astype(bf16)
        grad_hidden = (r.slope[at, :] * nt(grad_down, r.down[...])).astype(bf16)
        fold(blk * half, grad_hidden)
        grad_mid = nt(grad_hidden, r.up[...])
        mid_unit = r.mid_unit[at, :]
        grad_middle = r.cot_f[0, at, :] + norm_back(grad_mid * r.vecs[4:5, :], mid_unit, r.mid_scale[at, :])
        branch = grad_middle.astype(bf16)
        r.branch[at, :] = branch
        for d in range(width // LANES):
            q = d // 2
            r.lat_pay[d % 2, q % 2 * 2 + q // 2, at, :] = branch[:, d * LANES : (d + 1) * LANES]
        part = [
            jnp.sum(v, axis=0, keepdims=True)
            for v in (grad_down.astype(f32), grad_hidden.astype(f32), branch.astype(f32), grad_mid * mid_unit, grad_mid)
        ]
        total_sums = part if total_sums is None else [u + v for u, v in zip(total_sums, part)]
        gx = nt(r.wvo[...], branch)
        r.px_send[2 * blk] = gx[:, :own].astype(bf16)
        r.px_send[2 * blk + 1] = gx[:, own:].astype(bf16)
        part = [jnp.sum(gx * r.px_t[:, at].astype(f32), axis=1, keepdims=True), jnp.sum(gx, axis=1, keepdims=True)]
        ext_total = part if ext_total is None else [u + v for u, v in zip(ext_total, part)]
    gx_copies = send_z(lambda to: r.px_send.at[to], lambda s: r.gx_recv.at[place])
    r.gx_recv[place] = r.px_send[place]
    lane = lax.broadcasted_iota(jnp.int32, (WIDE, LANES), 1)
    ext_rows = jnp.where(lane == 0, ext_total[0], jnp.where(lane == 1, ext_total[1], 0.0)).T
    live = lax.broadcasted_iota(jnp.int32, (1, WIDE), 1) < FEAT
    gain_part = jnp.where(live, (ext_rows[0:1] - bias * ext_rows[1:2]) / jnp.where(live, gain, 1.0), 0.0)
    small = jnp.concatenate(
        total_sums
        + [jnp.pad(v, ((0, 0), (0, width - WIDE))) for v in (gain_part, jnp.where(live, ext_rows[1:2], 0.0))]
        + [jnp.zeros((PACK - WIDE - 7, width), f32)],
        axis=0,
    ).astype(bf16)
    for d in range(width // LANES):
        r.pack[d % 2, d // 2, WIDE:, :] = small[:, d * LANES : (d + 1) * LANES]


    def moments(jj, c):
        cols = pl.ds(pl.multiple_of(jj * 256, 256), 256)
        part = nn(r.px_t[...], r.branch[:, cols]).astype(bf16)
        for i in range(2):
            r.pack[i, jj, :WIDE] = part[:, i * LANES : (i + 1) * LANES]
        return c

    def up_grads(jj, c):
        cols = pl.ds(pl.multiple_of(jj * 256, 256), 256)
        part = nn(r.mid_t[...], unfold(jj * 256, 256)).astype(bf16)
        for i in range(2):
            r.up_pay[i, jj] = part[:, i * LANES : (i + 1) * LANES]
        return c

    lax.fori_loop(0, width // 256, moments, 0)
    if fused:
        core_pack = send(r.pack.at[1 - core], r.pack_c, mate)
        core_lat = send(r.lat_pay.at[1 - core], r.lat_c, mate)
    lax.fori_loop(0, width // 256, up_grads, 0)
    if fused:
        core_up = send(r.up_pay.at[1 - core], r.up_c, mate)

    if fused:
        unit, scale = norm(r.latents[...].astype(f32))
        r.mid_unit[...] = unit
        r.mid_scale[...] = scale
        lat_low = (unit * r.vecs[2:3, :] + r.vecs[3:4, :]).astype(bf16)
        fold(0, lat_low)
        queries = ((nn(lat_low, r.wq[...]) + r.vecs[0:1, :]) * factor).astype(bf16)
        r.branch[...] = queries
        r.qk_all[...] = nt(queries, r.wk[...])
    wait(gx_copies)
    gcb = jnp.zeros((own, WIDE), f32)
    levb = jnp.zeros((own, 1), f32)
    for n in range(images):
        at = slice(n * own, (n + 1) * own)
        gc = centred(r.gx_recv[n].T.astype(f32) * gain, 1) / r.tot[at, :]
        gc_low = gc.astype(bf16)
        level = jnp.sum(gc_low.astype(f32) * r.unit[at, :], axis=1, keepdims=True)
        r.gc[at, :] = gc_low
        r.lev[at, :] = level
        r.ext[n * 16 : (n + 1) * 16, :] = nt(pick, gc_low).astype(bf16)
        gcb = gcb + gc * is_big[n]
        levb = levb + level * is_big[n]
    r.gc[rows_all :, :] = r.qc[...]
    r.gcb[:own, :] = gcb.astype(bf16)
    r.gcb[own:, :] = r.qc[...]
    r.levb[...] = levb
    r.extb[:, own:] = nt(pick, r.gcb[:own, :]).astype(bf16)
    r.extb[:, :own] = r.ext[images * 16 :, :]

    if fused:
        core_pack.wait()
        r.pack_c[...] = r.pack_c[...] + r.pack[core]
        quad_pack = send_quad(lambda q: r.pack_c.at[q], lambda k: r.pack_q.at[k - 1])
        core_lat.wait()
        for b in range(4):
            r.lat_c[b] = r.lat_c[b] + r.lat_pay[core, b]
        first_lat = send(r.lat_c.at[pl.ds((1 - x) * 2, 2)], r.lat_1, away(1)[1])
        core_up.wait()
        for b in range(4):
            r.up_c[b] = r.up_c[b] + r.up_pay[core, b]
        first_up = send(r.up_c.at[pl.ds((1 - y) * 2, 2)], r.up_1, away(2)[1])

    r.dq_sum[...] = jnp.zeros_like(r.dq_sum)
    r.rgbp[...] = jnp.zeros_like(r.rgbp)

    def backward(mixed, js):
        tiles, grads = [], []
        for j in js:
            tile = r.feat[j]
            scale = r.stat[j, 0:1, :]
            mean = r.stat[j, 1:2, :]
            low_weights = r.wst[j]
            weights = low_weights.astype(f32)
            pulls = nn(r.gc[...] if mixed else r.gcb[...], tile)
            raw = pulls[-own:] * scale
            if mixed:
                segment = r.stat[j, 2:3, :]
                pull = jnp.zeros_like(weights)
                level = jnp.zeros_like(weights)
                for n in range(images):
                    at = slice(n * own, (n + 1) * own)
                    here = segment == n
                    pull = jnp.where(here, pulls[at], pull)
                    level = jnp.where(here, r.lev[at, :], level)
            else:
                pull = pulls[:own]
                level = r.levb[...]
            pull = pull * scale
            grad = weights * (pull - level)
            lean = jnp.sum(grad * raw + weights * pull, axis=0, keepdims=True) * (1.0 / FEAT)
            if mixed:
                colours = nn(r.ext[: images * 16, :], low_weights)
                back = nn(r.ext[images * 16 :, :], grad.astype(bf16))
                picked = jnp.zeros_like(back)
                for n in range(images):
                    picked = jnp.where(segment == n, colours[n * 16 : (n + 1) * 16], picked)
                back = back + picked
            else:
                back = nn(r.extb[...], jnp.concatenate([grad.astype(bf16), low_weights], axis=0))
            ext = tile[4 * BANDS :, :].astype(f32)
            part = (back - (ext - mean) * scale * lean) * scale
            for c in range(3):
                r.rgbp[c, pl.ds(j, 1), :] = part[c : c + 1]
            tiles.append(tile)
            grads.append((grad * scale).astype(bf16))
        r.dq_sum[...] += nt(side(tiles), side(grads))

    step = 2 * BIG_UNROLL
    loop(0, head, partial(backward, True), HEAD_UNROLL)
    loop(head, head + BIG_UNROLL, partial(backward, False), BIG_UNROLL)
    if fused:
        pack_rows = PACK // parts
        mine = pl.ds(pl.multiple_of(place * pack_rows, 16), pack_rows)
        wait(quad_pack)
        r.pack_m[...] = summed(r.pack_c[quad], r.pack_q).astype(bf16)
        z_pack = send_z(
            lambda to: r.pack_m.at[pl.ds(pl.multiple_of(to * pack_rows, 16), pack_rows)], lambda s: r.pack_z.at[s - 1]
        )
    at = head + BIG_UNROLL
    loop(at, at + step, partial(backward, False), BIG_UNROLL)
    if fused:
        first_down.wait()
        for b in range(2):
            r.down_1[b] = r.down_1[b] + r.down_c[x * 2 + b]
        second_down = send(r.down_1.at[1 - y], r.down_2, away(2)[1])
        wait(z_pack)
        r.pack_own[...] = summed(r.pack_m[mine, :], r.pack_z).astype(bf16)
        r.pack_all[core, quad, mine, :] = r.pack_own[...]
        all_pack = send_z(lambda to: r.pack_own, lambda s: r.pack_all.at[core, quad, mine])
    loop(at + step, at + 2 * step, partial(backward, False), BIG_UNROLL)
    if fused:
        wait(all_pack)
        all_pack = send_quad(lambda q: r.pack_all.at[core, quad], lambda k: r.pack_all.at[core, quad])
    loop(at + 2 * step, tail, partial(backward, False), BIG_UNROLL)
    loop(tail, last, partial(backward, True), HEAD_UNROLL)

    dq = r.dq_sum[...].T
    lanes = lax.broadcasted_iota(jnp.int32, dq.shape, 1)
    gs_sum = dq[:, FEAT : FEAT + 1] + dq[:, FEAT + 1 : FEAT + 2]
    dq = jnp.where(lanes == FEAT, gs_sum, centred(dq, 1)).astype(bf16)
    r.dq_pay[...] = jnp.zeros_like(r.dq_pay)
    each = own // 8
    for d in range(8):
        r.dq_pay[d % 2, d // 2, :, :WIDE] = dq[d * each : (d + 1) * each]
    if fused:
        core_dq = send(r.dq_pay.at[1 - core], r.dq_c, mate)

    for t in range(parts):
        r.rgb_send[t] = jnp.concatenate(
            [r.rgbp[c, t * per : (t + 1) * per, :] for c in range(3)] + [jnp.zeros((per, TILE), f32)], axis=0
        ).astype(bf16)
    back_copies = send_z(lambda to: r.rgb_send.at[to], lambda s: r.rgb_back.at[s - 1])

    if fused:
        core_dq.wait()
        r.dq_c[...] = r.dq_c[...] + r.dq_pay[core]
        quad_dq = send_quad(lambda q: r.dq_c.at[q], lambda k: r.dq_q.at[k - 1])
        first_lat.wait()
        for b in range(2):
            r.lat_1[b] = r.lat_1[b] + r.lat_c[x * 2 + b]
        second_lat = send(r.lat_1.at[1 - y], r.lat_2, away(2)[1])
        first_up.wait()
        for b in range(2):
            r.up_1[b] = r.up_1[b] + r.up_c[y * 2 + b]
        second_up = send(r.up_1.at[1 - x], r.up_2, away(1)[1])
        wait(all_pack)
        all_pack = send(r.pack_all.at[core], r.pack_all.at[core], mate)
        wait(quad_dq)
        r.dq_own[...] = summed(r.dq_c[quad], r.dq_q).astype(bf16)
        r.dq_all[core, quad, place] = r.dq_own[...]
        z_dq = send_z(lambda to: r.dq_own, lambda s: r.dq_all.at[core, quad, place])
        second_down.wait()
        r.down_2[...] = (r.down_1[y].astype(f32) + r.down_2[...].astype(f32)).astype(bf16)
        z_down = send_z(
            lambda to: r.down_2.at[pl.ds(pl.multiple_of(to * chunk, 16), chunk)], lambda s: r.down_z.at[s - 1]
        )
        all_pack.wait()

        own_cols = pl.ds(pl.multiple_of(lax.rem(group, 8) * LANES, LANES), LANES)
        lat_cols = pl.ds(pl.multiple_of(place * chunk, LANES), chunk)
        for d in range(8):
            r.moment[:, d * LANES : (d + 1) * LANES] = r.pack_all[d % 2, d // 2]
        order = order_of(264, DQ)
        wait(out_copies)
        r.value_out[...] = nt(nn(order[:, :WIDE], r.moment[:WIDE, :]).astype(bf16), r.wo[...])[:FEAT]
        r.out_out[...] = tn(r.wv[:, lat_cols], r.moment[:WIDE, own_cols])
        small = r.moment[WIDE : WIDE + 16, :]
        value_bias = nt(small, r.wo[...])[2:3]
        small = small.astype(f32)
        wait(z_dq)
        all_dq = send_quad(lambda q: r.dq_all.at[core, quad], lambda k: r.dq_all.at[core, quad])

        second_up.wait()
        r.up_2[...] = (r.up_1[x].astype(f32) + r.up_2[...].astype(f32)).astype(bf16)
        z_up = send_z(
            lambda to: r.up_2.at[pl.ds(pl.multiple_of(to * chunk, 16), chunk)], lambda s: r.up_z.at[s - 1]
        )
        second_lat.wait()
        r.lat_2[...] = (r.lat_1[y].astype(f32) + r.lat_2[...].astype(f32)).astype(bf16)
        z_lat = send_z(
            lambda to: r.lat_2.at[pl.ds(pl.multiple_of(to * own, 16), own)], lambda s: r.lat_z.at[s - 1]
        )
    wait(back_copies)
    r.rgb_out[...] = summed(r.rgb_send[place], r.rgb_back).astype(bf16)

    if fused:
        block = pl.ds(pl.multiple_of(place * chunk, 16), chunk)
        wait(z_down)
        r.down_out[...] = summed(r.down_2[block, :], r.down_z)
        wait(all_dq)
        all_dq = send(r.dq_all.at[core], r.dq_all.at[core], mate)
        all_dq.wait()

        for z in range(parts):
            for d in range(8):
                r.dq[(z * 8 + d) * each : (z * 8 + d + 1) * each, :] = r.dq_all[d % 2, d // 2, z]
        units = r.dq[...].astype(f32)
        lean = units[:, FEAT : FEAT + 1]
        units = jnp.where(lax.broadcasted_iota(jnp.int32, units.shape, 1) < FEAT, units, 0.0)
        gain_sum = jnp.sum(r.qk_all[...] * units, axis=0, keepdims=True)
        bias_sum = jnp.sum(r.qk_all[...] * lean, axis=0, keepdims=True)
        dx = (units * r.feats[0:1, :] + lean * r.feats[1:2, :]).astype(bf16)
        r.key_out[...] = nn(nt(order, dx).astype(bf16), r.branch[...])[:FEAT]
        gq = nn(dx, r.wk[...]) * factor
        gq_low = gq.astype(bf16)
        query_bias = jnp.sum(gq, axis=0, keepdims=True)
        grad_lat = nt(gq_low, r.wq[...])
        latent_gain = jnp.sum(grad_lat * r.mid_unit[...], axis=0, keepdims=True)
        latent_bias = jnp.sum(grad_lat, axis=0, keepdims=True)
        r.branch[...] = gq_low
        r.query_out[...] = tn(unfold(place * chunk, chunk), r.branch[:, own_cols])
        r.mid_unit[...] = norm_back(grad_lat * r.vecs[2:3, :], r.mid_unit[...], r.mid_scale[...])

        r.vec_out[...] = jnp.concatenate(
            [small[:8], value_bias, query_bias, latent_gain, latent_bias, jnp.zeros((4, width), f32)], axis=0
        )
        ends_of = jnp.concatenate(
            [small[5:6, :DQ] + gain_sum, small[6:7, :DQ] + bias_sum, jnp.zeros((6, DQ), f32)], axis=0
        )
        r.ext_out[...] = moved(ends_of, order_of(DQ, DQ), nt)

        wait(z_up)
        r.up_out[...] = summed(r.up_2[block, :], r.up_z)
        wait(z_lat)
        r.latents_out[...] = summed(r.lat_2[rows, :], r.lat_z) + r.mid_unit[rows, own_cols]
    else:
        wait(out_copies)


def layer(images, slots, parts, fused, sizes, pixel_rgb, latents, wq, wo, up, down, wk, wv, cot, vectors):
    count, width = latents.shape
    own, chunk = count // parts, width // parts
    rows = images * own
    hidden = up.shape[1]
    tiles = slots // TILE
    colours = (4 * tiles // parts, TILE)
    last = tiles_of(images, slots)[2]
    each = own // 8
    any_, vm = pl.BlockSpec(memory_space=pl.ANY), pl.BlockSpec(memory_space=pltpu.VMEM)
    sds = jax.ShapeDtypeStruct
    V = pltpu.VMEM
    ins = [
        ("sizes", sizes, pl.BlockSpec(memory_space=pltpu.SMEM)), ("pixel_rgb", pixel_rgb, vm), ("latents_h", latents, any_),
        ("wq_h", wq, any_), ("wo_h", wo, any_), ("up_h", up, any_), ("down_h", down, any_),
        ("wk_in", wk, vm), ("wv_h", wv, any_), ("cot_h", cot, any_),
    ] + [(f"vec{i}", v, vm) for i, v in enumerate(vectors)]
    pays = [
        ("down_pay", (2, 4, hidden, LANES), bf16), ("up_pay", (2, 4, width, LANES), bf16), ("lat_pay", (2, 4, count, LANES), bf16),
        ("pack", (2, 4, PACK, LANES), bf16), ("dq_pay", (2, 4, each, DQ), bf16),
        ("wk", (DQ, width), bf16), ("wv", (WIDE, width), bf16), ("feats", (8, DQ), f32),
    ]
    outs = [("out_rows", cot.shape, f32), ("rgb_out", colours, bf16)]
    scratch = [
        ("feat", (last, WIDE, TILE), bf16), ("stat", (last, 8, TILE), f32), ("wst", (last, own, TILE), bf16),
        ("rgb_in", colours, bf16), ("vecs", (16, width), f32), ("rgb_recv", (parts - 1,) + colours, bf16), ("rgbf", (3, tiles, TILE), f32), ("rgbp", (3, tiles, TILE), f32),
        ("rgb_send", (parts,) + colours, bf16), ("rgb_back", (parts - 1,) + colours, bf16),
        ("latents", latents.shape, bf16), ("wv_in", wv.shape, bf16), ("wq", wq.shape, bf16), ("wo", wo.shape, bf16), ("up", up.shape, bf16), ("down", down.shape, bf16),
        ("cot_f", cot.shape, f32), ("slope", (count, hidden), f32),
        ("px_send", (images, WIDE, own), bf16), ("px_recv", (parts, WIDE, own), bf16),
        ("gx_recv", (images, WIDE, own), bf16),
        ("qc", (own, WIDE), bf16), ("qb", (own, 1), f32), ("ext", (images * 16 + 16, own), bf16),
        ("extb", (16, 2 * own), bf16),
        ("acc", (WIDE, rows), f32), ("acc_big", (WIDE, own), f32), ("unit", (rows, WIDE), f32),
        ("wvo", (WIDE, width), bf16), ("tot", (rows, 1), f32),
        ("mid_unit", (count, width), f32), ("mid_scale", (count, 1), f32),
        ("act_t", (hidden, count), bf16), ("mid_t", (width, count), bf16), ("px_t", (WIDE, count), bf16),
        ("branch", (count, width), bf16),
        ("gc", (rows + own, WIDE), bf16), ("gcb", (2 * own, WIDE), bf16), ("lev", (rows, 1), f32), ("levb", (own, 1), f32),
        ("dq_sum", (WIDE, own), f32),
    ]
    if fused:
        outs += [
            ("down_out", (chunk, LANES), f32), ("up_out", (chunk, LANES), f32), ("out_out", (chunk, LANES), f32),
            ("query_out", (chunk, LANES), f32), ("latents_out", (own, LANES), f32), ("key_out", (FEAT, width), f32),
            ("value_out", (FEAT, width), f32), ("vec_out", (16, width), f32), ("ext_out", (8, DQ), f32),
        ]
        scratch += pays + [
            ("down_c", (4, hidden, LANES), bf16), ("down_1", (2, hidden, LANES), bf16), ("down_2", (hidden, LANES), bf16),
            ("down_z", (parts - 1, chunk, LANES), bf16),
            ("up_c", (4, width, LANES), bf16), ("up_1", (2, width, LANES), bf16), ("up_2", (width, LANES), bf16),
            ("lat_c", (4, count, LANES), bf16), ("lat_1", (2, count, LANES), bf16), ("lat_2", (count, LANES), bf16),
            ("up_z", (parts - 1, chunk, LANES), bf16),
            ("lat_z", (parts - 1, own, LANES), bf16),
            ("pack_c", (4, PACK, LANES), bf16), ("pack_q", (3, PACK, LANES), bf16), ("pack_m", (PACK, LANES), bf16),
            ("pack_z", (parts - 1, PACK // parts, LANES), bf16), ("pack_own", (PACK // parts, LANES), bf16),
            ("pack_all", (2, 4, PACK, LANES), bf16),
            ("dq_c", (4, each, DQ), bf16), ("dq_q", (3, each, DQ), bf16), ("dq_own", (each, DQ), bf16),
            ("dq_all", (2, 4, parts, each, DQ), bf16), ("dq", (count, DQ), bf16), ("moment", (PACK, width), bf16),
            ("qk_all", (count, DQ), f32),
        ]
    else:
        outs += pays
        scratch += [("stage0", (2 * own, width), f32), ("stage1", (2 * own, width), f32)]
    names = [n for n, _, _ in ins + outs + scratch] + ["load_sems", "sems"]
    return pl.pallas_call(
        partial(layer_kernel, images, slots, parts, fused, names),
        out_shape=tuple(sds(s, d) for _, s, d in outs),
        in_specs=[spec for _, _, spec in ins],
        out_specs=(any_,) + (vm,) * (len(outs) - 1),
        scratch_shapes=[V(s, d) for _, s, d in scratch]
        + [pltpu.SemaphoreType.DMA((9,)), pltpu.SemaphoreType.DMA((2, SENDS))],
        compiler_params=pltpu.CompilerParams(collective_id=0, has_side_effects=True, vmem_limit_bytes=VMEM_LIMIT),
        name="layer",
    )(*[a for _, a, _ in ins])


def finish_kernel(moves, rgb, vec, ext, *refs):
    whole, whole_out = refs[:moves], refs[moves : 2 * moves]
    rgb_grad, *vec_out = refs[2 * moves :]
    for a, b in zip(whole, whole_out):
        b[...] = a[...]
    colours = rgb[...].astype(f32)
    per = rgb.shape[0] // 4
    rgb_grad[...] = jnp.concatenate(
        [
            jnp.concatenate([colours[c * per + j : c * per + j + 1] for j in range(per)], axis=1)
            for c in range(3)
        ],
        axis=0,
    ).astype(bf16)
    for i, out in enumerate(vec_out[:9]):
        out[...] = vec[i if i < 5 else i + 3, :]
    for i, out in enumerate(vec_out[9:]):
        out[...] = ext[i, :FEAT]


def finish(rgb, vec, ext, *whole):
    width = vec.shape[1]
    vm = pl.BlockSpec(memory_space=pltpu.VMEM)
    sds = jax.ShapeDtypeStruct
    n = len(whole)
    outs = (
        tuple(sds(a.shape, a.dtype) for a in whole)
        + (sds((3, rgb.shape[0] // 4 * TILE), bf16),)
        + (sds((width,), f32),) * 9
        + (sds((FEAT,), f32),) * 2
    )
    return pl.pallas_call(
        partial(finish_kernel, n),
        out_shape=outs,
        in_specs=[vm] * (3 + n),
        out_specs=(vm,) * len(outs),
        compiler_params=pltpu.CompilerParams(vmem_limit_bytes=VMEM_LIMIT),
        name="finish",
    )(rgb, vec, ext, *whole)


def restore(rows):
    b = 2 * BANDS
    return jnp.concatenate(
        [rows[2 * b : 2 * b + 4], rows[:b], rows[2 * b + 4 : 2 * b + 5], rows[b : 2 * b]], axis=0
    )


def sums_plain(parts, down_pay, up_pay, lat_pay, pack, dq, latents, wq, wo, wk, wv, vecs, feats):
    count, width = latents.shape
    own, chunk = count // parts, width // parts
    place, group, groups = lax.axis_index("pix"), lax.axis_index("dp"), lax.axis_size("dp")
    cols = width // groups
    factor = 1.0 / math.sqrt(width)

    def flat(a):
        return a.transpose(2, 1, 0, 3).reshape(a.shape[2], width).astype(f32)

    def scattered(a):
        a = lax.psum_scatter(a, "dp", scatter_dimension=1, tiled=True)
        return lax.psum_scatter(a, "pix", scatter_dimension=0, tiled=True)

    def turned(a):
        return a.reshape(2, 2, 2, *a.shape[2:]).transpose(0, 2, 1, 3, 4).reshape(a.shape)

    down_total, up_total = scattered(flat(turned(down_pay))), scattered(flat(up_pay))
    latents_sum = scattered(flat(turned(lat_pay)))
    moment = lax.psum(flat(pack), ("dp", "pix"))
    small, moment = moment[WIDE : WIDE + 8], moment[:WIDE].astype(bf16)
    units = lax.psum(dq.transpose(1, 0, 2, 3).reshape(own, DQ).astype(f32), "dp")
    units = lax.all_gather(units, "pix", axis=0, tiled=True)

    unit, scale = norm(latents.astype(f32))
    lat_in = (unit * vecs[2] + vecs[3]).astype(bf16)
    queries = ((nn(lat_in, wq) + vecs[0]) * factor).astype(bf16)
    lean = units[:, FEAT : FEAT + 1]
    units = units * (jnp.arange(DQ) < FEAT)
    qk = nt(queries, wk)
    ext = jnp.zeros((8, DQ), f32)
    ext = ext.at[0].set(small[5, :DQ] + jnp.sum(qk * units, axis=0))
    ext = ext.at[1].set(small[6, :DQ] + jnp.sum(qk * lean, axis=0))
    dx = (units * feats[0] + lean * feats[1]).astype(bf16)
    key_total = restore(tn(dx, queries))
    gq = nn(dx, wk) * factor
    gq_low = gq.astype(bf16)
    grad_lat = nt(gq_low, wq)
    own_cols = lambda a: lax.dynamic_slice_in_dim(a, group * cols, cols, axis=1)
    own_rows = lambda a: lax.dynamic_slice_in_dim(a, place * chunk, chunk, axis=1)
    query_total = tn(own_rows(lat_in), own_cols(gq_low))
    back = norm_back(grad_lat * vecs[2], unit, scale)
    latents_total = latents_sum + own_cols(lax.dynamic_slice_in_dim(back, place * own, own, axis=0))
    value_total = restore(nt(moment, wo))
    out_total = tn(own_rows(wv), own_cols(moment))
    vec = jnp.concatenate(
        [
            small,
            nt(small.astype(bf16), wo)[2:3],
            jnp.sum(gq, axis=0, keepdims=True),
            jnp.sum(grad_lat * unit, axis=0, keepdims=True),
            jnp.sum(grad_lat, axis=0, keepdims=True),
        ],
        axis=0,
    )
    return down_total, up_total, out_total, query_total, latents_total, key_total, value_total, vec, ext

def shards(
    latents,
    pixel_rgb,
    coords,
    segment_ids,
    image_sizes,
    input_gain,
    input_bias,
    query_weight,
    query_bias,
    key_weight,
    value_weight,
    value_bias,
    out_weight,
    out_bias,
    latent_gain,
    latent_bias,
    mlp_gain,
    mlp_bias,
    up_weight,
    up_bias,
    down_weight,
    down_bias,
    cotangent,
):
    images = image_sizes.shape[1]
    width = latents.shape[1]
    parts = lax.axis_size("pix")
    slots = pixel_rgb.shape[1] * parts
    tiles = pixel_rgb.shape[1] // TILE
    vectors = (
        query_bias, out_bias, latent_gain, latent_bias, mlp_gain, mlp_bias, up_bias, down_bias,
        input_gain, input_bias, value_bias,
    )
    fused = lax.axis_size("dp") == 8
    rows, rgb_out, *rest = layer(
        images, slots, parts, fused, image_sizes, pixel_rgb, latents, query_weight, out_weight, up_weight, down_weight,
        key_weight, value_weight, cotangent, vectors,
    )
    if fused:
        down, up, out, query, latents_sum, key, value, vec, ext = rest
        (
            latents_out, down, up, out, query, latents_sum, key, value, rgb_grad,
            db, ub, ob, mg, mb, vb, qb, lg, lb, gain, bias,
        ) = finish(rgb_out, vec, ext, rows, down, up, out, query, latents_sum, key, value)
    else:
        down, up, out, query, latents_sum, key, value, vec, ext = sums_plain(
            parts, *rest[:5], latents, query_weight, out_weight, rest[5], rest[6], jnp.stack(vectors[:8]), rest[7]
        )
        latents_out = rows
        rgb_grad = rgb_out.reshape(4, tiles, TILE)[:3].reshape(3, tiles * TILE)
        db, ub, ob, mg, mb = (vec[i] for i in range(5))
        vb, qb, lg, lb = (vec[i] for i in range(8, 12))
        gain, bias = restore(ext[0]), restore(ext[1])
    return (
        latents_out, rgb_grad, latents_sum, query, qb, key, value, vb, out, ob, lg, lb, mg, mb, up, ub, down, db,
        gain, bias,
    )


def solution(mesh):
    whole = P()
    placed = (
        whole,
        P(None, ("dp", "pix")),
        P(None, ("dp", "pix")),
        P(("dp", "pix")),
        P(None, "dp"),
    ) + (whole,) * 17 + (P(("dp", "pix"), None, None),)
    square = P("pix", "dp")
    return jax.shard_map(
        shards,
        mesh=mesh,
        in_specs=placed,
        out_specs=(
            P(("dp", "pix"), None, None),
            P(None, ("dp", "pix")),
            square,
            square,
            whole,
            whole,
            whole,
            whole,
            square,
            whole,
            whole,
            whole,
            whole,
            whole,
            square,
            whole,
            square,
            whole,
            whole,
            whole,
        ),
        check_vma=False,
    )
```

```python
from functools import partial
import math
from types import SimpleNamespace

import jax
import jax.numpy as jnp
from jax import lax
from jax.experimental import pallas as pl
from jax.experimental.pallas import tpu as pltpu
from jax.sharding import PartitionSpec as P

BANDS = 64
MAXRES = 224
BIG_SIDE = 112
SMALL_SIDE = 32
EPSILON = 1e-05
FEAT = 4 * BANDS + 5
WIDE = FEAT + 11
DQ = 384
PACK = 320
TILE = 512
LANES = 128
MESH = pl.DeviceIdType.MESH
SENDS = 55
VMEM_LIMIT = 62 * 2**20

bf16 = jnp.bfloat16
f32 = jnp.float32


def dot(a, b, dims):
    return lax.dot_general(a, b, (dims, ((), ())), preferred_element_type=f32)


def nn(a, b):
    return dot(a, b, ((1,), (0,)))


def nt(a, b):
    return dot(a, b, ((1,), (1,)))


def tn(a, b):
    return dot(a, b, ((0,), (0,)))


def order_of(rows, cols, flip=False):
    b = 2 * BANDS
    f = lax.broadcasted_iota(jnp.int32, (rows, cols), 1 if flip else 0)
    g = lax.broadcasted_iota(jnp.int32, (rows, cols), 0 if flip else 1)
    to = jnp.where(f < 4, f + 2 * b, jnp.where(f < 4 + b, f - 4, jnp.where(f == 4 + b, 2 * b + 4, f - 5)))
    return ((to == g) & (f < FEAT)).astype(bf16)


def moved(rows, order, product):
    total = None
    for _ in range(3):
        part = rows.astype(bf16)
        rows = rows - part.astype(f32)
        piece = product(part, order)
        total = piece if total is None else total + piece
    return total


def centred(rows, axis):
    live = lax.broadcasted_iota(jnp.int32, rows.shape, axis) < FEAT
    rows = jnp.where(live, rows, 0.0)
    return jnp.where(live, rows - jnp.sum(rows, axis=axis, keepdims=True) * (1.0 / FEAT), 0.0)


def norm(rows):
    centre = rows - jnp.mean(rows, axis=-1, keepdims=True)
    scale = lax.rsqrt(jnp.mean(centre * centre, axis=-1, keepdims=True) + EPSILON)
    return centre * scale, scale


def norm_back(grad, unit, scale):
    return (
        grad
        - jnp.mean(grad, axis=-1, keepdims=True)
        - unit * jnp.mean(grad * unit, axis=-1, keepdims=True)
    ) * scale


def tanh(a):
    return 1.0 - 2.0 / (1.0 + jnp.exp(jnp.minimum(2.0 * a, 80.0)))


def sin_cos_pi(p):
    n = jnp.floor(p + 0.5)
    z = (p - n) * math.pi
    q = z * z
    s = z * (1.0 + q * (-1.0 / 6 + q * (1.0 / 120 + q * (-1.0 / 5040 + q * (1.0 / 362880 - q * (1.0 / 39916800))))))
    c = 1.0 + q * (
        -0.5 + q * (1.0 / 24 + q * (-1.0 / 720 + q * (1.0 / 40320 + q * (-1.0 / 3628800 + q * (1.0 / 479001600)))))
    )
    sign = 1.0 - 2.0 * (n - 2.0 * jnp.floor(n * 0.5))
    return s * sign, c * sign


def tiles_of(images, slots):
    spare = (images - 1) * SMALL_SIDE * SMALL_SIDE
    head = -(-spare // TILE)
    tail = BIG_SIDE * BIG_SIDE // TILE
    last = min(-(-(BIG_SIDE * BIG_SIDE + spare) // TILE), slots // TILE)
    return head, max(head, tail), last


def loop(lo, hi, body, unroll):
    steps = (hi - lo) // unroll
    if steps > 0:
        lax.fori_loop(0, steps, lambda i, c: (body([lo + i * unroll + k for k in range(unroll)]), c)[1], 0)
    if lo + steps * unroll < hi:
        body(list(range(lo + steps * unroll, hi)))


def wait(copies):
    for copy in copies:
        copy.wait()


def summed(first, others):
    total = first.astype(f32)
    for i in range(others.shape[0]):
        total = total + others[i].astype(f32)
    return total


MLP_UNROLL = 2
HEAD_UNROLL = 3
BIG_UNROLL = 3


def layer_kernel(images, slots, parts, fused, names, *refs):
    r = SimpleNamespace(**dict(zip(names, refs)))
    group, place = lax.axis_index("dp"), lax.axis_index("pix")
    count, width = r.latents_h.shape
    own, chunk = count // parts, width // parts
    rows_all = images * own
    head, tail, last = tiles_of(images, slots)
    per = r.rgb_in.shape[0] // 4
    factor = 1.0 / math.sqrt(width)
    core, quad = lax.rem(group, 2), lax.rem(group // 2, 4)
    base = group // 8 * 4
    x, y = lax.rem(quad, 2), quad // 2
    mate = ((base + quad) * 2 + 1 - core, place)

    def away(k):
        other = (1 - x if k % 2 else x) + 2 * (1 - y if k // 2 else y)
        return other, ((base + other) * 2 + core, place)

    zs = [(s, lax.rem(place + s, parts), lax.rem(place + parts - s, parts)) for s in range(1, parts)]
    used = [0]

    def send(src, dst, target):
        i = used[0]
        used[0] += 1
        copy = pltpu.make_async_remote_copy(
            src_ref=src, dst_ref=dst, send_sem=r.sems.at[0, i], recv_sem=r.sems.at[1, i],
            device_id=target, device_id_type=MESH,
        )
        copy.start()
        return copy

    def send_z(pick, put):
        return [send(pick(to), put(s), (group, to)) for s, to, _ in zs]

    def send_quad(pick, put):
        return [send(pick(away(k)[0]), put(k), away(k)[1]) for k in (1, 2, 3)]

    barrier = pltpu.get_barrier_semaphore()
    friends = [(group, to) for _, to, _ in zs]
    if fused:
        friends += [mate] + [away(k)[1] for k in (1, 2, 3)]
    for device in friends:
        pl.semaphore_signal(barrier, inc=1, device_id=device, device_id_type=MESH)
    loads = [
        pltpu.make_async_copy(a, b, r.load_sems.at[i])
        for i, (a, b) in enumerate(
            (
                (r.wq_h, r.wq), (r.wo_h, r.wo), (r.cot_h, r.cot_f), (r.up_h, r.up), (r.down_h, r.down),
                (r.latents_h, r.latents), (r.wv_h, r.wv_in),
            )
        )
    ]
    for i in (5, 0, 6, 1, 2, 3, 4):
        loads[i].start()

    shades = r.pixel_rgb[...].astype(f32)
    pieces = [shades[c : c + 1, j * TILE : (j + 1) * TILE] for c in range(3) for j in range(per)]
    r.rgb_in[...] = jnp.concatenate(pieces + [jnp.zeros((per, TILE), f32)], axis=0).astype(bf16)
    r.vecs[...] = jnp.zeros_like(r.vecs)
    for i in range(11):
        vec = getattr(r, f"vec{i}")
        r.vecs[i : i + 1, : vec.shape[0]] = vec[...].reshape(1, vec.shape[0])

    to_waves = order_of(WIDE, FEAT, flip=True)
    r.wk[:WIDE] = nn(to_waves, r.wk_in[...]).astype(bf16)
    r.wk[WIDE:] = jnp.zeros_like(r.wk[WIDE:])
    feats = moved(r.vecs[8:16, :DQ], order_of(DQ, DQ), nn)
    r.feats[...] = feats
    gain, bias = feats[0:1, :WIDE], feats[1:2, :WIDE]

    pl.semaphore_wait(barrier, len(friends))
    rgb_copies = send_z(lambda to: r.rgb_in, lambda s: r.rgb_recv.at[s - 1])

    loads[5].wait()
    loads[0].wait()
    rows = pl.ds(pl.multiple_of(place * own, own), own)
    lat_rows = r.latents[rows, :].astype(f32)
    own_unit, _ = norm(lat_rows)
    own_in = (own_unit * r.vecs[2:3, :] + r.vecs[3:4, :]).astype(bf16)
    own_queries = ((nn(own_in, r.wq[...]) + r.vecs[0:1, :]) * factor).astype(bf16)
    qk = nt(own_queries, r.wk[:WIDE])
    qc = centred(qk * gain, 1).astype(bf16)
    r.qc[...] = qc
    r.qb[...] = jnp.sum(qk * bias, axis=1, keepdims=True)
    pick = (
        lax.broadcasted_iota(jnp.int32, (16, WIDE), 1)
        == lax.broadcasted_iota(jnp.int32, (16, WIDE), 0) + 4 * BANDS
    ).astype(bf16)
    r.ext[images * 16 :, :] = nt(pick, qc).astype(bf16)

    loads[6].wait()
    vb = r.vecs[10:11, :]
    vb_high = vb.astype(bf16).astype(f32)
    row = lax.broadcasted_iota(jnp.int32, (WIDE, width), 0)
    wv = nn(to_waves, r.wv_in[...])
    r.wv[...] = jnp.where(row == FEAT, vb_high, jnp.where(row == FEAT + 1, vb - vb_high, wv)).astype(bf16)

    wait(rgb_copies)
    for c in range(3):
        at = slice(c * per, (c + 1) * per)
        r.rgbf[c, pl.ds(pl.multiple_of(place * per, per), per), :] = r.rgb_in[at, :].astype(f32)
        for s, _, source in zs:
            r.rgbf[c, pl.ds(pl.multiple_of(source * per, per), per), :] = r.rgb_recv[s - 1, at, :].astype(f32)

    ends, high, wide = [], [], []
    end = jnp.int32(0)
    for i in range(images):
        end = end + r.sizes[0, i] * r.sizes[1, i]
        ends.append(end.astype(f32))
        high.append(jnp.maximum(r.sizes[0, i] - 1, 1).astype(f32))
        wide.append(r.sizes[1, i].astype(f32))
    is_big = [(r.sizes[0, n] > SMALL_SIDE).astype(f32) for n in range(images)]

    def features(j):
        shape = (8, TILE)
        lane = lax.broadcasted_iota(jnp.int32, shape, 1)
        sub = lax.broadcasted_iota(jnp.int32, shape, 0)
        slot = (lane + j * TILE).astype(f32)
        segment = jnp.zeros(shape, f32)
        start = jnp.zeros(shape, f32)
        tall = jnp.full(shape, high[0])
        across = jnp.full(shape, wide[0])
        for i in range(images):
            past = slot >= ends[i]
            segment = jnp.where(past, segment + 1.0, segment)
            if i + 1 < images:
                start = jnp.where(past, ends[i], start)
                tall = jnp.where(past, high[i + 1], tall)
                across = jnp.where(past, wide[i + 1], across)
            else:
                start = jnp.where(past, slot, start)
        local = slot - start
        row = jnp.floor((local + 0.5) / across)
        col = local - row * across
        y = 2.0 * row / tall - 1.0
        x = 2.0 * col / jnp.maximum(across - 1.0, 1.0) - 1.0
        step = (MAXRES / 2.0 - 1.0) / (BANDS - 1)
        lowest = 1.0 + sub.astype(f32) * step
        total = None
        pieces = []
        for spot in (y, x):
            s, c = sin_cos_pi(lowest * spot)
            rs, rc = sin_cos_pi((8 * step) * spot)
            sines, cosines = [s], [c]
            for _ in range(BANDS // 8 - 1):
                s, c = s * rc + c * rs, c * rc - s * rs
                sines.append(s)
                cosines.append(c)
            for k in range(BANDS // 8):
                total = sines[k] + cosines[k] if total is None else total + (sines[k] + cosines[k])
            pieces.append(jnp.concatenate(sines, axis=0).astype(bf16))
            pieces.append(jnp.concatenate(cosines, axis=0).astype(bf16))
        total = jnp.sum(total, axis=0, keepdims=True)
        red, green, blue = (r.rgbf[c, pl.ds(j, 1), :] for c in range(3))
        y, x, segment = y[0:1], x[0:1], segment[0:1]
        total = total + (red + green + blue + y + x)
        squares = red * red + green * green + blue * blue + y * y + x * x + 2.0 * BANDS
        mean = total * (1.0 / FEAT)
        spread = squares * (1.0 / FEAT) - mean * mean + EPSILON
        scale = lax.rsqrt(spread)
        deviation = spread * scale
        rest = deviation - deviation.astype(bf16).astype(f32)
        ext = jnp.zeros(shape, f32)
        for k, v in enumerate((red, green, blue, y, x, deviation, rest)):
            ext = jnp.where(sub == k, v, ext)
        pieces.append(jnp.concatenate([ext, jnp.zeros(shape, f32)], axis=0).astype(bf16))
        tile = jnp.concatenate(pieces, axis=0)
        r.feat[j] = tile
        r.stat[j] = jnp.where(sub == 0, scale, jnp.where(sub == 1, mean, segment))
        return tile, scale, segment

    r.acc[...] = jnp.zeros_like(r.acc)
    r.acc_big[...] = jnp.zeros_like(r.acc_big)

    def side(parts_of):
        return parts_of[0] if len(parts_of) == 1 else jnp.concatenate(parts_of, axis=1)

    def forward(mixed, js):
        tiles, mixes = [], []
        for j in js:
            tile, scale, segment = features(j)
            weights = jnp.exp(nn(r.qc[...], tile) * scale + r.qb[...])
            if mixed:
                weights = jnp.where(segment < images, weights, 0.0)
            r.wst[j] = weights.astype(bf16)
            scaled = (weights * scale).astype(bf16)
            if mixed:
                none = jnp.zeros_like(scaled)
                scaled = jnp.concatenate([jnp.where(segment == n, scaled, none) for n in range(images)], axis=0)
            tiles.append(tile)
            mixes.append(scaled)
        into = r.acc if mixed else r.acc_big
        into[...] += nt(side(tiles), side(mixes))

    loop(0, head, partial(forward, True), HEAD_UNROLL)
    loop(head, tail, partial(forward, False), BIG_UNROLL)
    loop(tail, last, partial(forward, True), HEAD_UNROLL)

    lane = lax.broadcasted_iota(jnp.int32, (own, WIDE), 1)
    ones = ((lane == FEAT) | (lane == FEAT + 1)).astype(f32)
    big = r.acc_big[...]
    mix_all = (r.acc[...] + jnp.concatenate([big * is_big[n] for n in range(images)], axis=1)).T
    for n in range(images):
        at = slice(n * own, (n + 1) * own)
        mix = mix_all[at]
        totals = mix[:, FEAT : FEAT + 1] + mix[:, FEAT + 1 : FEAT + 2]
        unit = centred(mix, 1) / totals
        r.tot[at, :] = totals
        r.unit[at, :] = unit
        r.px_send[n] = (unit * gain + bias + ones).astype(bf16).T
    px_copies = send_z(lambda to: r.px_send.at[to], lambda s: r.px_recv.at[place])
    r.px_recv[place] = r.px_send[place]

    loads[1].wait()
    wvo = nn(r.wv[...], r.wo[...])
    const = wvo[FEAT : FEAT + 1] + wvo[FEAT + 1 : FEAT + 2] + r.vecs[1:2, :]
    r.wvo[...] = jnp.where(row < FEAT, wvo, 0.0).astype(bf16)
    loads[2].wait()
    loads[3].wait()
    loads[4].wait()
    k = math.sqrt(2.0 / math.pi)
    half = 2 * own
    wait(px_copies)
    out_copies = []
    for blk in range(count // half):
        at = slice(blk * half, (blk + 1) * half)
        px_t = jnp.concatenate([r.px_recv[2 * blk + i] for i in range(2)], axis=1)
        r.px_t[:, at] = px_t
        middle = r.latents[at, :].astype(f32) + nn(px_t.T, r.wvo[...]) + const
        mid_unit, mid_scale = norm(middle)
        mid_in = (mid_unit * r.vecs[4:5, :] + r.vecs[5:6, :]).astype(bf16)
        hidden = nn(mid_in, r.up[...]) + r.vecs[6:7, :]
        th = tanh(k * (hidden + 0.044715 * hidden * hidden * hidden))
        active = (0.5 * hidden * (1.0 + th)).astype(bf16)
        r.slope[at, :] = 0.5 * (1.0 + th) + 0.5 * hidden * (1.0 - th * th) * k * (
            1.0 + 3 * 0.044715 * hidden * hidden
        )
        stage = (r.key_out, r.value_out)[blk].at[pl.ds(0, half)] if fused else (r.stage0, r.stage1)[blk]
        stage[...] = middle + nn(active, r.down[...]) + r.vecs[7:8, :]
        copy = pltpu.make_async_copy(stage, r.out_rows.at[0, pl.ds(blk * half, half)], r.load_sems.at[7 + blk])
        copy.start()
        out_copies.append(copy)
        r.mid_unit[at, :] = mid_unit
        r.mid_scale[at, :] = mid_scale
        r.act_t[:, at] = active.T
        r.mid_t[:, at] = mid_in.T

    def down_grads(jj, c):
        cols = pl.ds(pl.multiple_of(jj * 256, 256), 256)
        part = nn(r.act_t[...], r.cot_f[0, :, cols].astype(bf16)).astype(bf16)
        for i in range(2):
            r.down_pay[i, lax.rem(jj, 2) * 2 + jj // 2] = part[:, i * LANES : (i + 1) * LANES]
        return c

    lax.fori_loop(0, width // 256, down_grads, 0)
    if fused:
        core_down = send(r.down_pay.at[1 - core], r.down_c, mate)

    def fold(first, value):
        for i in range(width // count):
            r.act_t[i * count + first : i * count + first + value.shape[0], :] = value[:, i * count : (i + 1) * count]

    def unfold(first, size):
        at = pl.ds(pl.multiple_of(first // count * count, count), count)
        return r.act_t[at, pl.ds(pl.multiple_of(lax.rem(first, count), LANES), size)]

    total_sums, ext_total = None, None
    for blk in range(count // half):
        at = slice(blk * half, (blk + 1) * half)
        if fused and blk == 1:
            core_down.wait()
            for b in range(4):
                r.down_c[b] = r.down_c[b] + r.down_pay[core, b]
            first_down = send(r.down_c.at[pl.ds((1 - x) * 2, 2)], r.down_1, away(1)[1])
        grad_down = r.cot_f[0, at, :].astype(bf16)
        grad_hidden = (r.slope[at, :] * nt(grad_down, r.down[...])).astype(bf16)
        fold(blk * half, grad_hidden)
        grad_mid = nt(grad_hidden, r.up[...])
        mid_unit = r.mid_unit[at, :]
        grad_middle = r.cot_f[0, at, :] + norm_back(grad_mid * r.vecs[4:5, :], mid_unit, r.mid_scale[at, :])
        branch = grad_middle.astype(bf16)
        r.branch[at, :] = branch
        for d in range(width // LANES):
            q = d // 2
            r.lat_pay[d % 2, q % 2 * 2 + q // 2, at, :] = branch[:, d * LANES : (d + 1) * LANES]
        part = [
            jnp.sum(v, axis=0, keepdims=True)
            for v in (grad_down.astype(f32), grad_hidden.astype(f32), branch.astype(f32), grad_mid * mid_unit, grad_mid)
        ]
        total_sums = part if total_sums is None else [u + v for u, v in zip(total_sums, part)]
        gx = nt(r.wvo[...], branch)
        r.px_send[2 * blk] = gx[:, :own].astype(bf16)
        r.px_send[2 * blk + 1] = gx[:, own:].astype(bf16)
        part = [jnp.sum(gx * r.px_t[:, at].astype(f32), axis=1, keepdims=True), jnp.sum(gx, axis=1, keepdims=True)]
        ext_total = part if ext_total is None else [u + v for u, v in zip(ext_total, part)]
    gx_copies = send_z(lambda to: r.px_send.at[to], lambda s: r.gx_recv.at[place])
    r.gx_recv[place] = r.px_send[place]
    lane = lax.broadcasted_iota(jnp.int32, (WIDE, LANES), 1)
    ext_rows = jnp.where(lane == 0, ext_total[0], jnp.where(lane == 1, ext_total[1], 0.0)).T
    live = lax.broadcasted_iota(jnp.int32, (1, WIDE), 1) < FEAT
    gain_part = jnp.where(live, (ext_rows[0:1] - bias * ext_rows[1:2]) / jnp.where(live, gain, 1.0), 0.0)
    small = jnp.concatenate(
        total_sums
        + [jnp.pad(v, ((0, 0), (0, width - WIDE))) for v in (gain_part, jnp.where(live, ext_rows[1:2], 0.0))]
        + [jnp.zeros((PACK - WIDE - 7, width), f32)],
        axis=0,
    ).astype(bf16)
    for d in range(width // LANES):
        r.pack[d % 2, d // 2, WIDE:, :] = small[:, d * LANES : (d + 1) * LANES]


    def moments(jj, c):
        cols = pl.ds(pl.multiple_of(jj * 256, 256), 256)
        part = nn(r.px_t[...], r.branch[:, cols]).astype(bf16)
        for i in range(2):
            r.pack[i, jj, :WIDE] = part[:, i * LANES : (i + 1) * LANES]
        return c

    def up_grads(jj, c):
        cols = pl.ds(pl.multiple_of(jj * 256, 256), 256)
        part = nn(r.mid_t[...], unfold(jj * 256, 256)).astype(bf16)
        for i in range(2):
            r.up_pay[i, jj] = part[:, i * LANES : (i + 1) * LANES]
        return c

    lax.fori_loop(0, width // 256, moments, 0)
    if fused:
        core_pack = send(r.pack.at[1 - core], r.pack_c, mate)
        core_lat = send(r.lat_pay.at[1 - core], r.lat_c, mate)
    lax.fori_loop(0, width // 256, up_grads, 0)
    if fused:
        core_up = send(r.up_pay.at[1 - core], r.up_c, mate)

    if fused:
        unit, scale = norm(r.latents[...].astype(f32))
        r.mid_unit[...] = unit
        r.mid_scale[...] = scale
        lat_low = (unit * r.vecs[2:3, :] + r.vecs[3:4, :]).astype(bf16)
        fold(0, lat_low)
        queries = ((nn(lat_low, r.wq[...]) + r.vecs[0:1, :]) * factor).astype(bf16)
        r.branch[...] = queries
        r.qk_all[...] = nt(queries, r.wk[...])
    wait(gx_copies)
    gcb = jnp.zeros((own, WIDE), f32)
    levb = jnp.zeros((own, 1), f32)
    for n in range(images):
        at = slice(n * own, (n + 1) * own)
        gc = centred(r.gx_recv[n].T.astype(f32) * gain, 1) / r.tot[at, :]
        gc_low = gc.astype(bf16)
        level = jnp.sum(gc_low.astype(f32) * r.unit[at, :], axis=1, keepdims=True)
        r.gc[at, :] = gc_low
        r.lev[at, :] = level
        r.ext[n * 16 : (n + 1) * 16, :] = nt(pick, gc_low).astype(bf16)
        gcb = gcb + gc * is_big[n]
        levb = levb + level * is_big[n]
    r.gc[rows_all :, :] = r.qc[...]
    r.gcb[:own, :] = gcb.astype(bf16)
    r.gcb[own:, :] = r.qc[...]
    r.levb[...] = levb
    r.extb[:, own:] = nt(pick, r.gcb[:own, :]).astype(bf16)
    r.extb[:, :own] = r.ext[images * 16 :, :]

    if fused:
        core_pack.wait()
        r.pack_c[...] = r.pack_c[...] + r.pack[core]
        quad_pack = send_quad(lambda q: r.pack_c.at[q], lambda k: r.pack_q.at[k - 1])
        core_lat.wait()
        for b in range(4):
            r.lat_c[b] = r.lat_c[b] + r.lat_pay[core, b]
        first_lat = send(r.lat_c.at[pl.ds((1 - x) * 2, 2)], r.lat_1, away(1)[1])
        core_up.wait()
        for b in range(4):
            r.up_c[b] = r.up_c[b] + r.up_pay[core, b]
        first_up = send(r.up_c.at[pl.ds((1 - y) * 2, 2)], r.up_1, away(2)[1])

    r.dq_sum[...] = jnp.zeros_like(r.dq_sum)
    r.rgbp[...] = jnp.zeros_like(r.rgbp)

    def backward(mixed, js):
        tiles, grads = [], []
        for j in js:
            tile = r.feat[j]
            scale = r.stat[j, 0:1, :]
            mean = r.stat[j, 1:2, :]
            low_weights = r.wst[j]
            weights = low_weights.astype(f32)
            pulls = nn(r.gc[...] if mixed else r.gcb[...], tile)
            raw = pulls[-own:] * scale
            if mixed:
                segment = r.stat[j, 2:3, :]
                pull = jnp.zeros_like(weights)
                level = jnp.zeros_like(weights)
                for n in range(images):
                    at = slice(n * own, (n + 1) * own)
                    here = segment == n
                    pull = jnp.where(here, pulls[at], pull)
                    level = jnp.where(here, r.lev[at, :], level)
            else:
                pull = pulls[:own]
                level = r.levb[...]
            pull = pull * scale
            grad = weights * (pull - level)
            lean = jnp.sum(grad * raw + weights * pull, axis=0, keepdims=True) * (1.0 / FEAT)
            if mixed:
                colours = nn(r.ext[: images * 16, :], low_weights)
                back = nn(r.ext[images * 16 :, :], grad.astype(bf16))
                picked = jnp.zeros_like(back)
                for n in range(images):
                    picked = jnp.where(segment == n, colours[n * 16 : (n + 1) * 16], picked)
                back = back + picked
            else:
                back = nn(r.extb[...], jnp.concatenate([grad.astype(bf16), low_weights], axis=0))
            ext = tile[4 * BANDS :, :].astype(f32)
            part = (back - (ext - mean) * scale * lean) * scale
            for c in range(3):
                r.rgbp[c, pl.ds(j, 1), :] = part[c : c + 1]
            tiles.append(tile)
            grads.append((grad * scale).astype(bf16))
        r.dq_sum[...] += nt(side(tiles), side(grads))

    step = 2 * BIG_UNROLL
    loop(0, head, partial(backward, True), HEAD_UNROLL)
    loop(head, head + BIG_UNROLL, partial(backward, False), BIG_UNROLL)
    if fused:
        pack_rows = PACK // parts
        mine = pl.ds(pl.multiple_of(place * pack_rows, 16), pack_rows)
    at = head + BIG_UNROLL
    loop(at, at + step, partial(backward, False), BIG_UNROLL)
    if fused:
        wait(quad_pack)
        r.pack_m[...] = summed(r.pack_c[quad], r.pack_q).astype(bf16)
        z_pack = send_z(
            lambda to: r.pack_m.at[pl.ds(pl.multiple_of(to * pack_rows, 16), pack_rows)], lambda s: r.pack_z.at[s - 1]
        )
        first_down.wait()
        for b in range(2):
            r.down_1[b] = r.down_1[b] + r.down_c[x * 2 + b]
        second_down = send(r.down_1.at[1 - y], r.down_2, away(2)[1])
    loop(at + step, at + 2 * step, partial(backward, False), BIG_UNROLL)
    if fused:
        wait(z_pack)
        r.pack_own[...] = summed(r.pack_m[mine, :], r.pack_z).astype(bf16)
        r.pack_all[core, quad, mine, :] = r.pack_own[...]
        all_pack = send_z(lambda to: r.pack_own, lambda s: r.pack_all.at[core, quad, mine])
    loop(at + 2 * step, tail, partial(backward, False), BIG_UNROLL)
    loop(tail, last, partial(backward, True), HEAD_UNROLL)

    dq = r.dq_sum[...].T
    lanes = lax.broadcasted_iota(jnp.int32, dq.shape, 1)
    gs_sum = dq[:, FEAT : FEAT + 1] + dq[:, FEAT + 1 : FEAT + 2]
    dq = jnp.where(lanes == FEAT, gs_sum, centred(dq, 1)).astype(bf16)
    r.dq_pay[...] = jnp.zeros_like(r.dq_pay)
    each = own // 8
    for d in range(8):
        r.dq_pay[d % 2, d // 2, :, :WIDE] = dq[d * each : (d + 1) * each]
    if fused:
        core_dq = send(r.dq_pay.at[1 - core], r.dq_c, mate)

    for t in range(parts):
        r.rgb_send[t] = jnp.concatenate(
            [r.rgbp[c, t * per : (t + 1) * per, :] for c in range(3)] + [jnp.zeros((per, TILE), f32)], axis=0
        ).astype(bf16)
    back_copies = send_z(lambda to: r.rgb_send.at[to], lambda s: r.rgb_back.at[s - 1])

    if fused:
        core_dq.wait()
        r.dq_c[...] = r.dq_c[...] + r.dq_pay[core]
        quad_dq = send_quad(lambda q: r.dq_c.at[q], lambda k: r.dq_q.at[k - 1])
        wait(all_pack)
        all_pack = send_quad(lambda q: r.pack_all.at[core, quad], lambda k: r.pack_all.at[core, quad])
        first_lat.wait()
        for b in range(2):
            r.lat_1[b] = r.lat_1[b] + r.lat_c[x * 2 + b]
        second_lat = send(r.lat_1.at[1 - y], r.lat_2, away(2)[1])
        first_up.wait()
        for b in range(2):
            r.up_1[b] = r.up_1[b] + r.up_c[y * 2 + b]
        second_up = send(r.up_1.at[1 - x], r.up_2, away(1)[1])
        wait(quad_dq)
        r.dq_own[...] = summed(r.dq_c[quad], r.dq_q).astype(bf16)
        r.dq_all[core, quad, place] = r.dq_own[...]
        z_dq = send_z(lambda to: r.dq_own, lambda s: r.dq_all.at[core, quad, place])
        second_down.wait()
        r.down_2[...] = (r.down_1[y].astype(f32) + r.down_2[...].astype(f32)).astype(bf16)
        z_down = send_z(
            lambda to: r.down_2.at[pl.ds(pl.multiple_of(to * chunk, 16), chunk)], lambda s: r.down_z.at[s - 1]
        )
        wait(all_pack)
        all_pack = send(r.pack_all.at[core], r.pack_all.at[core], mate)
        wait(z_dq)
        all_dq = send_quad(lambda q: r.dq_all.at[core, quad], lambda k: r.dq_all.at[core, quad])

        second_up.wait()
        r.up_2[...] = (r.up_1[x].astype(f32) + r.up_2[...].astype(f32)).astype(bf16)
        z_up = send_z(
            lambda to: r.up_2.at[pl.ds(pl.multiple_of(to * chunk, 16), chunk)], lambda s: r.up_z.at[s - 1]
        )
        second_lat.wait()
        r.lat_2[...] = (r.lat_1[y].astype(f32) + r.lat_2[...].astype(f32)).astype(bf16)
        z_lat = send_z(
            lambda to: r.lat_2.at[pl.ds(pl.multiple_of(to * own, 16), own)], lambda s: r.lat_z.at[s - 1]
        )
        all_pack.wait()

        own_cols = pl.ds(pl.multiple_of(lax.rem(group, 8) * LANES, LANES), LANES)
        lat_cols = pl.ds(pl.multiple_of(place * chunk, LANES), chunk)
        for d in range(8):
            r.moment[:, d * LANES : (d + 1) * LANES] = r.pack_all[d % 2, d // 2]
        order = order_of(264, DQ)
        wait(out_copies)
        r.value_out[...] = nt(nn(order[:, :WIDE], r.moment[:WIDE, :]).astype(bf16), r.wo[...])[:FEAT]
        r.out_out[...] = tn(r.wv[:, lat_cols], r.moment[:WIDE, own_cols])
        small = r.moment[WIDE : WIDE + 16, :]
        value_bias = nt(small, r.wo[...])[2:3]
        small = small.astype(f32)
    wait(back_copies)
    r.rgb_out[...] = summed(r.rgb_send[place], r.rgb_back).astype(bf16)

    if fused:
        block = pl.ds(pl.multiple_of(place * chunk, 16), chunk)
        wait(z_down)
        r.down_out[...] = summed(r.down_2[block, :], r.down_z)
        wait(all_dq)
        all_dq = send(r.dq_all.at[core], r.dq_all.at[core], mate)
        all_dq.wait()

        for z in range(parts):
            for d in range(8):
                r.dq[(z * 8 + d) * each : (z * 8 + d + 1) * each, :] = r.dq_all[d % 2, d // 2, z]
        units = r.dq[...].astype(f32)
        lean = units[:, FEAT : FEAT + 1]
        units = jnp.where(lax.broadcasted_iota(jnp.int32, units.shape, 1) < FEAT, units, 0.0)
        gain_sum = jnp.sum(r.qk_all[...] * units, axis=0, keepdims=True)
        bias_sum = jnp.sum(r.qk_all[...] * lean, axis=0, keepdims=True)
        dx = (units * r.feats[0:1, :] + lean * r.feats[1:2, :]).astype(bf16)
        r.key_out[...] = nn(nt(order, dx).astype(bf16), r.branch[...])[:FEAT]
        gq = nn(dx, r.wk[...]) * factor
        gq_low = gq.astype(bf16)
        query_bias = jnp.sum(gq, axis=0, keepdims=True)
        grad_lat = nt(gq_low, r.wq[...])
        latent_gain = jnp.sum(grad_lat * r.mid_unit[...], axis=0, keepdims=True)
        latent_bias = jnp.sum(grad_lat, axis=0, keepdims=True)
        r.branch[...] = gq_low
        r.query_out[...] = tn(unfold(place * chunk, chunk), r.branch[:, own_cols])
        r.mid_unit[...] = norm_back(grad_lat * r.vecs[2:3, :], r.mid_unit[...], r.mid_scale[...])

        r.vec_out[...] = jnp.concatenate(
            [small[:8], value_bias, query_bias, latent_gain, latent_bias, jnp.zeros((4, width), f32)], axis=0
        )
        ends_of = jnp.concatenate(
            [small[5:6, :DQ] + gain_sum, small[6:7, :DQ] + bias_sum, jnp.zeros((6, DQ), f32)], axis=0
        )
        r.ext_out[...] = moved(ends_of, order_of(DQ, DQ), nt)

        wait(z_up)
        r.up_out[...] = summed(r.up_2[block, :], r.up_z)
        wait(z_lat)
        r.latents_out[...] = summed(r.lat_2[rows, :], r.lat_z) + r.mid_unit[rows, own_cols]
    else:
        wait(out_copies)


def layer(images, slots, parts, fused, sizes, pixel_rgb, latents, wq, wo, up, down, wk, wv, cot, vectors):
    count, width = latents.shape
    own, chunk = count // parts, width // parts
    rows = images * own
    hidden = up.shape[1]
    tiles = slots // TILE
    colours = (4 * tiles // parts, TILE)
    last = tiles_of(images, slots)[2]
    each = own // 8
    any_, vm = pl.BlockSpec(memory_space=pl.ANY), pl.BlockSpec(memory_space=pltpu.VMEM)
    sds = jax.ShapeDtypeStruct
    V = pltpu.VMEM
    ins = [
        ("sizes", sizes, pl.BlockSpec(memory_space=pltpu.SMEM)), ("pixel_rgb", pixel_rgb, vm), ("latents_h", latents, any_),
        ("wq_h", wq, any_), ("wo_h", wo, any_), ("up_h", up, any_), ("down_h", down, any_),
        ("wk_in", wk, vm), ("wv_h", wv, any_), ("cot_h", cot, any_),
    ] + [(f"vec{i}", v, vm) for i, v in enumerate(vectors)]
    pays = [
        ("down_pay", (2, 4, hidden, LANES), bf16), ("up_pay", (2, 4, width, LANES), bf16), ("lat_pay", (2, 4, count, LANES), bf16),
        ("pack", (2, 4, PACK, LANES), bf16), ("dq_pay", (2, 4, each, DQ), bf16),
        ("wk", (DQ, width), bf16), ("wv", (WIDE, width), bf16), ("feats", (8, DQ), f32),
    ]
    outs = [("out_rows", cot.shape, f32), ("rgb_out", colours, bf16)]
    scratch = [
        ("feat", (last, WIDE, TILE), bf16), ("stat", (last, 8, TILE), f32), ("wst", (last, own, TILE), bf16),
        ("rgb_in", colours, bf16), ("vecs", (16, width), f32), ("rgb_recv", (parts - 1,) + colours, bf16), ("rgbf", (3, tiles, TILE), f32), ("rgbp", (3, tiles, TILE), f32),
        ("rgb_send", (parts,) + colours, bf16), ("rgb_back", (parts - 1,) + colours, bf16),
        ("latents", latents.shape, bf16), ("wv_in", wv.shape, bf16), ("wq", wq.shape, bf16), ("wo", wo.shape, bf16), ("up", up.shape, bf16), ("down", down.shape, bf16),
        ("cot_f", cot.shape, f32), ("slope", (count, hidden), f32),
        ("px_send", (images, WIDE, own), bf16), ("px_recv", (parts, WIDE, own), bf16),
        ("gx_recv", (images, WIDE, own), bf16),
        ("qc", (own, WIDE), bf16), ("qb", (own, 1), f32), ("ext", (images * 16 + 16, own), bf16),
        ("extb", (16, 2 * own), bf16),
        ("acc", (WIDE, rows), f32), ("acc_big", (WIDE, own), f32), ("unit", (rows, WIDE), f32),
        ("wvo", (WIDE, width), bf16), ("tot", (rows, 1), f32),
        ("mid_unit", (count, width), f32), ("mid_scale", (count, 1), f32),
        ("act_t", (hidden, count), bf16), ("mid_t", (width, count), bf16), ("px_t", (WIDE, count), bf16),
        ("branch", (count, width), bf16),
        ("gc", (rows + own, WIDE), bf16), ("gcb", (2 * own, WIDE), bf16), ("lev", (rows, 1), f32), ("levb", (own, 1), f32),
        ("dq_sum", (WIDE, own), f32),
    ]
    if fused:
        outs += [
            ("down_out", (chunk, LANES), f32), ("up_out", (chunk, LANES), f32), ("out_out", (chunk, LANES), f32),
            ("query_out", (chunk, LANES), f32), ("latents_out", (own, LANES), f32), ("key_out", (FEAT, width), f32),
            ("value_out", (FEAT, width), f32), ("vec_out", (16, width), f32), ("ext_out", (8, DQ), f32),
        ]
        scratch += pays + [
            ("down_c", (4, hidden, LANES), bf16), ("down_1", (2, hidden, LANES), bf16), ("down_2", (hidden, LANES), bf16),
            ("down_z", (parts - 1, chunk, LANES), bf16),
            ("up_c", (4, width, LANES), bf16), ("up_1", (2, width, LANES), bf16), ("up_2", (width, LANES), bf16),
            ("lat_c", (4, count, LANES), bf16), ("lat_1", (2, count, LANES), bf16), ("lat_2", (count, LANES), bf16),
            ("up_z", (parts - 1, chunk, LANES), bf16),
            ("lat_z", (parts - 1, own, LANES), bf16),
            ("pack_c", (4, PACK, LANES), bf16), ("pack_q", (3, PACK, LANES), bf16), ("pack_m", (PACK, LANES), bf16),
            ("pack_z", (parts - 1, PACK // parts, LANES), bf16), ("pack_own", (PACK // parts, LANES), bf16),
            ("pack_all", (2, 4, PACK, LANES), bf16),
            ("dq_c", (4, each, DQ), bf16), ("dq_q", (3, each, DQ), bf16), ("dq_own", (each, DQ), bf16),
            ("dq_all", (2, 4, parts, each, DQ), bf16), ("dq", (count, DQ), bf16), ("moment", (PACK, width), bf16),
            ("qk_all", (count, DQ), f32),
        ]
    else:
        outs += pays
        scratch += [("stage0", (2 * own, width), f32), ("stage1", (2 * own, width), f32)]
    names = [n for n, _, _ in ins + outs + scratch] + ["load_sems", "sems"]
    return pl.pallas_call(
        partial(layer_kernel, images, slots, parts, fused, names),
        out_shape=tuple(sds(s, d) for _, s, d in outs),
        in_specs=[spec for _, _, spec in ins],
        out_specs=(any_,) + (vm,) * (len(outs) - 1),
        scratch_shapes=[V(s, d) for _, s, d in scratch]
        + [pltpu.SemaphoreType.DMA((9,)), pltpu.SemaphoreType.DMA((2, SENDS))],
        compiler_params=pltpu.CompilerParams(collective_id=0, has_side_effects=True, vmem_limit_bytes=VMEM_LIMIT),
        name="layer",
    )(*[a for _, a, _ in ins])


def finish_kernel(moves, rgb, vec, ext, *refs):
    whole, whole_out = refs[:moves], refs[moves : 2 * moves]
    rgb_grad, *vec_out = refs[2 * moves :]
    for a, b in zip(whole, whole_out):
        b[...] = a[...]
    colours = rgb[...].astype(f32)
    per = rgb.shape[0] // 4
    rgb_grad[...] = jnp.concatenate(
        [
            jnp.concatenate([colours[c * per + j : c * per + j + 1] for j in range(per)], axis=1)
            for c in range(3)
        ],
        axis=0,
    ).astype(bf16)
    for i, out in enumerate(vec_out[:9]):
        out[...] = vec[i if i < 5 else i + 3, :]
    for i, out in enumerate(vec_out[9:]):
        out[...] = ext[i, :FEAT]


def finish(rgb, vec, ext, *whole):
    width = vec.shape[1]
    vm = pl.BlockSpec(memory_space=pltpu.VMEM)
    sds = jax.ShapeDtypeStruct
    n = len(whole)
    outs = (
        tuple(sds(a.shape, a.dtype) for a in whole)
        + (sds((3, rgb.shape[0] // 4 * TILE), bf16),)
        + (sds((width,), f32),) * 9
        + (sds((FEAT,), f32),) * 2
    )
    return pl.pallas_call(
        partial(finish_kernel, n),
        out_shape=outs,
        in_specs=[vm] * (3 + n),
        out_specs=(vm,) * len(outs),
        compiler_params=pltpu.CompilerParams(vmem_limit_bytes=VMEM_LIMIT),
        name="finish",
    )(rgb, vec, ext, *whole)


def restore(rows):
    b = 2 * BANDS
    return jnp.concatenate(
        [rows[2 * b : 2 * b + 4], rows[:b], rows[2 * b + 4 : 2 * b + 5], rows[b : 2 * b]], axis=0
    )


def sums_plain(parts, down_pay, up_pay, lat_pay, pack, dq, latents, wq, wo, wk, wv, vecs, feats):
    count, width = latents.shape
    own, chunk = count // parts, width // parts
    place, group, groups = lax.axis_index("pix"), lax.axis_index("dp"), lax.axis_size("dp")
    cols = width // groups
    factor = 1.0 / math.sqrt(width)

    def flat(a):
        return a.transpose(2, 1, 0, 3).reshape(a.shape[2], width).astype(f32)

    def scattered(a):
        a = lax.psum_scatter(a, "dp", scatter_dimension=1, tiled=True)
        return lax.psum_scatter(a, "pix", scatter_dimension=0, tiled=True)

    def turned(a):
        return a.reshape(2, 2, 2, *a.shape[2:]).transpose(0, 2, 1, 3, 4).reshape(a.shape)

    down_total, up_total = scattered(flat(turned(down_pay))), scattered(flat(up_pay))
    latents_sum = scattered(flat(turned(lat_pay)))
    moment = lax.psum(flat(pack), ("dp", "pix"))
    small, moment = moment[WIDE : WIDE + 8], moment[:WIDE].astype(bf16)
    units = lax.psum(dq.transpose(1, 0, 2, 3).reshape(own, DQ).astype(f32), "dp")
    units = lax.all_gather(units, "pix", axis=0, tiled=True)

    unit, scale = norm(latents.astype(f32))
    lat_in = (unit * vecs[2] + vecs[3]).astype(bf16)
    queries = ((nn(lat_in, wq) + vecs[0]) * factor).astype(bf16)
    lean = units[:, FEAT : FEAT + 1]
    units = units * (jnp.arange(DQ) < FEAT)
    qk = nt(queries, wk)
    ext = jnp.zeros((8, DQ), f32)
    ext = ext.at[0].set(small[5, :DQ] + jnp.sum(qk * units, axis=0))
    ext = ext.at[1].set(small[6, :DQ] + jnp.sum(qk * lean, axis=0))
    dx = (units * feats[0] + lean * feats[1]).astype(bf16)
    key_total = restore(tn(dx, queries))
    gq = nn(dx, wk) * factor
    gq_low = gq.astype(bf16)
    grad_lat = nt(gq_low, wq)
    own_cols = lambda a: lax.dynamic_slice_in_dim(a, group * cols, cols, axis=1)
    own_rows = lambda a: lax.dynamic_slice_in_dim(a, place * chunk, chunk, axis=1)
    query_total = tn(own_rows(lat_in), own_cols(gq_low))
    back = norm_back(grad_lat * vecs[2], unit, scale)
    latents_total = latents_sum + own_cols(lax.dynamic_slice_in_dim(back, place * own, own, axis=0))
    value_total = restore(nt(moment, wo))
    out_total = tn(own_rows(wv), own_cols(moment))
    vec = jnp.concatenate(
        [
            small,
            nt(small.astype(bf16), wo)[2:3],
            jnp.sum(gq, axis=0, keepdims=True),
            jnp.sum(grad_lat * unit, axis=0, keepdims=True),
            jnp.sum(grad_lat, axis=0, keepdims=True),
        ],
        axis=0,
    )
    return down_total, up_total, out_total, query_total, latents_total, key_total, value_total, vec, ext

def shards(
    latents,
    pixel_rgb,
    coords,
    segment_ids,
    image_sizes,
    input_gain,
    input_bias,
    query_weight,
    query_bias,
    key_weight,
    value_weight,
    value_bias,
    out_weight,
    out_bias,
    latent_gain,
    latent_bias,
    mlp_gain,
    mlp_bias,
    up_weight,
    up_bias,
    down_weight,
    down_bias,
    cotangent,
):
    images = image_sizes.shape[1]
    width = latents.shape[1]
    parts = lax.axis_size("pix")
    slots = pixel_rgb.shape[1] * parts
    tiles = pixel_rgb.shape[1] // TILE
    vectors = (
        query_bias, out_bias, latent_gain, latent_bias, mlp_gain, mlp_bias, up_bias, down_bias,
        input_gain, input_bias, value_bias,
    )
    fused = lax.axis_size("dp") == 8
    rows, rgb_out, *rest = layer(
        images, slots, parts, fused, image_sizes, pixel_rgb, latents, query_weight, out_weight, up_weight, down_weight,
        key_weight, value_weight, cotangent, vectors,
    )
    if fused:
        down, up, out, query, latents_sum, key, value, vec, ext = rest
        (
            latents_out, down, up, out, query, latents_sum, key, value, rgb_grad,
            db, ub, ob, mg, mb, vb, qb, lg, lb, gain, bias,
        ) = finish(rgb_out, vec, ext, rows, down, up, out, query, latents_sum, key, value)
    else:
        down, up, out, query, latents_sum, key, value, vec, ext = sums_plain(
            parts, *rest[:5], latents, query_weight, out_weight, rest[5], rest[6], jnp.stack(vectors[:8]), rest[7]
        )
        latents_out = rows
        rgb_grad = rgb_out.reshape(4, tiles, TILE)[:3].reshape(3, tiles * TILE)
        db, ub, ob, mg, mb = (vec[i] for i in range(5))
        vb, qb, lg, lb = (vec[i] for i in range(8, 12))
        gain, bias = restore(ext[0]), restore(ext[1])
    return (
        latents_out, rgb_grad, latents_sum, query, qb, key, value, vb, out, ob, lg, lb, mg, mb, up, ub, down, db,
        gain, bias,
    )


def solution(mesh):
    whole = P()
    placed = (
        whole,
        P(None, ("dp", "pix")),
        P(None, ("dp", "pix")),
        P(("dp", "pix")),
        P(None, "dp"),
    ) + (whole,) * 17 + (P(("dp", "pix"), None, None),)
    square = P("pix", "dp")
    return jax.shard_map(
        shards,
        mesh=mesh,
        in_specs=placed,
        out_specs=(
            P(("dp", "pix"), None, None),
            P(None, ("dp", "pix")),
            square,
            square,
            whole,
            whole,
            whole,
            whole,
            square,
            whole,
            whole,
            whole,
            whole,
            whole,
            square,
            whole,
            square,
            whole,
            whole,
            whole,
        ),
        check_vma=False,
    )
```
